512 devices in a mesh: blk: 32 (over z, y_lo, core), head: 16 (over y_hi, x).
Axes of the slice: x: 4, y: 8 (y_hi: 4, y_lo: 2; y = y_hi * 2 + y_lo), z: 8, core: 2. Of those that a mesh axis runs over, the one named last changes fastest.
Arguments:
- queries: bfloat16 [4096, 128, 192], P('blk', 'head'), may hold values from -8 to 8
- latent: bfloat16 [4096, 576], P(('blk', 'head')), may hold values from -8 to 8
- key_up_weight: bfloat16 [128, 128, 512], P('head'), may hold values from -0.5 to 0.5
- value_up_weight: bfloat16 [128, 512, 128], P('head'), may hold values from -0.25 to 0.25
- w_o: bfloat16 [16384, 3584], P('head', 'blk'), may hold values from -0.046875 to 0.046875
- block_order: int32 [64], replicated, may hold values from 0 to 63, each once
Outputs:
- attended: bfloat16 [4096, 3584], P(('blk', 'head'))
The draws below stay inside these ranges and needn't reach their ends.
All inputs are finite; a program needn't handle non-finite values.
Results may differ from the reference program's by a relative error of at most 0.023.
Values may be sent and summed in bfloat16 or wider, within the bound.
A program may use at most 128 MiB of HBM per device.

```python
import jax
import jax.numpy as jnp
from jax import lax

HEAD_COUNT = 128
PLAIN_QUERY_DIM = 128
ROTARY_WIDTH = 64
LATENT_WIDTH = 512
VALUE_WIDTH = 128
D_OUT = 3584
BLOCK_TOKENS = 128
BLOCK_SPAN = 8
HALF = 64
SEQUENCE_TOKENS = 4096
H_DEV = 8
N_BLK = 32
N_HEAD = 16


def draw_queries(key, part):
    key = jax.random.fold_in(key, 11)
    sampled_values = jax.random.truncated_normal(key, -8.0, 8.0, (SEQUENCE_TOKENS, HEAD_COUNT, PLAIN_QUERY_DIM + ROTARY_WIDTH), jnp.float32)
    return sampled_values.astype(jnp.bfloat16)


def draw_latent(key, part):
    key = jax.random.fold_in(key, 23)
    sampled_values = jax.random.truncated_normal(key, -8.0, 8.0, (SEQUENCE_TOKENS, LATENT_WIDTH + ROTARY_WIDTH), jnp.float32)
    return sampled_values.astype(jnp.bfloat16)


def shard_levels(stream_key, dims, cuts, low, high):
    def one(dim, blocks):
        heights = jax.random.uniform(jax.random.fold_in(jax.random.fold_in(stream_key, 6), dim), (blocks,), jnp.float32, low / len(cuts), high / len(cuts))
        return jnp.repeat(jnp.exp(heights), dims[dim] // blocks).reshape((-1,) + (1,) * (len(dims) - dim - 1))

    level = one(*cuts[0])
    for cut in cuts[1:]:
        level = level * one(*cut)
    return level


def normal_values(rng, dims, scale, limit, cuts=(), kind=jnp.bfloat16):
    drawn = jax.random.normal(rng, dims, jnp.float32) * scale
    if len(cuts) > 0:
        drawn = shard_levels(rng, dims, cuts, -0.22, 0.18) * drawn
    return jnp.clip(drawn, min=-limit, max=limit).astype(kind)


def setup_inputs(seed: int = 0) -> dict:
    streams_of = jax.random.split(jax.random.key(seed), 7)
    queries = draw_queries(jax.random.fold_in(streams_of[6], 71), 0)
    latent = draw_latent(jax.random.fold_in(streams_of[6], 71), 0)
    key_up_weight = normal_values(streams_of[2], (HEAD_COUNT, PLAIN_QUERY_DIM, LATENT_WIDTH), PLAIN_QUERY_DIM ** -0.5, 0.5, ((0, 16),))
    value_up_weight = normal_values(streams_of[3], (HEAD_COUNT, LATENT_WIDTH, VALUE_WIDTH), LATENT_WIDTH ** -0.5, 0.25, ((0, 16),))
    w_o = normal_values(streams_of[4], (HEAD_COUNT * VALUE_WIDTH, D_OUT), (HEAD_COUNT * VALUE_WIDTH) ** -0.5, 0.046875, ((0, 16), (1, 32)))
    block_order = jax.random.permutation(streams_of[5], SEQUENCE_TOKENS // HALF).astype(jnp.int32)
    return {"queries": queries, "latent": latent, "key_up_weight": key_up_weight, "value_up_weight": value_up_weight, "w_o": w_o, "block_order": block_order}


def reference(queries, latent, key_up_weight, value_up_weight, w_o, block_order):
    rows = jnp.arange(SEQUENCE_TOKENS, dtype=jnp.int32)
    pos = block_order[rows // HALF] * HALF + rows % HALF
    q_lat = jnp.einsum('thn,hnc->thc', queries[:, :, :PLAIN_QUERY_DIM].astype(jnp.float32), key_up_weight.astype(jnp.float32)).astype(jnp.bfloat16)
    q_full = jnp.concatenate([q_lat, queries[:, :, PLAIN_QUERY_DIM:]], axis=-1)
    scale = (PLAIN_QUERY_DIM + ROTARY_WIDTH) ** -0.5
    block_list = latent.reshape(N_BLK, BLOCK_TOKENS, LATENT_WIDTH + ROTARY_WIDTH)
    block_pos = pos.reshape(N_BLK, BLOCK_TOKENS)

    def one_block(index):
        start = (index * BLOCK_TOKENS).astype(jnp.int32)
        q_here = lax.dynamic_slice_in_dim(q_full, start, BLOCK_TOKENS, 0).astype(jnp.float32)
        q_pos = lax.dynamic_slice_in_dim(pos, start, BLOCK_TOKENS, 0)
        source_blocks = ((index - jnp.arange(BLOCK_SPAN, dtype=jnp.int32)) % N_BLK).astype(jnp.int32)
        key_rows = block_list[source_blocks].reshape(BLOCK_SPAN * BLOCK_TOKENS, LATENT_WIDTH + ROTARY_WIDTH).astype(jnp.float32)
        key_pos = block_pos[source_blocks].reshape(BLOCK_SPAN * BLOCK_TOKENS)
        scores = jnp.einsum('thc,uc->thu', q_here, key_rows) * scale
        visible = key_pos[None, None, :] <= q_pos[:, None, None]
        top = jnp.max(jnp.where(visible, scores, -1e30), axis=-1)
        expo = jnp.where(visible, jnp.exp(scores - top[..., None]), 0.0)
        grand_total = jnp.sum(expo, axis=-1)
        score_weights = expo.astype(jnp.bfloat16).astype(jnp.float32)
        context_rows = (jnp.einsum('qnj,jy->qny', score_weights, key_rows[:, :LATENT_WIDTH]) / grand_total[..., None]).astype(jnp.bfloat16)
        values = jnp.einsum('thc,hcv->thv', context_rows.astype(jnp.float32), value_up_weight.astype(jnp.float32)).astype(jnp.bfloat16)
        grouped = values.reshape(BLOCK_TOKENS, N_HEAD, H_DEV * VALUE_WIDTH).astype(jnp.float32)
        proj = w_o.reshape(N_HEAD, H_DEV * VALUE_WIDTH, D_OUT).astype(jnp.float32)
        terms = jnp.einsum('tgk,gkd->gtd', grouped, proj).astype(jnp.bfloat16)
        terms = lax.optimization_barrier(terms).astype(jnp.float32)
        return jnp.sum(terms, axis=0).astype(jnp.bfloat16)

    result = lax.map(one_block, jnp.arange(N_BLK, dtype=jnp.int32))
    return result.reshape(SEQUENCE_TOKENS, D_OUT)
```

```python
import functools
import math

import jax
import jax.numpy as jnp
from jax import lax
from jax.experimental import pallas as pl
from jax.experimental.pallas import tpu as pltpu
from jax.sharding import PartitionSpec as P

NOPE = 128
ROT = 64
LAT = 512
WIDTH = LAT + ROT
VAL = 128
HEADS = 8
TOKENS = 128
HALF = 64
SPAN = 8
NBLK = 32
COLS = 112
MINE = 1792
WIDE = ((0, 512), (1024, 384))
GAIN = (NOPE + ROT) ** (-0.5) * math.log2(math.e)
HIDDEN = -1e30
NT = (((1,), (1,)), ((), ()))
F32 = jnp.float32
BF16 = jnp.bfloat16


def nt_dot(a, b):
    return lax.dot_general(a, b, NT, preferred_element_type=F32)


def remote(src, dst, send, recv, device):
    return pltpu.make_async_remote_copy(
        src_ref=src, dst_ref=dst, send_sem=send, recv_sem=recv,
        device_id=device, device_id_type=pl.DeviceIdType.MESH,
    )


def kernel(
    order, latent, q_hbm, ku_hbm, vu_hbm, wo_hbm, out,
    q_raw, q_plain, q_rot, ku, vu, wo, q_full, bias, pack, keys, wt, vals,
    top, total, accum, terms_a, terms_b, got_a, got_b, part_a, part_b, fin_a, fin_b,
    load_sem, ps, pr, lzs, lzr, lcs, lcr, lys, lyr, lds, ldr,
    wps, wpr, wms, wmr, wcs, wcr, vs, vr, xs, xr, yss, ysr, yos, yor,
):
    b = lax.axis_index("blk")
    h = lax.axis_index("head")
    z, c = b // 4, b % 4
    lo, core = c // 2, c % 2
    hi, x = h // 4, h % 4
    up = (b + 4) % NBLK
    down = (b + NBLK - 4) % NBLK
    mate = b + 1 - 2 * core
    side = b + 2 - 4 * lo
    c_mate = c + 1 - 2 * core
    c_side = c + 2 - 4 * lo
    c_diag = c_side + 1 - 2 * core

    loads = [
        pltpu.make_async_copy(src, dst, load_sem.at[i])
        for i, (src, dst) in enumerate(((wo_hbm, wo), (q_hbm, q_raw), (ku_hbm, ku), (vu_hbm, vu)))
    ]
    for load in loads:
        load.start()

    rows = latent[...].astype(F32)
    second = jnp.concatenate([rows[:, 384:], jnp.zeros((8, 192), F32)], axis=1)
    pack[h] = jnp.concatenate([rows[:, :384], second], axis=0).astype(BF16)

    barrier = pltpu.get_barrier_semaphore()

    def greet(device):
        pl.semaphore_signal(barrier, inc=1, device_id=device, device_id_type=pl.DeviceIdType.MESH)

    @pl.loop(1, 16)
    def _(i):
        greet({"head": (h + i) % 16})

    @pl.loop(0, 4)
    def _(i):
        greet({"blk": side, "head": (hi + i) % 4 * 4 + x})

    greet({"blk": up})
    greet({"blk": down})
    greet({"blk": mate})
    pl.semaphore_wait(barrier, 22)

    def own_rows(i):
        return remote(pack.at[h], pack.at[h], ps.at[i], pr.at[i], {"head": (h + i) % 16})

    @pl.loop(1, 16)
    def _(i):
        own_rows(i).start()

    def shard(zz, cc):
        return wt.at[pl.ds(pl.multiple_of((zz * 2 + cc) * COLS, 16), COLS)]

    def w_plus(k):
        ref = shard((z + 8 - k) % 8, core)
        return remote(ref, ref, wps.at[k], wpr.at[k], {"blk": up})

    def w_minus(k):
        ref = shard((z + k) % 8, core)
        return remote(ref, ref, wms.at[k], wmr.at[k], {"blk": down})

    def w_core(k):
        zz = (z + 8 - k) % 8 if k < 4 else (z + k - 3) % 8
        ref = shard(zz, core)
        return remote(ref, ref, wcs.at[k], wcr.at[k], {"blk": mate})

    def w_core_in(k):
        zz = (z + 8 - k) % 8 if k < 4 else (z + k - 3) % 8
        ref = shard(zz, 1 - core)
        return remote(ref, ref, wcs.at[k], wcr.at[k], {"blk": mate})

    def w_plus_in(k):
        ref = shard((z + 7 - k) % 8, core)
        return remote(ref, ref, wps.at[k], wpr.at[k], {"blk": up})

    def w_minus_in(k):
        ref = shard((z + 1 + k) % 8, core)
        return remote(ref, ref, wms.at[k], wmr.at[k], {"blk": down})

    loads[0].wait()
    r = lax.broadcasted_iota(jnp.int32, (COLS, COLS), 0)
    s = lax.broadcasted_iota(jnp.int32, (COLS, COLS), 1)
    eye = jnp.where(r == s, 1.0, 0.0).astype(BF16)
    wt[pl.ds(pl.multiple_of((z * 2 + core) * COLS, 16), COLS), :] = nt_dot(eye, wo[...]).astype(BF16)
    w_plus(0).start()
    w_minus(0).start()
    w_core(0).start()

    loads[1].wait()
    q_plain[...] = q_raw[:, :, :NOPE].astype(F32).reshape(TOKENS * HEADS, NOPE)
    q_rot[:, :ROT] = q_raw[:, :, NOPE:].astype(F32).reshape(TOKENS * HEADS, ROT)
    loads[2].wait()
    for n in range(HEADS):
        plain = q_plain[pl.ds(n, TOKENS, stride=HEADS), :].astype(BF16)
        q_full[n * TOKENS:(n + 1) * TOKENS, :LAT] = jnp.dot(
            plain, ku[n], preferred_element_type=F32
        ).astype(BF16)
        q_full[n * TOKENS:(n + 1) * TOKENS, LAT:] = q_rot[pl.ds(n, TOKENS, stride=HEADS), :][:, :ROT].astype(BF16)

    row = lax.broadcasted_iota(jnp.int32, (TOKENS, TOKENS), 0)
    col = lax.broadcasted_iota(jnp.int32, (TOKENS, TOKENS), 1)
    q_pos = jnp.where(row < HALF, order[2 * b], order[2 * b + 1]) * HALF + row % HALF
    for n in range(SPAN):
        src = (b + NBLK - 7 + n) % NBLK
        k_pos = jnp.where(col < HALF, order[2 * src], order[2 * src + 1]) * HALF + col % HALF
        bias[:, n * TOKENS:(n + 1) * TOKENS] = jnp.where(k_pos <= q_pos, 0.0, HIDDEN)

    @pl.loop(1, 16)
    def _(i):
        ref = pack.at[(h + 16 - i) % 16]
        remote(ref, ref, ps.at[i], pr.at[i], {"head": (h + i) % 16}).wait_recv()

    def slot(plane, cc):
        return keys.at[pl.ds(pl.multiple_of((8 - 4 * plane + cc) * TOKENS, TOKENS), TOKENS)]

    gathered = pack[...].astype(F32)
    base = pl.multiple_of((8 + c) * TOKENS, TOKENS)
    keys[pl.ds(base, TOKENS), :384] = gathered[:, :8, :].reshape(TOKENS, 384).astype(BF16)
    keys[pl.ds(base, TOKENS), 384:] = gathered[:, 8:, :192].reshape(TOKENS, 192).astype(BF16)

    def l_up(k):
        return remote(slot(k, c), slot(k + 1, c), lzs.at[k], lzr.at[k], {"blk": up})

    def l_up_in(k):
        return remote(slot(k + 1, c), slot(k + 1, c), lzs.at[k], lzr.at[k], {"blk": up})

    def l_core(p):
        return remote(slot(p, c), slot(p, c), lcs.at[p], lcr.at[p], {"blk": mate})

    def l_core_in(p):
        return remote(slot(p, c_mate), slot(p, c_mate), lcs.at[p], lcr.at[p], {"blk": mate})

    def l_side(j):
        ref = slot(j + lo, c)
        return remote(ref, ref, lys.at[j], lyr.at[j], {"blk": side})

    def l_side_in(j):
        ref = slot(j + 1 - lo, c_side)
        return remote(ref, ref, lys.at[j], lyr.at[j], {"blk": side})

    def l_diag(j):
        ref = slot(j + 1 - lo, c_side)
        return remote(ref, ref, lds.at[j], ldr.at[j], {"blk": mate})

    def l_diag_in(j):
        ref = slot(j + 1 - lo, c_diag)
        return remote(ref, ref, lds.at[j], ldr.at[j], {"blk": mate})

    def w_step_plus(k):
        w_plus_in(k - 1).wait_recv()
        if k < 3:
            w_plus(k).start()
        w_core(k).start()

    def w_step_minus(k):
        w_minus_in(k - 1).wait_recv()
        if k < 4:
            w_minus(k).start()
        w_core(3 + k).start()

    l_up(0).start()

    @pl.when(lo == 0)
    def _():
        l_side(0).start()

    l_core(0).start()

    w_step_minus(1)
    l_up_in(0).wait_recv()
    l_up(1).start()

    @pl.when(lo == 0)
    def _():
        l_side(1).start()

    @pl.when(lo == 1)
    def _():
        l_side(0).start()

    l_core(1).start()
    w_step_plus(1)
    l_side_in(0).wait_recv()
    l_diag(0).start()
    l_core_in(0).wait_recv()
    l_core_in(1).wait_recv()
    l_diag_in(0).wait_recv()

    def scores(i, start, first):
        q = q_full[pl.ds(pl.multiple_of(i * 256, 256), 256), :]
        k = keys[pl.ds(pl.multiple_of(start, TOKENS), 512), :]
        sc = nt_dot(q, k).reshape(2, TOKENS, 512) + bias[:, first:first + 512][None]
        return sc.reshape(256, 512), k

    def near(i):
        at = pl.ds(pl.multiple_of(i * 256, 256), 256)
        sc, k = scores(i, (c + 5) * TOKENS, 512)
        m = jnp.max(sc, axis=1, keepdims=True)
        e = jnp.exp2((sc - m) * GAIN)
        top[at, :] = jnp.broadcast_to(m, (256, 128))
        total[at, :] = jnp.broadcast_to(jnp.sum(e, axis=1, keepdims=True), (256, 128))
        accum[at, :] = jnp.dot(e.astype(BF16), k[:, :LAT], preferred_element_type=F32)

    def v_out(i):
        ref = vals.at[lo, :, pl.ds(pl.multiple_of(i * 256, 256), 256)]
        return remote(ref, ref, vs.at[i], vr.at[i], {"blk": side})

    def v_in(i):
        ref = vals.at[1 - lo, :, pl.ds(pl.multiple_of(i * 256, 256), 256)]
        return remote(ref, ref, vs.at[i], vr.at[i], {"blk": side})

    def far(i):
        at = pl.ds(pl.multiple_of(i * 256, 256), 256)
        sc, k = scores(i, (c + 1) * TOKENS, 0)
        old = top[at, :][:, :1]
        m = jnp.maximum(old, jnp.max(sc, axis=1, keepdims=True))
        e = jnp.exp2((sc - m) * GAIN)
        shrink = jnp.exp2((old - m) * GAIN)
        tot = total[at, :][:, :1] * shrink + jnp.sum(e, axis=1, keepdims=True)
        acc = accum[at, :] * shrink + jnp.dot(e.astype(BF16), k[:, :LAT], preferred_element_type=F32)
        ctx = (acc * (1.0 / tot)).astype(BF16)
        for n in range(2):
            v = jnp.dot(ctx[n * TOKENS:(n + 1) * TOKENS], vu[2 * i + n], preferred_element_type=F32)
            vals[lo, :, pl.ds(pl.multiple_of(i * 256 + n * VAL, VAL), VAL)] = v.astype(BF16)
        v_out(i).start()

    pl.loop(0, 2)(near)
    w_step_minus(2)
    w_step_plus(2)
    l_up_in(1).wait_recv()

    @pl.when(lo == 1)
    def _():
        l_side(1).start()

    l_core(2).start()
    pl.loop(2, 4)(near)
    l_side_in(1).wait_recv()
    l_diag(1).start()
    w_step_minus(3)
    w_step_plus(3)
    loads[3].wait()
    l_core_in(2).wait_recv()
    l_diag_in(1).wait_recv()
    pl.loop(0, 2)(far)
    w_step_minus(4)
    pl.loop(2, 4)(far)
    for k in range(8):
        w_core_in(k).wait_recv()

    def x_out(y, n, step, d):
        terms, got = ((terms_a, got_a), (terms_b, got_b))[n]
        xd = (x + d) % 4
        return remote(
            terms.at[y, :, xd], got.at[y, d - 1],
            xs.at[n, step, d - 1], xr.at[n, step, d - 1], {"head": hi * 4 + xd},
        )

    def project(y, n, step):
        first, width = WIDE[n]
        terms = (terms_a, terms_b)[n]
        t = nt_dot(vals[y], wt[first:first + 2 * width, :])
        left = t[:, :width].reshape(16, 8, width)
        right = t[:, width:].reshape(16, 8, width)
        both = jnp.concatenate([left, right], axis=1).astype(BF16)
        terms[y] = both.reshape(4, 4, 16, width)
        for d in (2, 1, 3):
            x_out(y, n, step, d).start()

    def y_same(n, e):
        part, fin = ((part_a, fin_a), (part_b, fin_b))[n]
        yd = (hi + e) % 4
        return remote(
            part.at[lo, yd], fin.at[0, e], yss.at[n, e], ysr.at[n, e], {"head": yd * 4 + x}
        )

    def y_other(n, e):
        part, fin = ((part_a, fin_a), (part_b, fin_b))[n]
        yd = (hi + e) % 4
        return remote(
            part.at[1 - lo, yd], fin.at[1, e], yos.at[n, e], yor.at[n, e],
            {"blk": side, "head": yd * 4 + x},
        )

    def combine(y, n, step):
        terms, got, part = ((terms_a, got_a, part_a), (terms_b, got_b, part_b))[n]
        for d in (1, 2, 3):
            x_out(y, n, step, d).wait_recv()
        t = terms[y, :, x].astype(F32)
        for d in range(3):
            t = t + got[y, d].astype(F32)
        part[y] = t.astype(BF16)

    for n in range(2):
        project(lo, n, 0)
    for i in range(4):
        v_in(i).wait_recv()
    for n in range(2):
        project(1 - lo, n, 1)
    for n in range(2):
        combine(lo, n, 0)
        for e in (2, 1, 3):
            y_same(n, e).start()
    for n in range(2):
        combine(1 - lo, n, 1)
        for e in (2, 1, 3, 0):
            y_other(n, e).start()
    for n, (first, width) in enumerate(WIDE):
        part, fin = ((part_a, fin_a), (part_b, fin_b))[n]
        same = part[lo, hi].astype(F32)
        for e in (1, 2, 3):
            y_same(n, e).wait_recv()
            same = same + fin[0, e].astype(F32)
        y_other(n, 0).wait_recv()
        other = fin[1, 0].astype(F32)
        for e in (1, 2, 3):
            y_other(n, e).wait_recv()
            other = other + fin[1, e].astype(F32)
        for y, v in ((lo, same), (1 - lo, other)):
            out[y, :, first:first + width] = v[:8]
            out[y, :, first + width:first + 2 * width] = v[8:]

    @pl.loop(1, 16)
    def _(i):
        own_rows(i).wait_send()

    for k in range(2):
        l_up(k).wait_send()
        l_side(k).wait_send()
        l_diag(k).wait_send()
    for k in range(3):
        l_core(k).wait_send()
        w_plus(k).wait_send()
    for k in range(4):
        w_minus(k).wait_send()
        v_out(k).wait_send()
    for k in range(8):
        w_core(k).wait_send()
    for n in range(2):
        for d in (1, 2, 3):
            x_out(lo, n, 0, d).wait_send()
            x_out(1 - lo, n, 1, d).wait_send()
            y_same(n, d).wait_send()
        for e in range(4):
            y_other(n, e).wait_send()


def shards(queries, latent, key_up_weight, value_up_weight, w_o, block_order):
    vmem = pl.BlockSpec(memory_space=pltpu.VMEM)
    anywhere = pl.BlockSpec(memory_space=pl.ANY)
    dma = pltpu.SemaphoreType.DMA
    rows = TOKENS * HEADS
    scratch = [
        pltpu.VMEM((TOKENS, HEADS, NOPE + ROT), BF16),
        pltpu.VMEM((rows, 128), F32),
        pltpu.VMEM((rows, 128), F32),
        pltpu.VMEM((HEADS, NOPE, LAT), BF16),
        pltpu.VMEM((HEADS, LAT, VAL), BF16),
        pltpu.VMEM((rows, COLS), BF16),
        pltpu.VMEM((rows, WIDTH), BF16),
        pltpu.VMEM((TOKENS, SPAN * TOKENS), F32),
        pltpu.VMEM((16, 16, 384), BF16),
        pltpu.VMEM((12 * TOKENS, WIDTH), BF16),
        pltpu.VMEM((MINE, HEADS * VAL), BF16),
        pltpu.VMEM((2, TOKENS, HEADS * VAL), BF16),
        pltpu.VMEM((rows, 128), F32),
        pltpu.VMEM((rows, 128), F32),
        pltpu.VMEM((rows, LAT), F32),
        pltpu.VMEM((2, 4, 4, 16, 512), BF16),
        pltpu.VMEM((2, 4, 4, 16, 384), BF16),
        pltpu.VMEM((2, 3, 4, 16, 512), BF16),
        pltpu.VMEM((2, 3, 4, 16, 384), BF16),
        pltpu.VMEM((2, 4, 16, 512), BF16),
        pltpu.VMEM((2, 4, 16, 384), BF16),
        pltpu.VMEM((2, 4, 16, 512), BF16),
        pltpu.VMEM((2, 4, 16, 384), BF16),
        dma((4,)),
        dma((16,)), dma((16,)),
        dma((2,)), dma((2,)),
        dma((3,)), dma((3,)),
        dma((2,)), dma((2,)),
        dma((2,)), dma((2,)),
        dma((3,)), dma((3,)),
        dma((4,)), dma((4,)),
        dma((8,)), dma((8,)),
        dma((4,)), dma((4,)),
        dma((2, 2, 3)), dma((2, 2, 3)),
        dma((2, 4)), dma((2, 4)),
        dma((2, 4)), dma((2, 4)),
    ]
    summed = pl.pallas_call(
        kernel,
        out_shape=jax.ShapeDtypeStruct((2, 8, MINE), F32),
        in_specs=[pl.BlockSpec(memory_space=pltpu.SMEM), vmem] + [anywhere] * 4,
        out_specs=vmem,
        scratch_shapes=scratch,
        compiler_params=pltpu.CompilerParams(
            collective_id=0, has_side_effects=True, vmem_limit_bytes=48 * 1024 * 1024
        ),
        cost_estimate=pl.CostEstimate(flops=3_500_000_000, bytes_accessed=3_000_000, transcendentals=1_048_576),
    )(block_order, latent, queries, key_up_weight, value_up_weight, w_o)
    return summed.reshape(2, 8, 8, 2 * COLS).transpose(1, 2, 0, 3).reshape(8, 32 * COLS).astype(BF16)


def solution(mesh):
    placed = (
        P("blk", "head", None),
        P(("blk", "head"), None),
        P("head", None, None),
        P("head", None, None),
        P("head", "blk"),
        P(),
    )
    return jax.shard_map(
        shards, mesh=mesh, in_specs=placed, out_specs=P(("blk", "head"), None), check_vma=False
    )
```

```python
import functools
import math

import jax
import jax.numpy as jnp
from jax import lax
from jax.experimental import pallas as pl
from jax.experimental.pallas import tpu as pltpu
from jax.sharding import PartitionSpec as P

NOPE = 128
ROT = 64
LAT = 512
WIDTH = LAT + ROT
VAL = 128
HEADS = 8
TOKENS = 128
HALF = 64
SPAN = 8
NBLK = 32
COLS = 112
MINE = 1792
WIDE = ((0, 512), (1024, 384))
GAIN = (NOPE + ROT) ** (-0.5) * math.log2(math.e)
HIDDEN = -1e30
NT = (((1,), (1,)), ((), ()))
F32 = jnp.float32
BF16 = jnp.bfloat16


def nt_dot(a, b):
    return lax.dot_general(a, b, NT, preferred_element_type=F32)


def remote(src, dst, send, recv, device):
    return pltpu.make_async_remote_copy(
        src_ref=src, dst_ref=dst, send_sem=send, recv_sem=recv,
        device_id=device, device_id_type=pl.DeviceIdType.MESH,
    )


def kernel(
    order, latent, q_hbm, ku_hbm, vu_hbm, wo_hbm, out,
    q_raw, ku, vu, q_full, bias, pack, keys, wt, vals,
    top, total, accum, terms_a, terms_b, got_a, got_b, relay_a, relay_b, part_a, part_b, fin_a, fin_b,
    load_sem, ps, pr, lzs, lzr, lcs, lcr, lys, lyr, lds, ldr,
    wps, wpr, wms, wmr, wcs, wcr, vs, vr, xs, xr, yss, ysr, yos, yor,
):
    b = lax.axis_index("blk")
    h = lax.axis_index("head")
    z, c = b // 4, b % 4
    lo, core = c // 2, c % 2
    hi, x = h // 4, h % 4
    up = (b + 4) % NBLK
    down = (b + NBLK - 4) % NBLK
    mate = b + 1 - 2 * core
    side = b + 2 - 4 * lo
    c_mate = c + 1 - 2 * core
    c_side = c + 2 - 4 * lo
    c_diag = c_side + 1 - 2 * core

    loads = [
        pltpu.make_async_copy(src, dst, load_sem.at[i])
        for i, (src, dst) in enumerate(((q_hbm, q_raw), (ku_hbm, ku), (vu_hbm, vu)))
    ]
    mine = wt.at[pl.ds(pl.multiple_of((z * 2 + core) * COLS, 16), COLS)]
    loads.append(pltpu.make_async_copy(wo_hbm, mine, load_sem.at[3]))
    for load in loads[3:] + loads[:3]:
        load.start()

    rows = latent[...].astype(F32)
    second = jnp.concatenate([rows[:, 384:], jnp.zeros((8, 192), F32)], axis=1)
    pack[h] = jnp.concatenate([rows[:, :384], second], axis=0).astype(BF16)

    barrier = pltpu.get_barrier_semaphore()

    def greet(device):
        pl.semaphore_signal(barrier, inc=1, device_id=device, device_id_type=pl.DeviceIdType.MESH)

    @pl.loop(1, 16)
    def _(i):
        greet({"head": (h + i) % 16})

    @pl.loop(0, 4)
    def _(i):
        greet({"blk": side, "head": (hi + i) % 4 * 4 + x})

    greet({"blk": up})
    greet({"blk": down})
    greet({"blk": mate})
    pl.semaphore_wait(barrier, 22)

    def own_rows(i):
        return remote(pack.at[h], pack.at[h], ps.at[i], pr.at[i], {"head": (h + i) % 16})

    @pl.loop(1, 16)
    def _(i):
        own_rows(i).start()

    def shard(zz, cc):
        return wt.at[pl.ds(pl.multiple_of((zz * 2 + cc) * COLS, 16), COLS)]

    def w_plus(k):
        ref = shard((z + 8 - k) % 8, core)
        return remote(ref, ref, wps.at[k], wpr.at[k], {"blk": up})

    def w_minus(k):
        ref = shard((z + k) % 8, core)
        return remote(ref, ref, wms.at[k], wmr.at[k], {"blk": down})

    def w_core(k):
        zz = (z + 8 - k) % 8 if k < 4 else (z + k - 3) % 8
        ref = shard(zz, core)
        return remote(ref, ref, wcs.at[k], wcr.at[k], {"blk": mate})

    def w_core_in(k):
        zz = (z + 8 - k) % 8 if k < 4 else (z + k - 3) % 8
        ref = shard(zz, 1 - core)
        return remote(ref, ref, wcs.at[k], wcr.at[k], {"blk": mate})

    def w_plus_in(k):
        ref = shard((z + 7 - k) % 8, core)
        return remote(ref, ref, wps.at[k], wpr.at[k], {"blk": up})

    def w_minus_in(k):
        ref = shard((z + 1 + k) % 8, core)
        return remote(ref, ref, wms.at[k], wmr.at[k], {"blk": down})

    loads[3].wait()
    w_plus(0).start()
    w_minus(0).start()
    w_core(0).start()

    loads[0].wait()
    loads[1].wait()
    for n in range(HEADS):
        at = slice(n * TOKENS, (n + 1) * TOKENS)
        q_full[at, :LAT] = lax.dot_general(
            q_raw[n, :NOPE, :], ku[n], (((0,), (0,)), ((), ())), preferred_element_type=F32
        ).astype(BF16)
        q_full[at, LAT:] = q_raw[n, NOPE:, :].astype(F32).T.astype(BF16)

    row = lax.broadcasted_iota(jnp.int32, (TOKENS, TOKENS), 0)
    col = lax.broadcasted_iota(jnp.int32, (TOKENS, TOKENS), 1)
    q_pos = jnp.where(row < HALF, order[2 * b], order[2 * b + 1]) * HALF + row % HALF
    for n in range(SPAN):
        src = (b + NBLK - 7 + n) % NBLK
        k_pos = jnp.where(col < HALF, order[2 * src], order[2 * src + 1]) * HALF + col % HALF
        bias[:, n * TOKENS:(n + 1) * TOKENS] = jnp.where(k_pos <= q_pos, 0.0, HIDDEN)

    @pl.loop(1, 16)
    def _(i):
        ref = pack.at[(h + 16 - i) % 16]
        remote(ref, ref, ps.at[i], pr.at[i], {"head": (h + i) % 16}).wait_recv()

    def slot(plane, cc):
        return keys.at[pl.ds(pl.multiple_of((8 - 4 * plane + cc) * TOKENS, TOKENS), TOKENS)]

    gathered = pack[...].astype(F32)
    base = pl.multiple_of((8 + c) * TOKENS, TOKENS)
    keys[pl.ds(base, TOKENS), :384] = gathered[:, :8, :].reshape(TOKENS, 384).astype(BF16)
    keys[pl.ds(base, TOKENS), 384:] = gathered[:, 8:, :192].reshape(TOKENS, 192).astype(BF16)

    def l_up(k):
        return remote(slot(k, c), slot(k + 1, c), lzs.at[k], lzr.at[k], {"blk": up})

    def l_up_in(k):
        return remote(slot(k + 1, c), slot(k + 1, c), lzs.at[k], lzr.at[k], {"blk": up})

    def l_core(p):
        return remote(slot(p, c), slot(p, c), lcs.at[p], lcr.at[p], {"blk": mate})

    def l_core_in(p):
        return remote(slot(p, c_mate), slot(p, c_mate), lcs.at[p], lcr.at[p], {"blk": mate})

    def l_side(j):
        ref = slot(j + lo, c)
        return remote(ref, ref, lys.at[j], lyr.at[j], {"blk": side})

    def l_side_in(j):
        ref = slot(j + 1 - lo, c_side)
        return remote(ref, ref, lys.at[j], lyr.at[j], {"blk": side})

    def l_diag(j):
        ref = slot(j + 1 - lo, c_side)
        return remote(ref, ref, lds.at[j], ldr.at[j], {"blk": mate})

    def l_diag_in(j):
        ref = slot(j + 1 - lo, c_diag)
        return remote(ref, ref, lds.at[j], ldr.at[j], {"blk": mate})

    def w_step_plus(k):
        w_plus_in(k - 1).wait_recv()
        if k < 3:
            w_plus(k).start()
        w_core(k).start()

    def w_step_minus(k):
        w_minus_in(k - 1).wait_recv()
        if k < 4:
            w_minus(k).start()
        w_core(3 + k).start()

    l_up(0).start()

    @pl.when(lo == 0)
    def _():
        l_side(0).start()

    l_core(0).start()

    w_step_minus(1)
    l_up_in(0).wait_recv()
    l_up(1).start()

    @pl.when(lo == 0)
    def _():
        l_side(1).start()

    @pl.when(lo == 1)
    def _():
        l_side(0).start()

    l_core(1).start()
    w_step_plus(1)
    l_side_in(0).wait_recv()
    l_diag(0).start()
    l_core_in(0).wait_recv()
    l_core_in(1).wait_recv()
    l_diag_in(0).wait_recv()

    def scores(i, start, first):
        q = q_full[pl.ds(pl.multiple_of(i * 256, 256), 256), :]
        k = keys[pl.ds(pl.multiple_of(start, TOKENS), 512), :]
        sc = nt_dot(q, k).reshape(2, TOKENS, 512) + bias[:, first:first + 512][None]
        return sc.reshape(256, 512), k

    def near(i):
        at = pl.ds(pl.multiple_of(i * 256, 256), 256)
        sc, k = scores(i, (c + 5) * TOKENS, 512)
        m = jnp.max(sc, axis=1, keepdims=True)
        e = jnp.exp2((sc - m) * GAIN)
        top[at, :] = jnp.broadcast_to(m, (256, 128))
        total[at, :] = jnp.broadcast_to(jnp.sum(e, axis=1, keepdims=True), (256, 128))
        accum[at, :] = jnp.dot(e.astype(BF16), k[:, :LAT], preferred_element_type=F32)

    def v_out(i):
        ref = vals.at[lo, :, pl.ds(pl.multiple_of(i * 256, 256), 256)]
        return remote(ref, ref, vs.at[i], vr.at[i], {"blk": side})

    def v_in(i):
        ref = vals.at[1 - lo, :, pl.ds(pl.multiple_of(i * 256, 256), 256)]
        return remote(ref, ref, vs.at[i], vr.at[i], {"blk": side})

    def far(i):
        at = pl.ds(pl.multiple_of(i * 256, 256), 256)
        sc, k = scores(i, (c + 1) * TOKENS, 0)
        old = top[at, :][:, :1]
        m = jnp.maximum(old, jnp.max(sc, axis=1, keepdims=True))
        e = jnp.exp2((sc - m) * GAIN)
        shrink = jnp.exp2((old - m) * GAIN)
        tot = total[at, :][:, :1] * shrink + jnp.sum(e, axis=1, keepdims=True)
        acc = accum[at, :] * shrink + jnp.dot(e.astype(BF16), k[:, :LAT], preferred_element_type=F32)
        ctx = (acc * (1.0 / tot)).astype(BF16)
        for n in range(2):
            v = jnp.dot(ctx[n * TOKENS:(n + 1) * TOKENS], vu[2 * i + n], preferred_element_type=F32)
            vals[lo, :, pl.ds(pl.multiple_of(i * 256 + n * VAL, VAL), VAL)] = v.astype(BF16)
        v_out(i).start()

    pl.loop(0, 2)(near)
    w_step_minus(2)
    w_step_plus(2)
    l_up_in(1).wait_recv()

    @pl.when(lo == 1)
    def _():
        l_side(1).start()

    l_core(2).start()
    pl.loop(2, 4)(near)
    l_side_in(1).wait_recv()
    l_diag(1).start()
    w_step_minus(3)
    w_step_plus(3)
    loads[2].wait()
    l_core_in(2).wait_recv()
    l_diag_in(1).wait_recv()
    pl.loop(0, 2)(far)
    w_step_minus(4)
    pl.loop(2, 4)(far)
    for k in range(8):
        w_core_in(k).wait_recv()

    def x_out(y, n, step, way, kind):
        terms, got, relay = ((terms_a, got_a, relay_a), (terms_b, got_b, relay_b))[n]
        xd = (x + 1 + 2 * way) % 4
        if kind == 0:
            src, dst = terms.at[y, way, :, (x + 2) % 4], relay.at[y, way]
        else:
            half = 1 - way if kind == 1 else way
            src, dst = terms.at[y, half, :, xd], got.at[y, way, half]
        sem = (n, step, way, kind)
        return remote(src, dst, xs.at[sem], xr.at[sem], {"head": hi * 4 + xd})

    def project(y, n, step):
        first, width = WIDE[n]
        terms = (terms_a, terms_b)[n]
        t = nt_dot(vals[y], wt[first:first + 2 * width, :])
        left = t[:, :width].reshape(16, 8, width)
        right = t[:, width:].reshape(16, 8, width)
        both = jnp.concatenate([left, right], axis=1).astype(BF16)
        terms[y] = both.reshape(2, 2, 4, 16, width)
        for kind in range(2):
            for way in range(2):
                x_out(y, n, step, way, kind).start()

    def pass_on(y, n, step):
        terms, relay = ((terms_a, relay_a), (terms_b, relay_b))[n]
        for way in range(2):
            x_out(y, n, step, way, 0).wait_recv()
            xd = (x + 1 + 2 * way) % 4
            t = terms[y, way, :, xd].astype(F32) + relay[y, way].astype(F32)
            terms[y, way, :, xd] = t.astype(BF16)
            x_out(y, n, step, way, 2).start()

    def y_same(n, e):
        part, fin = ((part_a, fin_a), (part_b, fin_b))[n]
        yd = (hi + e) % 4
        return remote(
            part.at[lo, yd], fin.at[0, e], yss.at[n, e], ysr.at[n, e], {"head": yd * 4 + x}
        )

    def y_other(n, e):
        part, fin = ((part_a, fin_a), (part_b, fin_b))[n]
        yd = (hi + e) % 4
        return remote(
            part.at[1 - lo, yd], fin.at[1, e], yos.at[n, e], yor.at[n, e],
            {"blk": side, "head": yd * 4 + x},
        )

    def combine(y, n, step):
        terms, got, part = ((terms_a, got_a, part_a), (terms_b, got_b, part_b))[n]
        width = WIDE[n][1]
        for way in range(2):
            x_out(y, n, step, way, 1).wait_recv()
            x_out(y, n, step, way, 2).wait_recv()
        t = terms[y, :, :, x].astype(F32) + got[y, 0].astype(F32) + got[y, 1].astype(F32)
        part[y] = t.reshape(4, 16, width).astype(BF16)

    project(lo, 0, 0)
    project(lo, 1, 0)
    pass_on(lo, 0, 0)
    for i in range(4):
        v_in(i).wait_recv()
    project(1 - lo, 0, 1)
    pass_on(lo, 1, 0)
    project(1 - lo, 1, 1)
    pass_on(1 - lo, 0, 1)
    pass_on(1 - lo, 1, 1)
    for n in range(2):
        combine(lo, n, 0)
        for e in (2, 1, 3):
            y_same(n, e).start()
    for n in range(2):
        combine(1 - lo, n, 1)
        for e in (2, 1, 3, 0):
            y_other(n, e).start()
    for n, (first, width) in enumerate(WIDE):
        part, fin = ((part_a, fin_a), (part_b, fin_b))[n]
        same = part[lo, hi].astype(F32)
        for e in (1, 2, 3):
            y_same(n, e).wait_recv()
            same = same + fin[0, e].astype(F32)
        y_other(n, 0).wait_recv()
        other = fin[1, 0].astype(F32)
        for e in (1, 2, 3):
            y_other(n, e).wait_recv()
            other = other + fin[1, e].astype(F32)
        for y, v in ((lo, same), (1 - lo, other)):
            out[y, :, first:first + width] = v[:8]
            out[y, :, first + width:first + 2 * width] = v[8:]

    @pl.loop(1, 16)
    def _(i):
        own_rows(i).wait_send()

    for k in range(2):
        l_up(k).wait_send()
        l_side(k).wait_send()
        l_diag(k).wait_send()
    for k in range(3):
        l_core(k).wait_send()
        w_plus(k).wait_send()
    for k in range(4):
        w_minus(k).wait_send()
        v_out(k).wait_send()
    for k in range(8):
        w_core(k).wait_send()
    for n in range(2):
        for way in range(2):
            for kind in range(3):
                x_out(lo, n, 0, way, kind).wait_send()
                x_out(1 - lo, n, 1, way, kind).wait_send()
        for e in (1, 2, 3):
            y_same(n, e).wait_send()
        for e in range(4):
            y_other(n, e).wait_send()


def shards(queries, latent, key_up_weight, value_up_weight, w_o, block_order):
    vmem = pl.BlockSpec(memory_space=pltpu.VMEM)
    anywhere = pl.BlockSpec(memory_space=pl.ANY)
    dma = pltpu.SemaphoreType.DMA
    rows = TOKENS * HEADS
    scratch = [
        pltpu.VMEM((HEADS, NOPE + ROT, TOKENS), BF16),
        pltpu.VMEM((HEADS, NOPE, LAT), BF16),
        pltpu.VMEM((HEADS, LAT, VAL), BF16),
        pltpu.VMEM((rows, WIDTH), BF16),
        pltpu.VMEM((TOKENS, SPAN * TOKENS), F32),
        pltpu.VMEM((16, 16, 384), BF16),
        pltpu.VMEM((12 * TOKENS, WIDTH), BF16),
        pltpu.VMEM((MINE, HEADS * VAL), BF16),
        pltpu.VMEM((2, TOKENS, HEADS * VAL), BF16),
        pltpu.VMEM((rows, 128), F32),
        pltpu.VMEM((rows, 128), F32),
        pltpu.VMEM((rows, LAT), F32),
        pltpu.VMEM((2, 2, 2, 4, 16, 512), BF16),
        pltpu.VMEM((2, 2, 2, 4, 16, 384), BF16),
        pltpu.VMEM((2, 2, 2, 2, 16, 512), BF16),
        pltpu.VMEM((2, 2, 2, 2, 16, 384), BF16),
        pltpu.VMEM((2, 2, 2, 16, 512), BF16),
        pltpu.VMEM((2, 2, 2, 16, 384), BF16),
        pltpu.VMEM((2, 4, 16, 512), BF16),
        pltpu.VMEM((2, 4, 16, 384), BF16),
        pltpu.VMEM((2, 4, 16, 512), BF16),
        pltpu.VMEM((2, 4, 16, 384), BF16),
        dma((4,)),
        dma((16,)), dma((16,)),
        dma((2,)), dma((2,)),
        dma((3,)), dma((3,)),
        dma((2,)), dma((2,)),
        dma((2,)), dma((2,)),
        dma((3,)), dma((3,)),
        dma((4,)), dma((4,)),
        dma((8,)), dma((8,)),
        dma((4,)), dma((4,)),
        dma((2, 2, 2, 3)), dma((2, 2, 2, 3)),
        dma((2, 4)), dma((2, 4)),
        dma((2, 4)), dma((2, 4)),
    ]
    summed = pl.pallas_call(
        kernel,
        out_shape=jax.ShapeDtypeStruct((2, 8, MINE), F32),
        in_specs=[pl.BlockSpec(memory_space=pltpu.SMEM), vmem] + [anywhere] * 4,
        out_specs=vmem,
        scratch_shapes=scratch,
        compiler_params=pltpu.CompilerParams(
            collective_id=0, has_side_effects=True, vmem_limit_bytes=60 * 1024 * 1024
        ),
        cost_estimate=pl.CostEstimate(flops=3_500_000_000, bytes_accessed=3_000_000, transcendentals=1_048_576),
    )(block_order, latent, queries.transpose(1, 2, 0), key_up_weight, value_up_weight, w_o.T)
    return summed.reshape(2, 8, 8, 2 * COLS).transpose(1, 2, 0, 3).reshape(8, 32 * COLS).astype(BF16)


def solution(mesh):
    placed = (
        P("blk", "head", None),
        P(("blk", "head"), None),
        P("head", None, None),
        P("head", None, None),
        P("head", "blk"),
        P(),
    )
    return jax.shard_map(
        shards, mesh=mesh, in_specs=placed, out_specs=P(("blk", "head"), None), check_vma=False
    )
```

```python
import functools
import math

import jax
import jax.numpy as jnp
from jax import lax
from jax.experimental import pallas as pl
from jax.experimental.pallas import tpu as pltpu
from jax.sharding import PartitionSpec as P

NOPE = 128
ROT = 64
LAT = 512
WIDTH = LAT + ROT
VAL = 128
HEADS = 8
TOKENS = 128
HALF = 64
SPAN = 8
NBLK = 32
COLS = 112
MINE = 1792
WIDE = ((0, 512), (1024, 384))
GAIN = (NOPE + ROT) ** (-0.5) * math.log2(math.e)
HIDDEN = -1e30
NT = (((1,), (1,)), ((), ()))
F32 = jnp.float32
BF16 = jnp.bfloat16


def nt_dot(a, b):
    return lax.dot_general(a, b, NT, preferred_element_type=F32)


def remote(src, dst, send, recv, device):
    return pltpu.make_async_remote_copy(
        src_ref=src, dst_ref=dst, send_sem=send, recv_sem=recv,
        device_id=device, device_id_type=pl.DeviceIdType.MESH,
    )


def kernel(
    order, latent, q_hbm, ku_hbm, vu_hbm, wo_hbm, out,
    q_raw, ku, vu, q_full, bias, pack, keys, wt, vals,
    top, total, accum, terms_a, terms_b, got_a, got_b, relay_a, relay_b, part_a, part_b, fin_a, fin_b,
    load_sem, ps, pr, lzs, lzr, lcs, lcr, lys, lyr, lds, ldr,
    wps, wpr, wms, wmr, wcs, wcr, vs, vr, xs, xr, yss, ysr, yos, yor,
):
    b = lax.axis_index("blk")
    h = lax.axis_index("head")
    z, c = b // 4, b % 4
    lo, core = c // 2, c % 2
    hi, x = h // 4, h % 4
    up = (b + 4) % NBLK
    down = (b + NBLK - 4) % NBLK
    mate = b + 1 - 2 * core
    side = b + 2 - 4 * lo
    c_mate = c + 1 - 2 * core
    c_side = c + 2 - 4 * lo
    c_diag = c_side + 1 - 2 * core

    loads = [
        pltpu.make_async_copy(src, dst, load_sem.at[i])
        for i, (src, dst) in enumerate(((q_hbm, q_raw), (ku_hbm, ku), (vu_hbm, vu)))
    ]
    mine = wt.at[pl.ds(pl.multiple_of((z * 2 + core) * COLS, 16), COLS)]
    loads.append(pltpu.make_async_copy(wo_hbm, mine, load_sem.at[3]))
    for load in loads[3:] + loads[:3]:
        load.start()

    rows = latent[...].astype(F32)
    second = jnp.concatenate([rows[:, 384:], jnp.zeros((8, 192), F32)], axis=1)
    pack[h] = jnp.concatenate([rows[:, :384], second], axis=0).astype(BF16)

    barrier = pltpu.get_barrier_semaphore()

    def greet(device):
        pl.semaphore_signal(barrier, inc=1, device_id=device, device_id_type=pl.DeviceIdType.MESH)

    @pl.loop(1, 16)
    def _(i):
        greet({"head": (h + i) % 16})

    @pl.loop(0, 4)
    def _(i):
        greet({"blk": side, "head": (hi + i) % 4 * 4 + x})

    greet({"blk": up})
    greet({"blk": down})
    greet({"blk": mate})
    pl.semaphore_wait(barrier, 22)

    def own_rows(i):
        return remote(pack.at[h], pack.at[h], ps.at[i], pr.at[i], {"head": (h + i) % 16})

    def shard(zz, cc):
        return wt.at[pl.ds(pl.multiple_of((zz * 2 + cc) * COLS, 16), COLS)]

    def w_plus(k):
        ref = shard((z + 8 - k) % 8, core)
        return remote(ref, ref, wps.at[k], wpr.at[k], {"blk": up})

    def w_minus(k):
        ref = shard((z + k) % 8, core)
        return remote(ref, ref, wms.at[k], wmr.at[k], {"blk": down})

    def w_core(k):
        zz = (z + 8 - k) % 8 if k < 4 else (z + k - 3) % 8
        ref = shard(zz, core)
        return remote(ref, ref, wcs.at[k], wcr.at[k], {"blk": mate})

    def w_core_in(k):
        zz = (z + 8 - k) % 8 if k < 4 else (z + k - 3) % 8
        ref = shard(zz, 1 - core)
        return remote(ref, ref, wcs.at[k], wcr.at[k], {"blk": mate})

    def w_plus_in(k):
        ref = shard((z + 7 - k) % 8, core)
        return remote(ref, ref, wps.at[k], wpr.at[k], {"blk": up})

    def w_minus_in(k):
        ref = shard((z + 1 + k) % 8, core)
        return remote(ref, ref, wms.at[k], wmr.at[k], {"blk": down})

    loads[3].wait()
    w_plus(0).start()
    w_minus(0).start()

    @pl.loop(1, 16)
    def _(i):
        own_rows(i).start()

    w_core(0).start()

    loads[0].wait()
    loads[1].wait()
    for n in range(HEADS):
        at = slice(n * TOKENS, (n + 1) * TOKENS)
        q_full[at, :LAT] = lax.dot_general(
            q_raw[n, :NOPE, :], ku[n], (((0,), (0,)), ((), ())), preferred_element_type=F32
        ).astype(BF16)
        q_full[at, LAT:] = q_raw[n, NOPE:, :].astype(F32).T.astype(BF16)

    row = lax.broadcasted_iota(jnp.int32, (TOKENS, TOKENS), 0)
    col = lax.broadcasted_iota(jnp.int32, (TOKENS, TOKENS), 1)
    q_pos = jnp.where(row < HALF, order[2 * b], order[2 * b + 1]) * HALF + row % HALF
    for n in range(SPAN):
        src = (b + NBLK - 7 + n) % NBLK
        k_pos = jnp.where(col < HALF, order[2 * src], order[2 * src + 1]) * HALF + col % HALF
        bias[:, n * TOKENS:(n + 1) * TOKENS] = jnp.where(k_pos <= q_pos, 0.0, HIDDEN)

    @pl.loop(1, 16)
    def _(i):
        ref = pack.at[(h + 16 - i) % 16]
        remote(ref, ref, ps.at[i], pr.at[i], {"head": (h + i) % 16}).wait_recv()

    def part_slot(plane, cc, half):
        first = (8 - 4 * plane + cc) * TOKENS + half * HALF
        return keys.at[pl.ds(pl.multiple_of(first, HALF), HALF)]

    def slot(plane, cc):
        return keys.at[pl.ds(pl.multiple_of((8 - 4 * plane + cc) * TOKENS, TOKENS), TOKENS)]

    gathered = pack[...].astype(F32)
    base = pl.multiple_of((8 + c) * TOKENS, TOKENS)
    keys[pl.ds(base, TOKENS), :384] = gathered[:, :8, :].reshape(TOKENS, 384).astype(BF16)
    keys[pl.ds(base, TOKENS), 384:] = gathered[:, 8:, :192].reshape(TOKENS, 192).astype(BF16)

    def l_up(k, half):
        src, dst = part_slot(k, c, half), part_slot(k + 1, c, half)
        return remote(src, dst, lzs.at[k, half], lzr.at[k, half], {"blk": up})

    def l_up_in(k, half):
        ref = part_slot(k + 1, c, half)
        return remote(ref, ref, lzs.at[k, half], lzr.at[k, half], {"blk": up})

    def l_core(p):
        return remote(slot(p, c), slot(p, c), lcs.at[p], lcr.at[p], {"blk": mate})

    def l_core_in(p):
        return remote(slot(p, c_mate), slot(p, c_mate), lcs.at[p], lcr.at[p], {"blk": mate})

    def l_side(j, half):
        ref = part_slot(j + lo, c, half)
        return remote(ref, ref, lys.at[j, half], lyr.at[j, half], {"blk": side})

    def l_side_in(j, half):
        ref = part_slot(j + 1 - lo, c_side, half)
        return remote(ref, ref, lys.at[j, half], lyr.at[j, half], {"blk": side})

    def l_diag(j):
        ref = slot(j + 1 - lo, c_side)
        return remote(ref, ref, lds.at[j], ldr.at[j], {"blk": mate})

    def l_diag_in(j):
        ref = slot(j + 1 - lo, c_diag)
        return remote(ref, ref, lds.at[j], ldr.at[j], {"blk": mate})

    def w_step_plus(k):
        w_plus_in(k - 1).wait_recv()
        if k < 3:
            w_plus(k).start()
        w_core(k).start()

    def w_step_minus(k):
        w_minus_in(k - 1).wait_recv()
        if k < 4:
            w_minus(k).start()
        w_core(3 + k).start()

    l_up(0, 0).start()
    l_up(0, 1).start()

    @pl.when(lo == 0)
    def _():
        l_side(0, 0).start()
        l_side(0, 1).start()

    l_core(0).start()
    w_step_minus(1)
    for half in range(2):
        l_up_in(0, half).wait_recv()
        l_up(1, half).start()
        l_side(1 - lo, half).start()

    l_core(1).start()
    w_step_plus(1)
    l_side_in(0, 0).wait_recv()
    l_side_in(0, 1).wait_recv()
    l_diag(0).start()
    for half in range(2):
        l_up_in(1, half).wait_recv()

        @pl.when(lo == 1)
        def _():
            l_side(1, half).start()

    l_core(2).start()
    w_step_minus(2)
    l_core_in(0).wait_recv()
    l_core_in(1).wait_recv()
    l_diag_in(0).wait_recv()

    def scores(i, start, first):
        q = q_full[pl.ds(pl.multiple_of(i * 256, 256), 256), :]
        k = keys[pl.ds(pl.multiple_of(start, TOKENS), 512), :]
        sc = nt_dot(q, k).reshape(2, TOKENS, 512) + bias[:, first:first + 512][None]
        return sc.reshape(256, 512), k

    def near(i):
        at = pl.ds(pl.multiple_of(i * 256, 256), 256)
        sc, k = scores(i, (c + 5) * TOKENS, 512)
        m = jnp.max(sc, axis=1, keepdims=True)
        e = jnp.exp2((sc - m) * GAIN)
        top[at, :] = jnp.broadcast_to(m, (256, 128))
        total[at, :] = jnp.broadcast_to(jnp.sum(e, axis=1, keepdims=True), (256, 128))
        accum[at, :] = jnp.dot(e.astype(BF16), k[:, :LAT], preferred_element_type=F32)

    def v_out(i):
        ref = vals.at[lo, :, pl.ds(pl.multiple_of(i * 256, 256), 256)]
        return remote(ref, ref, vs.at[i], vr.at[i], {"blk": side})

    def v_in(i):
        ref = vals.at[1 - lo, :, pl.ds(pl.multiple_of(i * 256, 256), 256)]
        return remote(ref, ref, vs.at[i], vr.at[i], {"blk": side})

    def far(i):
        at = pl.ds(pl.multiple_of(i * 256, 256), 256)
        sc, k = scores(i, (c + 1) * TOKENS, 0)
        old = top[at, :][:, :1]
        m = jnp.maximum(old, jnp.max(sc, axis=1, keepdims=True))
        e = jnp.exp2((sc - m) * GAIN)
        shrink = jnp.exp2((old - m) * GAIN)
        tot = total[at, :][:, :1] * shrink + jnp.sum(e, axis=1, keepdims=True)
        acc = accum[at, :] * shrink + jnp.dot(e.astype(BF16), k[:, :LAT], preferred_element_type=F32)
        ctx = (acc * (1.0 / tot)).astype(BF16)
        for n in range(2):
            v = jnp.dot(ctx[n * TOKENS:(n + 1) * TOKENS], vu[2 * i + n], preferred_element_type=F32)
            vals[lo, :, pl.ds(pl.multiple_of(i * 256 + n * VAL, VAL), VAL)] = v.astype(BF16)
        v_out(i).start()

    pl.loop(0, 2)(near)
    w_step_plus(2)
    l_side_in(1, 0).wait_recv()
    l_side_in(1, 1).wait_recv()
    l_diag(1).start()
    pl.loop(2, 4)(near)
    w_step_minus(3)
    loads[2].wait()
    l_core_in(2).wait_recv()
    l_diag_in(1).wait_recv()
    pl.loop(0, 2)(far)
    w_step_plus(3)
    pl.loop(2, 4)(far)
    w_step_minus(4)
    for k in range(8):
        w_core_in(k).wait_recv()

    def x_out(y, n, step, way, kind):
        terms, got, relay = ((terms_a, got_a, relay_a), (terms_b, got_b, relay_b))[n]
        xd = (x + 1 + 2 * way) % 4
        if kind == 0:
            src, dst = terms.at[y, way, :, (x + 2) % 4], relay.at[y, way]
        else:
            half = 1 - way if kind == 1 else way
            src, dst = terms.at[y, half, :, xd], got.at[y, way, half]
        sem = (n, step, way, kind)
        return remote(src, dst, xs.at[sem], xr.at[sem], {"head": hi * 4 + xd})

    def project(y, n, step):
        first, width = WIDE[n]
        terms = (terms_a, terms_b)[n]
        t = nt_dot(vals[y], wt[first:first + 2 * width, :])
        left = t[:, :width].reshape(16, 8, width)
        right = t[:, width:].reshape(16, 8, width)
        both = jnp.concatenate([left, right], axis=1).astype(BF16)
        terms[y] = both.reshape(2, 2, 4, 16, width)
        for kind in range(2):
            for way in range(2):
                x_out(y, n, step, way, kind).start()

    def pass_on(y, n, step):
        terms, relay = ((terms_a, relay_a), (terms_b, relay_b))[n]
        for way in range(2):
            x_out(y, n, step, way, 0).wait_recv()
            xd = (x + 1 + 2 * way) % 4
            t = terms[y, way, :, xd].astype(F32) + relay[y, way].astype(F32)
            terms[y, way, :, xd] = t.astype(BF16)
            x_out(y, n, step, way, 2).start()

    def y_same(n, e):
        part, fin = ((part_a, fin_a), (part_b, fin_b))[n]
        yd = (hi + e) % 4
        return remote(
            part.at[lo, yd], fin.at[0, e], yss.at[n, e], ysr.at[n, e], {"head": yd * 4 + x}
        )

    def y_other(n, e):
        part, fin = ((part_a, fin_a), (part_b, fin_b))[n]
        yd = (hi + e) % 4
        return remote(
            part.at[1 - lo, yd], fin.at[1, e], yos.at[n, e], yor.at[n, e],
            {"blk": side, "head": yd * 4 + x},
        )

    def combine(y, n, step):
        terms, got, part = ((terms_a, got_a, part_a), (terms_b, got_b, part_b))[n]
        width = WIDE[n][1]
        for way in range(2):
            x_out(y, n, step, way, 1).wait_recv()
            x_out(y, n, step, way, 2).wait_recv()
        t = terms[y, :, :, x].astype(F32) + got[y, 0].astype(F32) + got[y, 1].astype(F32)
        part[y] = t.reshape(4, 16, width).astype(BF16)

    project(lo, 0, 0)
    project(lo, 1, 0)
    pass_on(lo, 0, 0)
    for i in range(4):
        v_in(i).wait_recv()
    project(1 - lo, 0, 1)
    pass_on(lo, 1, 0)
    project(1 - lo, 1, 1)
    pass_on(1 - lo, 0, 1)
    pass_on(1 - lo, 1, 1)
    for n in range(2):
        combine(lo, n, 0)
        for e in (2, 1, 3):
            y_same(n, e).start()
    for n in range(2):
        combine(1 - lo, n, 1)
        for e in (2, 1, 3, 0):
            y_other(n, e).start()
    same_cols, other_cols = [], []
    for n in range(2):
        part, fin = ((part_a, fin_a), (part_b, fin_b))[n]
        same = part[lo, hi].astype(F32)
        for e in (1, 2, 3):
            y_same(n, e).wait_recv()
            same = same + fin[0, e].astype(F32)
        y_other(n, 0).wait_recv()
        other = fin[1, 0].astype(F32)
        for e in (1, 2, 3):
            y_other(n, e).wait_recv()
            other = other + fin[1, e].astype(F32)
        same_cols += [same[:8], same[8:]]
        other_cols += [other[:8], other[8:]]
    same = jnp.concatenate(same_cols, axis=1)
    other = jnp.concatenate(other_cols, axis=1)
    by_y = (jnp.where(lo == 0, same, other), jnp.where(lo == 0, other, same))
    pair = 2 * COLS
    out[...] = jnp.concatenate(
        [by_y[i % 2][:, i // 2 * pair:(i // 2 + 1) * pair] for i in range(16)], axis=1
    ).astype(BF16)

    @pl.loop(1, 16)
    def _(i):
        own_rows(i).wait_send()

    for k in range(2):
        for half in range(2):
            l_up(k, half).wait_send()
            l_side(k, half).wait_send()
        l_diag(k).wait_send()
    for k in range(3):
        l_core(k).wait_send()
        w_plus(k).wait_send()
    for k in range(4):
        w_minus(k).wait_send()
        v_out(k).wait_send()
    for k in range(8):
        w_core(k).wait_send()
    for n in range(2):
        for way in range(2):
            for kind in range(3):
                x_out(lo, n, 0, way, kind).wait_send()
                x_out(1 - lo, n, 1, way, kind).wait_send()
        for e in (1, 2, 3):
            y_same(n, e).wait_send()
        for e in range(4):
            y_other(n, e).wait_send()


def shards(queries, latent, key_up_weight, value_up_weight, w_o, block_order):
    vmem = pl.BlockSpec(memory_space=pltpu.VMEM)
    anywhere = pl.BlockSpec(memory_space=pl.ANY)
    dma = pltpu.SemaphoreType.DMA
    rows = TOKENS * HEADS
    scratch = [
        pltpu.VMEM((HEADS, NOPE + ROT, TOKENS), BF16),
        pltpu.VMEM((HEADS, NOPE, LAT), BF16),
        pltpu.VMEM((HEADS, LAT, VAL), BF16),
        pltpu.VMEM((rows, WIDTH), BF16),
        pltpu.VMEM((TOKENS, SPAN * TOKENS), F32),
        pltpu.VMEM((16, 16, 384), BF16),
        pltpu.VMEM((12 * TOKENS, WIDTH), BF16),
        pltpu.VMEM((MINE, HEADS * VAL), BF16),
        pltpu.VMEM((2, TOKENS, HEADS * VAL), BF16),
        pltpu.VMEM((rows, 128), F32),
        pltpu.VMEM((rows, 128), F32),
        pltpu.VMEM((rows, LAT), F32),
        pltpu.VMEM((2, 2, 2, 4, 16, 512), BF16),
        pltpu.VMEM((2, 2, 2, 4, 16, 384), BF16),
        pltpu.VMEM((2, 2, 2, 2, 16, 512), BF16),
        pltpu.VMEM((2, 2, 2, 2, 16, 384), BF16),
        pltpu.VMEM((2, 2, 2, 16, 512), BF16),
        pltpu.VMEM((2, 2, 2, 16, 384), BF16),
        pltpu.VMEM((2, 4, 16, 512), BF16),
        pltpu.VMEM((2, 4, 16, 384), BF16),
        pltpu.VMEM((2, 4, 16, 512), BF16),
        pltpu.VMEM((2, 4, 16, 384), BF16),
        dma((4,)),
        dma((16,)), dma((16,)),
        dma((2, 2)), dma((2, 2)),
        dma((3,)), dma((3,)),
        dma((2, 2)), dma((2, 2)),
        dma((2,)), dma((2,)),
        dma((3,)), dma((3,)),
        dma((4,)), dma((4,)),
        dma((8,)), dma((8,)),
        dma((4,)), dma((4,)),
        dma((2, 2, 2, 3)), dma((2, 2, 2, 3)),
        dma((2, 4)), dma((2, 4)),
        dma((2, 4)), dma((2, 4)),
    ]
    return pl.pallas_call(
        kernel,
        out_shape=jax.ShapeDtypeStruct((8, 2 * MINE), BF16),
        in_specs=[pl.BlockSpec(memory_space=pltpu.SMEM), vmem] + [anywhere] * 4,
        out_specs=vmem,
        scratch_shapes=scratch,
        compiler_params=pltpu.CompilerParams(
            collective_id=0, has_side_effects=True, vmem_limit_bytes=60 * 1024 * 1024
        ),
        cost_estimate=pl.CostEstimate(flops=3_500_000_000, bytes_accessed=3_000_000, transcendentals=1_048_576),
    )(block_order, latent, queries.transpose(1, 2, 0), key_up_weight, value_up_weight, w_o.T)


def solution(mesh):
    placed = (
        P("blk", "head", None),
        P(("blk", "head"), None),
        P("head", None, None),
        P("head", None, None),
        P("head", "blk"),
        P(),
    )
    return jax.shard_map(
        shards, mesh=mesh, in_specs=placed, out_specs=P(("blk", "head"), None), check_vma=False
    )
```

```python
import functools
import math

import jax
import jax.numpy as jnp
from jax import lax
from jax.experimental import pallas as pl
from jax.experimental.pallas import tpu as pltpu
from jax.sharding import PartitionSpec as P

NOPE = 128
ROT = 64
LAT = 512
WIDTH = LAT + ROT
VAL = 128
HEADS = 8
TOKENS = 128
HALF = 64
SPAN = 8
NBLK = 32
COLS = 112
MINE = 1792
WIDE = ((0, 512), (1024, 384))
GAIN = (NOPE + ROT) ** (-0.5) * math.log2(math.e)
HIDDEN = -1e30
NT = (((1,), (1,)), ((), ()))
F32 = jnp.float32
BF16 = jnp.bfloat16


def nt_dot(a, b):
    return lax.dot_general(a, b, NT, preferred_element_type=F32)


def remote(src, dst, send, recv, device):
    return pltpu.make_async_remote_copy(
        src_ref=src, dst_ref=dst, send_sem=send, recv_sem=recv,
        device_id=device, device_id_type=pl.DeviceIdType.MESH,
    )


def kernel(
    order, latent, q_hbm, ku_hbm, vu_hbm, wo_hbm, out,
    q_raw, ku, vu, q_full, bias, pack, keys, wt, vals,
    top, total, accum, score, prob, ctx, terms_a, terms_b, got_a, got_b, relay_a, relay_b, part_a, part_b, fin_a, fin_b,
    load_sem, ps, pr, lzs, lzr, lcs, lcr, lys, lyr, lds, ldr,
    wps, wpr, wms, wmr, wcs, wcr, vs, vr, xs, xr, yss, ysr, yos, yor,
):
    b = lax.axis_index("blk")
    h = lax.axis_index("head")
    z, c = b // 4, b % 4
    lo, core = c // 2, c % 2
    hi, x = h // 4, h % 4
    up = (b + 4) % NBLK
    down = (b + NBLK - 4) % NBLK
    mate = b + 1 - 2 * core
    side = b + 2 - 4 * lo
    c_mate = c + 1 - 2 * core
    c_side = c + 2 - 4 * lo
    c_diag = c_side + 1 - 2 * core

    loads = [
        pltpu.make_async_copy(src, dst, load_sem.at[i])
        for i, (src, dst) in enumerate(((q_hbm, q_raw), (ku_hbm, ku), (vu_hbm, vu)))
    ]
    mine = wt.at[pl.ds(pl.multiple_of((z * 2 + core) * COLS, 16), COLS)]
    loads.append(pltpu.make_async_copy(wo_hbm, mine, load_sem.at[3]))
    for load in loads[3:] + loads[:3]:
        load.start()

    rows = latent[...].astype(F32)
    second = jnp.concatenate([rows[:, 384:], jnp.zeros((8, 192), F32)], axis=1)
    pack[h] = jnp.concatenate([rows[:, :384], second], axis=0).astype(BF16)

    barrier = pltpu.get_barrier_semaphore()

    def greet(device):
        pl.semaphore_signal(barrier, inc=1, device_id=device, device_id_type=pl.DeviceIdType.MESH)

    @pl.loop(1, 16)
    def _(i):
        greet({"head": (h + i) % 16})

    @pl.loop(0, 4)
    def _(i):
        greet({"blk": side, "head": (hi + i) % 4 * 4 + x})

    greet({"blk": up})
    greet({"blk": down})
    greet({"blk": mate})
    pl.semaphore_wait(barrier, 22)

    def own_rows(i):
        return remote(pack.at[h], pack.at[h], ps.at[i], pr.at[i], {"head": (h + i) % 16})

    def shard(zz, cc):
        return wt.at[pl.ds(pl.multiple_of((zz * 2 + cc) * COLS, 16), COLS)]

    def w_plus(k):
        ref = shard((z + 8 - k) % 8, core)
        return remote(ref, ref, wps.at[k], wpr.at[k], {"blk": up})

    def w_minus(k):
        ref = shard((z + k) % 8, core)
        return remote(ref, ref, wms.at[k], wmr.at[k], {"blk": down})

    def w_core(k):
        zz = (z + 8 - k) % 8 if k < 4 else (z + k - 3) % 8
        ref = shard(zz, core)
        return remote(ref, ref, wcs.at[k], wcr.at[k], {"blk": mate})

    def w_core_in(k):
        zz = (z + 8 - k) % 8 if k < 4 else (z + k - 3) % 8
        ref = shard(zz, 1 - core)
        return remote(ref, ref, wcs.at[k], wcr.at[k], {"blk": mate})

    def w_plus_in(k):
        ref = shard((z + 7 - k) % 8, core)
        return remote(ref, ref, wps.at[k], wpr.at[k], {"blk": up})

    def w_minus_in(k):
        ref = shard((z + 1 + k) % 8, core)
        return remote(ref, ref, wms.at[k], wmr.at[k], {"blk": down})

    loads[3].wait()
    w_plus(0).start()
    w_minus(0).start()

    @pl.loop(1, 16)
    def _(i):
        own_rows(i).start()

    w_core(0).start()

    loads[0].wait()
    loads[1].wait()
    for n in range(HEADS):
        lat = lax.dot_general(
            q_raw[n, :NOPE, :], ku[n], (((0,), (0,)), ((), ())), preferred_element_type=F32
        ).astype(BF16)
        turned = q_raw[n, NOPE:, :].astype(F32).T.astype(BF16)
        for t in range(2):
            at = slice(t * 512 + n * HALF, t * 512 + (n + 1) * HALF)
            q_full[at, :LAT] = lat[t * HALF:(t + 1) * HALF]
            q_full[at, LAT:] = turned[t * HALF:(t + 1) * HALF]

    row = lax.broadcasted_iota(jnp.int32, (TOKENS, TOKENS), 0)
    col = lax.broadcasted_iota(jnp.int32, (TOKENS, TOKENS), 1)
    q_pos = jnp.where(row < HALF, order[2 * b], order[2 * b + 1]) * HALF + row % HALF
    for n in range(SPAN):
        src = (b + NBLK - 7 + n) % NBLK
        k_pos = jnp.where(col < HALF, order[2 * src], order[2 * src + 1]) * HALF + col % HALF
        bias[:, n * TOKENS:(n + 1) * TOKENS] = jnp.where(k_pos <= q_pos, 0.0, HIDDEN)

    @pl.loop(1, 16)
    def _(i):
        ref = pack.at[(h + 16 - i) % 16]
        remote(ref, ref, ps.at[i], pr.at[i], {"head": (h + i) % 16}).wait_recv()

    def part_slot(plane, cc, half):
        first = (8 - 4 * plane + cc) * TOKENS + half * HALF
        return keys.at[pl.ds(pl.multiple_of(first, HALF), HALF)]

    def slot(plane, cc):
        return keys.at[pl.ds(pl.multiple_of((8 - 4 * plane + cc) * TOKENS, TOKENS), TOKENS)]

    gathered = pack[...].astype(F32)
    base = pl.multiple_of((8 + c) * TOKENS, TOKENS)
    keys[pl.ds(base, TOKENS), :384] = gathered[:, :8, :].reshape(TOKENS, 384).astype(BF16)
    keys[pl.ds(base, TOKENS), 384:] = gathered[:, 8:, :192].reshape(TOKENS, 192).astype(BF16)

    def l_up(k, half):
        src, dst = part_slot(k, c, half), part_slot(k + 1, c, half)
        return remote(src, dst, lzs.at[k, half], lzr.at[k, half], {"blk": up})

    def l_up_in(k, half):
        ref = part_slot(k + 1, c, half)
        return remote(ref, ref, lzs.at[k, half], lzr.at[k, half], {"blk": up})

    def l_core(p):
        return remote(slot(p, c), slot(p, c), lcs.at[p], lcr.at[p], {"blk": mate})

    def l_core_in(p):
        return remote(slot(p, c_mate), slot(p, c_mate), lcs.at[p], lcr.at[p], {"blk": mate})

    def l_side(j, half):
        ref = part_slot(j + lo, c, half)
        return remote(ref, ref, lys.at[j, half], lyr.at[j, half], {"blk": side})

    def l_side_in(j, half):
        ref = part_slot(j + 1 - lo, c_side, half)
        return remote(ref, ref, lys.at[j, half], lyr.at[j, half], {"blk": side})

    def l_diag(j):
        ref = slot(j + 1 - lo, c_side)
        return remote(ref, ref, lds.at[j], ldr.at[j], {"blk": mate})

    def l_diag_in(j):
        ref = slot(j + 1 - lo, c_diag)
        return remote(ref, ref, lds.at[j], ldr.at[j], {"blk": mate})

    def w_step_plus(k):
        w_plus_in(k - 1).wait_recv()
        if k < 3:
            w_plus(k).start()
        w_core(k).start()

    def w_step_minus(k):
        w_minus_in(k - 1).wait_recv()
        if k < 4:
            w_minus(k).start()
        w_core(3 + k).start()

    l_up(0, 0).start()
    l_up(0, 1).start()

    @pl.when(lo == 0)
    def _():
        l_side(0, 0).start()
        l_side(0, 1).start()

    l_core(0).start()
    w_step_minus(1)
    for half in range(2):
        l_up_in(0, half).wait_recv()
        l_up(1, half).start()
        l_side(1 - lo, half).start()

    l_core(1).start()
    w_step_plus(1)
    l_side_in(0, 0).wait_recv()
    l_side_in(0, 1).wait_recv()
    l_diag(0).start()
    for half in range(2):
        l_up_in(1, half).wait_recv()

        @pl.when(lo == 1)
        def _():
            l_side(1, half).start()

    l_core(2).start()
    w_step_minus(2)
    l_core_in(0).wait_recv()
    l_core_in(1).wait_recv()
    l_diag_in(0).wait_recv()

    def v_out(t):
        ref = vals.at[t, lo]
        return remote(ref, ref, vs.at[t], vr.at[t], {"blk": side})

    def v_in(t):
        ref = vals.at[t, 1 - lo]
        return remote(ref, ref, vs.at[t], vr.at[t], {"blk": side})

    def rows_at(t, g, first, count):
        return pl.ds(pl.multiple_of(t * 512 + g * 256 + first, 32), count)

    def step(t, start, first, last):
        k = keys[pl.ds(pl.multiple_of(start, TOKENS), 512), :]
        for g in range(2):
            score[g] = nt_dot(q_full[rows_at(t, g, 0, 256), :], k)
        for g in range(2):
            factors = []
            for r in range(8):
                at = rows_at(t, g, r * 32, 32)
                tok = pl.ds(pl.multiple_of(t * HALF + r % 2 * 32, 32), 32)
                sc = score[g, r * 32:(r + 1) * 32, :] + bias[tok, first:first + 512]
                m = jnp.max(sc, axis=1, keepdims=True)
                if last:
                    old = top[at, :][:, :1]
                    m = jnp.maximum(m, old)
                e = jnp.exp2((sc - m) * GAIN)
                add = jnp.sum(e, axis=1, keepdims=True)
                prob[g, r * 32:(r + 1) * 32, :] = e.astype(BF16)
                if last:
                    shrink = jnp.exp2((old - m) * GAIN)
                    inverse = 1.0 / (total[at, :][:, :1] * shrink + add)
                    factors.append((shrink * inverse, inverse))
                else:
                    top[at, :] = jnp.broadcast_to(m, (32, 128))
                    total[at, :] = jnp.broadcast_to(add, (32, 128))
            got = jnp.dot(prob[g], k[:, :LAT], preferred_element_type=F32)
            if not last:
                accum[rows_at(t, g, 0, 256), :] = got
                continue
            score[g] = got
            for r in range(8):
                old, new = factors[r]
                ctx[g, r * 32:(r + 1) * 32, :] = (
                    accum[rows_at(t, g, r * 32, 32), :] * old + score[g, r * 32:(r + 1) * 32, :] * new
                ).astype(BF16)
            for n in range(4):
                head = 4 * g + n
                v = jnp.dot(ctx[g, n * HALF:(n + 1) * HALF, :], vu[head], preferred_element_type=F32)
                vals[t, lo, :, head * VAL:(head + 1) * VAL] = v.astype(BF16)

    @pl.loop(0, 2)
    def _(t):
        step(t, (c + 5) * TOKENS, 512, False)

        @pl.when(t == 0)
        def _():
            w_step_plus(2)
            l_side_in(1, 0).wait_recv()
            l_side_in(1, 1).wait_recv()
            l_diag(1).start()

    w_step_minus(3)
    loads[2].wait()
    l_core_in(2).wait_recv()
    l_diag_in(1).wait_recv()

    @pl.loop(0, 2)
    def _(t):
        step(t, (c + 1) * TOKENS, 0, True)
        v_out(t).start()

        @pl.when(t == 0)
        def _():
            w_step_plus(3)

    w_step_minus(4)
    for k in range(8):
        w_core_in(k).wait_recv()

    def x_out(t, n, way, kind):
        terms, got, relay = ((terms_a, got_a, relay_a), (terms_b, got_b, relay_b))[n]
        xd = (x + 1 + 2 * way) % 4
        if kind == 0:
            src, dst = terms.at[t, way, (x + 2) % 4], relay.at[t, way]
        else:
            r = 1 - way if kind == 1 else way
            src, dst = terms.at[t, r, xd], got.at[t, way, r]
        sem = (t, n, way, kind)
        return remote(src, dst, xs.at[sem], xr.at[sem], {"head": hi * 4 + xd})

    def project(t, n):
        first, width = WIDE[n]
        terms = (terms_a, terms_b)[n]
        both = vals[t].reshape(TOKENS, HEADS * VAL)
        out = nt_dot(both, wt[first:first + 2 * width, :])
        for y in range(2):
            left = out[y * HALF:(y + 1) * HALF, :width].reshape(8, 8, width)
            right = out[y * HALF:(y + 1) * HALF, width:].reshape(8, 8, width)
            pair = jnp.concatenate([left, right], axis=1).astype(BF16)
            terms[t, :, :, y] = pair.reshape(2, 4, 16, width)
        for kind in range(2):
            for way in range(2):
                x_out(t, n, way, kind).start()

    def pass_on(t, n):
        terms, relay = ((terms_a, relay_a), (terms_b, relay_b))[n]
        for way in range(2):
            x_out(t, n, way, 0).wait_recv()
            xd = (x + 1 + 2 * way) % 4
            both = terms[t, way, xd].astype(F32) + relay[t, way].astype(F32)
            terms[t, way, xd] = both.astype(BF16)
            x_out(t, n, way, 2).start()

    def y_same(n, yd, src):
        part, fin = ((part_a, fin_a), (part_b, fin_b))[n]
        return remote(
            part.at[yd, lo], fin.at[0, src], yss.at[n, yd], ysr.at[n, src], {"head": yd * 4 + x}
        )

    def y_other(n, yd, src):
        part, fin = ((part_a, fin_a), (part_b, fin_b))[n]
        return remote(
            part.at[yd, 1 - lo], fin.at[1, src], yos.at[n, yd], yor.at[n, src],
            {"blk": side, "head": yd * 4 + x},
        )

    def combine(t, n):
        terms, got, part = ((terms_a, got_a, part_a), (terms_b, got_b, part_b))[n]
        for way in range(2):
            x_out(t, n, way, 1).wait_recv()
            x_out(t, n, way, 2).wait_recv()
        both = terms[t, :, x].astype(F32) + got[t, 0].astype(F32) + got[t, 1].astype(F32)
        part[2 * t:2 * t + 2] = both.astype(BF16)
        for yd in (2 * t, 2 * t + 1):
            y_other(n, yd, hi).start()

            @pl.when(hi != yd)
            def _():
                y_same(n, yd, hi).start()

    v_in(0).wait_recv()
    project(0, 0)
    project(0, 1)
    pass_on(0, 0)
    v_in(1).wait_recv()
    project(1, 0)
    pass_on(0, 1)
    project(1, 1)
    combine(0, 0)
    pass_on(1, 0)
    combine(0, 1)
    pass_on(1, 1)
    combine(1, 0)
    combine(1, 1)
    same_cols, other_cols = [], []
    for n in range(2):
        part, fin = ((part_a, fin_a), (part_b, fin_b))[n]
        same = part[hi, lo].astype(F32)
        other = jnp.zeros_like(same)
        for e in (1, 2, 3):
            src = (hi + e) % 4
            y_same(n, src, src).wait_recv()
            same = same + fin[0, src].astype(F32)
        for src in range(4):
            y_other(n, src, src).wait_recv()
            other = other + fin[1, src].astype(F32)
        same_cols += [same[:8], same[8:]]
        other_cols += [other[:8], other[8:]]
    same = jnp.concatenate(same_cols, axis=1)
    other = jnp.concatenate(other_cols, axis=1)
    by_y = (jnp.where(lo == 0, same, other), jnp.where(lo == 0, other, same))
    pair = 2 * COLS
    out[...] = jnp.concatenate(
        [by_y[i % 2][:, i // 2 * pair:(i // 2 + 1) * pair] for i in range(16)], axis=1
    ).astype(BF16)

    @pl.loop(1, 16)
    def _(i):
        own_rows(i).wait_send()

    for k in range(2):
        for half in range(2):
            l_up(k, half).wait_send()
            l_side(k, half).wait_send()
        l_diag(k).wait_send()
    for k in range(3):
        l_core(k).wait_send()
        w_plus(k).wait_send()
    for k in range(4):
        w_minus(k).wait_send()
    for k in range(8):
        w_core(k).wait_send()
    for t in range(2):
        v_out(t).wait_send()
    for n in range(2):
        for t in range(2):
            for way in range(2):
                for kind in range(3):
                    x_out(t, n, way, kind).wait_send()
        for yd in range(4):
            y_other(n, yd, hi).wait_send()
        for e in (1, 2, 3):
            y_same(n, (hi + e) % 4, hi).wait_send()


def shards(queries, latent, key_up_weight, value_up_weight, w_o, block_order):
    vmem = pl.BlockSpec(memory_space=pltpu.VMEM)
    anywhere = pl.BlockSpec(memory_space=pl.ANY)
    dma = pltpu.SemaphoreType.DMA
    rows = TOKENS * HEADS
    scratch = [
        pltpu.VMEM((HEADS, NOPE + ROT, TOKENS), BF16),
        pltpu.VMEM((HEADS, NOPE, LAT), BF16),
        pltpu.VMEM((HEADS, LAT, VAL), BF16),
        pltpu.VMEM((rows, WIDTH), BF16),
        pltpu.VMEM((TOKENS, SPAN * TOKENS), F32),
        pltpu.VMEM((16, 16, 384), BF16),
        pltpu.VMEM((12 * TOKENS, WIDTH), BF16),
        pltpu.VMEM((MINE, HEADS * VAL), BF16),
        pltpu.VMEM((2, 2, HALF, HEADS * VAL), BF16),
        pltpu.VMEM((rows, 128), F32),
        pltpu.VMEM((rows, 128), F32),
        pltpu.VMEM((rows, LAT), F32),
        pltpu.VMEM((2, 256, LAT), F32),
        pltpu.VMEM((2, 256, LAT), BF16),
        pltpu.VMEM((2, 256, LAT), BF16),
        pltpu.VMEM((2, 2, 4, 2, 16, 512), BF16),
        pltpu.VMEM((2, 2, 4, 2, 16, 384), BF16),
        pltpu.VMEM((2, 2, 2, 2, 16, 512), BF16),
        pltpu.VMEM((2, 2, 2, 2, 16, 384), BF16),
        pltpu.VMEM((2, 2, 2, 16, 512), BF16),
        pltpu.VMEM((2, 2, 2, 16, 384), BF16),
        pltpu.VMEM((4, 2, 16, 512), BF16),
        pltpu.VMEM((4, 2, 16, 384), BF16),
        pltpu.VMEM((2, 4, 16, 512), BF16),
        pltpu.VMEM((2, 4, 16, 384), BF16),
        dma((4,)),
        dma((16,)), dma((16,)),
        dma((2, 2)), dma((2, 2)),
        dma((3,)), dma((3,)),
        dma((2, 2)), dma((2, 2)),
        dma((2,)), dma((2,)),
        dma((3,)), dma((3,)),
        dma((4,)), dma((4,)),
        dma((8,)), dma((8,)),
        dma((2,)), dma((2,)),
        dma((2, 2, 2, 3)), dma((2, 2, 2, 3)),
        dma((2, 4)), dma((2, 4)),
        dma((2, 4)), dma((2, 4)),
    ]
    return pl.pallas_call(
        kernel,
        out_shape=jax.ShapeDtypeStruct((8, 2 * MINE), BF16),
        in_specs=[pl.BlockSpec(memory_space=pltpu.SMEM), vmem] + [anywhere] * 4,
        out_specs=vmem,
        scratch_shapes=scratch,
        compiler_params=pltpu.CompilerParams(
            collective_id=0, has_side_effects=True, vmem_limit_bytes=60 * 1024 * 1024
        ),
        cost_estimate=pl.CostEstimate(flops=3_500_000_000, bytes_accessed=3_000_000, transcendentals=1_048_576),
    )(block_order, latent, queries.transpose(1, 2, 0), key_up_weight, value_up_weight, w_o.T)


def solution(mesh):
    placed = (
        P("blk", "head", None),
        P(("blk", "head"), None),
        P("head", None, None),
        P("head", None, None),
        P("head", "blk"),
        P(),
    )
    return jax.shard_map(
        shards, mesh=mesh, in_specs=placed, out_specs=P(("blk", "head"), None), check_vma=False
    )
```

```python
import functools
import math

import jax
import jax.numpy as jnp
from jax import lax
from jax.experimental import pallas as pl
from jax.experimental.pallas import tpu as pltpu
from jax.sharding import PartitionSpec as P

NOPE = 128
ROT = 64
LAT = 512
WIDTH = LAT + ROT
VAL = 128
HEADS = 8
TOKENS = 128
HALF = 64
SPAN = 8
NBLK = 32
COLS = 112
MINE = 1792
WIDE = ((0, 512), (1024, 384))
GAIN = (NOPE + ROT) ** (-0.5) * math.log2(math.e)
HIDDEN = -1e30
NT = (((1,), (1,)), ((), ()))
F32 = jnp.float32
BF16 = jnp.bfloat16


def nt_dot(a, b):
    return lax.dot_general(a, b, NT, preferred_element_type=F32)


def remote(src, dst, send, recv, device):
    return pltpu.make_async_remote_copy(
        src_ref=src, dst_ref=dst, send_sem=send, recv_sem=recv,
        device_id=device, device_id_type=pl.DeviceIdType.MESH,
    )


def kernel(
    order, latent, q_hbm, ku_hbm, vu_hbm, wo_hbm, out,
    q_raw, ku, vu, q_full, bias, pack, keys, wt, vals,
    top, total, accum, score, prob, ctx, terms_a, terms_b, got_a, got_b, relay_a, relay_b, part_a, part_b, fin_a, fin_b,
    load_sem, ps, pr, lzs, lzr, lcs, lcr, lys, lyr, lds, ldr,
    wps, wpr, wms, wmr, wcs, wcr, vs, vr, xs, xr, yss, ysr, yos, yor,
):
    b = lax.axis_index("blk")
    h = lax.axis_index("head")
    z, c = b // 4, b % 4
    lo, core = c // 2, c % 2
    hi, x = h // 4, h % 4
    up = (b + 4) % NBLK
    down = (b + NBLK - 4) % NBLK
    mate = b + 1 - 2 * core
    side = b + 2 - 4 * lo
    c_mate = c + 1 - 2 * core
    c_side = c + 2 - 4 * lo
    c_diag = c_side + 1 - 2 * core

    loads = [
        pltpu.make_async_copy(src, dst, load_sem.at[i])
        for i, (src, dst) in enumerate(((q_hbm, q_raw), (ku_hbm, ku), (vu_hbm, vu)))
    ]
    mine = wt.at[pl.ds(pl.multiple_of((z * 2 + core) * COLS, 16), COLS)]
    loads.append(pltpu.make_async_copy(wo_hbm, mine, load_sem.at[3]))
    for load in loads[3:] + loads[:3]:
        load.start()

    rows = latent[...].astype(F32)
    second = jnp.concatenate([rows[:, 384:], jnp.zeros((8, 192), F32)], axis=1)
    pack[h] = jnp.concatenate([rows[:, :384], second], axis=0).astype(BF16)

    barrier = pltpu.get_barrier_semaphore()

    def greet(device):
        pl.semaphore_signal(barrier, inc=1, device_id=device, device_id_type=pl.DeviceIdType.MESH)

    @pl.loop(1, 16)
    def _(i):
        greet({"head": (h + i) % 16})

    @pl.loop(0, 4)
    def _(i):
        greet({"blk": side, "head": (hi + i) % 4 * 4 + x})

    greet({"blk": up})
    greet({"blk": down})
    greet({"blk": mate})
    pl.semaphore_wait(barrier, 22)

    def own_rows(i):
        return remote(pack.at[h], pack.at[h], ps.at[i], pr.at[i], {"head": (h + i) % 16})

    def shard(zz, cc, half):
        first = (zz * 2 + cc) * COLS + 64 * half
        return wt.at[pl.ds(pl.multiple_of(first, 16), (64, 48)[half])]

    def w_plus(k, half):
        ref = shard((z + 8 - k) % 8, core, half)
        return remote(ref, ref, wps.at[k, half], wpr.at[k, half], {"blk": up})

    def w_minus(k, half):
        ref = shard((z + k) % 8, core, half)
        return remote(ref, ref, wms.at[k, half], wmr.at[k, half], {"blk": down})

    def w_core(k, half):
        zz = (z + 8 - k) % 8 if k < 4 else (z + k - 3) % 8
        ref = shard(zz, core, half)
        return remote(ref, ref, wcs.at[k, half], wcr.at[k, half], {"blk": mate})

    def w_core_in(k, half):
        zz = (z + 8 - k) % 8 if k < 4 else (z + k - 3) % 8
        ref = shard(zz, 1 - core, half)
        return remote(ref, ref, wcs.at[k, half], wcr.at[k, half], {"blk": mate})

    def w_plus_in(k, half):
        ref = shard((z + 7 - k) % 8, core, half)
        return remote(ref, ref, wps.at[k, half], wpr.at[k, half], {"blk": up})

    def w_minus_in(k, half):
        ref = shard((z + 1 + k) % 8, core, half)
        return remote(ref, ref, wms.at[k, half], wmr.at[k, half], {"blk": down})

    def w_step_plus(k, half):
        w_plus_in(k - 1, half).wait_recv()
        if k < 3:
            w_plus(k, half).start()
        w_core(k, half).start()

    def w_step_minus(k, half):
        w_minus_in(k - 1, half).wait_recv()
        if k < 4:
            w_minus(k, half).start()
        w_core(3 + k, half).start()

    loads[3].wait()
    for half in range(2):
        w_plus(0, half).start()
        w_minus(0, half).start()

    @pl.loop(1, 16)
    def _(i):
        own_rows(i).start()

    for half in range(2):
        w_core(0, half).start()

    loads[0].wait()
    loads[1].wait()
    for n in range(HEADS):
        lat = lax.dot_general(
            q_raw[n, :NOPE, :], ku[n], (((0,), (0,)), ((), ())), preferred_element_type=F32
        ).astype(BF16)
        turned = q_raw[n, NOPE:, :].astype(F32).T.astype(BF16)
        for t in range(2):
            at = slice(t * 512 + n * HALF, t * 512 + (n + 1) * HALF)
            q_full[at, :LAT] = lat[t * HALF:(t + 1) * HALF]
            q_full[at, LAT:] = turned[t * HALF:(t + 1) * HALF]

    row = lax.broadcasted_iota(jnp.int32, (TOKENS, TOKENS), 0)
    col = lax.broadcasted_iota(jnp.int32, (TOKENS, TOKENS), 1)
    q_pos = jnp.where(row < HALF, order[2 * b], order[2 * b + 1]) * HALF + row % HALF
    for n in range(SPAN):
        src = (b + NBLK - 7 + n) % NBLK
        k_pos = jnp.where(col < HALF, order[2 * src], order[2 * src + 1]) * HALF + col % HALF
        bias[:, n * TOKENS:(n + 1) * TOKENS] = jnp.where(k_pos <= q_pos, 0.0, HIDDEN)

    @pl.loop(1, 16)
    def _(i):
        ref = pack.at[(h + 16 - i) % 16]
        remote(ref, ref, ps.at[i], pr.at[i], {"head": (h + i) % 16}).wait_recv()

    def part_slot(plane, cc, half):
        first = (8 - 4 * plane + cc) * TOKENS + half * HALF
        return keys.at[pl.ds(pl.multiple_of(first, HALF), HALF)]

    def slot(plane, cc):
        return keys.at[pl.ds(pl.multiple_of((8 - 4 * plane + cc) * TOKENS, TOKENS), TOKENS)]

    gathered = pack[...].astype(F32)
    base = pl.multiple_of((8 + c) * TOKENS, TOKENS)
    keys[pl.ds(base, TOKENS), :384] = gathered[:, :8, :].reshape(TOKENS, 384).astype(BF16)
    keys[pl.ds(base, TOKENS), 384:] = gathered[:, 8:, :192].reshape(TOKENS, 192).astype(BF16)

    def l_up(k, half):
        src, dst = part_slot(k, c, half), part_slot(k + 1, c, half)
        return remote(src, dst, lzs.at[k, half], lzr.at[k, half], {"blk": up})

    def l_up_in(k, half):
        ref = part_slot(k + 1, c, half)
        return remote(ref, ref, lzs.at[k, half], lzr.at[k, half], {"blk": up})

    def l_core(p):
        return remote(slot(p, c), slot(p, c), lcs.at[p], lcr.at[p], {"blk": mate})

    def l_core_in(p):
        return remote(slot(p, c_mate), slot(p, c_mate), lcs.at[p], lcr.at[p], {"blk": mate})

    def l_side(j, half):
        ref = part_slot(j + lo, c, half)
        return remote(ref, ref, lys.at[j, half], lyr.at[j, half], {"blk": side})

    def l_side_in(j, half):
        ref = part_slot(j + 1 - lo, c_side, half)
        return remote(ref, ref, lys.at[j, half], lyr.at[j, half], {"blk": side})

    def l_diag(j):
        ref = slot(j + 1 - lo, c_side)
        return remote(ref, ref, lds.at[j], ldr.at[j], {"blk": mate})

    def l_diag_in(j):
        ref = slot(j + 1 - lo, c_diag)
        return remote(ref, ref, lds.at[j], ldr.at[j], {"blk": mate})

    l_up(0, 0).start()
    l_up(0, 1).start()

    @pl.when(lo == 0)
    def _():
        l_side(0, 0).start()
        l_side(0, 1).start()

    l_core(0).start()
    for half in range(2):
        w_step_minus(1, half)
        w_step_plus(1, half)
    for half in range(2):
        l_up_in(0, half).wait_recv()
        l_up(1, half).start()
        l_side(1 - lo, half).start()

    l_core(1).start()
    for half in range(2):
        w_step_minus(2, half)
        w_step_plus(2, half)
    l_side_in(0, 0).wait_recv()
    l_side_in(0, 1).wait_recv()
    l_diag(0).start()
    for half in range(2):
        l_up_in(1, half).wait_recv()

        @pl.when(lo == 1)
        def _():
            l_side(1, half).start()

    l_core(2).start()
    for half in range(2):
        w_step_minus(3, half)
    l_core_in(0).wait_recv()
    l_core_in(1).wait_recv()
    l_diag_in(0).wait_recv()

    def v_out(t):
        ref = vals.at[t, lo]
        return remote(ref, ref, vs.at[t], vr.at[t], {"blk": side})

    def v_in(t):
        ref = vals.at[t, 1 - lo]
        return remote(ref, ref, vs.at[t], vr.at[t], {"blk": side})

    def rows_at(t, g, first, count):
        return pl.ds(pl.multiple_of(t * 512 + g * 256 + first, 32), count)

    def step(t, start, first, last):
        k = keys[pl.ds(pl.multiple_of(start, TOKENS), 512), :]
        for g in range(2):
            score[g] = nt_dot(q_full[rows_at(t, g, 0, 256), :], k)
        for g in range(2):
            factors = []
            for r in range(8):
                at = rows_at(t, g, r * 32, 32)
                tok = pl.ds(pl.multiple_of(t * HALF + r % 2 * 32, 32), 32)
                sc = score[g, r * 32:(r + 1) * 32, :] + bias[tok, first:first + 512]
                m = jnp.max(sc, axis=1, keepdims=True)
                if last:
                    old = top[at, :][:, :1]
                    m = jnp.maximum(m, old)
                e = jnp.exp2((sc - m) * GAIN)
                add = jnp.sum(e, axis=1, keepdims=True)
                prob[g, r * 32:(r + 1) * 32, :] = e.astype(BF16)
                if last:
                    shrink = jnp.exp2((old - m) * GAIN)
                    inverse = 1.0 / (total[at, :][:, :1] * shrink + add)
                    factors.append((shrink * inverse, inverse))
                else:
                    top[at, :] = jnp.broadcast_to(m, (32, 128))
                    total[at, :] = jnp.broadcast_to(add, (32, 128))
            got = jnp.dot(prob[g], k[:, :LAT], preferred_element_type=F32)
            if not last:
                accum[rows_at(t, g, 0, 256), :] = got
                continue
            score[g] = got
            for r in range(8):
                old, new = factors[r]
                ctx[g, r * 32:(r + 1) * 32, :] = (
                    accum[rows_at(t, g, r * 32, 32), :] * old + score[g, r * 32:(r + 1) * 32, :] * new
                ).astype(BF16)
            for n in range(4):
                head = 4 * g + n
                v = jnp.dot(ctx[g, n * HALF:(n + 1) * HALF, :], vu[head], preferred_element_type=F32)
                vals[t, lo, :, head * VAL:(head + 1) * VAL] = v.astype(BF16)

    @pl.loop(0, 2)
    def _(t):
        step(t, (c + 5) * TOKENS, 512, False)

        @pl.when(t == 0)
        def _():
            l_side_in(1, 0).wait_recv()
            l_side_in(1, 1).wait_recv()
            l_diag(1).start()

    for half in range(2):
        w_step_plus(3, half)
    loads[2].wait()
    l_core_in(2).wait_recv()
    l_diag_in(1).wait_recv()

    @pl.loop(0, 2)
    def _(t):
        step(t, (c + 1) * TOKENS, 0, True)
        v_out(t).start()

        @pl.when(t == 0)
        def _():
            for half in range(2):
                w_step_minus(4, half)

    for k in range(8):
        for half in range(2):
            w_core_in(k, half).wait_recv()

    def x_out(t, n, way, kind):
        terms, got, relay = ((terms_a, got_a, relay_a), (terms_b, got_b, relay_b))[n]
        xd = (x + 1 + 2 * way) % 4
        if kind == 0:
            src, dst = terms.at[t, way, (x + 2) % 4], relay.at[t, way]
        else:
            r = 1 - way if kind == 1 else way
            src, dst = terms.at[t, r, xd], got.at[t, way, r]
        sem = (t, n, way, kind)
        return remote(src, dst, xs.at[sem], xr.at[sem], {"head": hi * 4 + xd})

    def project(t, n):
        first, width = WIDE[n]
        terms = (terms_a, terms_b)[n]
        both = vals[t].reshape(TOKENS, HEADS * VAL)
        out = nt_dot(both, wt[first:first + 2 * width, :])
        for y in range(2):
            left = out[y * HALF:(y + 1) * HALF, :width].reshape(8, 8, width)
            right = out[y * HALF:(y + 1) * HALF, width:].reshape(8, 8, width)
            pair = jnp.concatenate([left, right], axis=1).astype(BF16)
            terms[t, :, :, y] = pair.reshape(2, 4, 16, width)
        for kind in range(2):
            for way in range(2):
                x_out(t, n, way, kind).start()

    def pass_on(t, n):
        terms, relay = ((terms_a, relay_a), (terms_b, relay_b))[n]
        for way in range(2):
            x_out(t, n, way, 0).wait_recv()
            xd = (x + 1 + 2 * way) % 4
            both = terms[t, way, xd].astype(F32) + relay[t, way].astype(F32)
            terms[t, way, xd] = both.astype(BF16)
            x_out(t, n, way, 2).start()

    def y_same(n, yd, src):
        part, fin = ((part_a, fin_a), (part_b, fin_b))[n]
        return remote(
            part.at[yd, lo], fin.at[0, src], yss.at[n, yd], ysr.at[n, src], {"head": yd * 4 + x}
        )

    def y_other(n, yd, src):
        part, fin = ((part_a, fin_a), (part_b, fin_b))[n]
        return remote(
            part.at[yd, 1 - lo], fin.at[1, src], yos.at[n, yd], yor.at[n, src],
            {"blk": side, "head": yd * 4 + x},
        )

    def combine(t, n):
        terms, got, part = ((terms_a, got_a, part_a), (terms_b, got_b, part_b))[n]
        for way in range(2):
            x_out(t, n, way, 1).wait_recv()
            x_out(t, n, way, 2).wait_recv()
        both = terms[t, :, x].astype(F32) + got[t, 0].astype(F32) + got[t, 1].astype(F32)
        part[2 * t:2 * t + 2] = both.astype(BF16)
        for yd in (2 * t, 2 * t + 1):
            y_other(n, yd, hi).start()

            @pl.when(hi != yd)
            def _():
                y_same(n, yd, hi).start()

    v_in(0).wait_recv()
    project(0, 0)
    project(0, 1)
    pass_on(0, 0)
    v_in(1).wait_recv()
    project(1, 0)
    pass_on(0, 1)
    project(1, 1)
    combine(0, 0)
    pass_on(1, 0)
    combine(0, 1)
    pass_on(1, 1)
    combine(1, 0)
    combine(1, 1)
    same_cols, other_cols = [], []
    for n in range(2):
        part, fin = ((part_a, fin_a), (part_b, fin_b))[n]
        same = part[hi, lo].astype(F32)
        other = jnp.zeros_like(same)
        for e in (1, 2, 3):
            src = (hi + e) % 4
            y_same(n, src, src).wait_recv()
            same = same + fin[0, src].astype(F32)
        for src in range(4):
            y_other(n, src, src).wait_recv()
            other = other + fin[1, src].astype(F32)
        same_cols += [same[:8], same[8:]]
        other_cols += [other[:8], other[8:]]
    same = jnp.concatenate(same_cols, axis=1)
    other = jnp.concatenate(other_cols, axis=1)
    by_y = (jnp.where(lo == 0, same, other), jnp.where(lo == 0, other, same))
    pair = 2 * COLS
    out[...] = jnp.concatenate(
        [by_y[i % 2][:, i // 2 * pair:(i // 2 + 1) * pair] for i in range(16)], axis=1
    ).astype(BF16)

    @pl.loop(1, 16)
    def _(i):
        own_rows(i).wait_send()

    for k in range(2):
        for half in range(2):
            l_up(k, half).wait_send()
            l_side(k, half).wait_send()
        l_diag(k).wait_send()
    for k in range(3):
        l_core(k).wait_send()
    for half in range(2):
        for k in range(3):
            w_plus(k, half).wait_send()
        for k in range(4):
            w_minus(k, half).wait_send()
        for k in range(8):
            w_core(k, half).wait_send()
    for t in range(2):
        v_out(t).wait_send()
    for n in range(2):
        for t in range(2):
            for way in range(2):
                for kind in range(3):
                    x_out(t, n, way, kind).wait_send()
        for yd in range(4):
            y_other(n, yd, hi).wait_send()
        for e in (1, 2, 3):
            y_same(n, (hi + e) % 4, hi).wait_send()


def shards(queries, latent, key_up_weight, value_up_weight, w_o, block_order):
    vmem = pl.BlockSpec(memory_space=pltpu.VMEM)
    anywhere = pl.BlockSpec(memory_space=pl.ANY)
    dma = pltpu.SemaphoreType.DMA
    rows = TOKENS * HEADS
    scratch = [
        pltpu.VMEM((HEADS, NOPE + ROT, TOKENS), BF16),
        pltpu.VMEM((HEADS, NOPE, LAT), BF16),
        pltpu.VMEM((HEADS, LAT, VAL), BF16),
        pltpu.VMEM((rows, WIDTH), BF16),
        pltpu.VMEM((TOKENS, SPAN * TOKENS), F32),
        pltpu.VMEM((16, 16, 384), BF16),
        pltpu.VMEM((12 * TOKENS, WIDTH), BF16),
        pltpu.VMEM((MINE, HEADS * VAL), BF16),
        pltpu.VMEM((2, 2, HALF, HEADS * VAL), BF16),
        pltpu.VMEM((rows, 128), F32),
        pltpu.VMEM((rows, 128), F32),
        pltpu.VMEM((rows, LAT), F32),
        pltpu.VMEM((2, 256, LAT), F32),
        pltpu.VMEM((2, 256, LAT), BF16),
        pltpu.VMEM((2, 256, LAT), BF16),
        pltpu.VMEM((2, 2, 4, 2, 16, 512), BF16),
        pltpu.VMEM((2, 2, 4, 2, 16, 384), BF16),
        pltpu.VMEM((2, 2, 2, 2, 16, 512), BF16),
        pltpu.VMEM((2, 2, 2, 2, 16, 384), BF16),
        pltpu.VMEM((2, 2, 2, 16, 512), BF16),
        pltpu.VMEM((2, 2, 2, 16, 384), BF16),
        pltpu.VMEM((4, 2, 16, 512), BF16),
        pltpu.VMEM((4, 2, 16, 384), BF16),
        pltpu.VMEM((2, 4, 16, 512), BF16),
        pltpu.VMEM((2, 4, 16, 384), BF16),
        dma((4,)),
        dma((16,)), dma((16,)),
        dma((2, 2)), dma((2, 2)),
        dma((3,)), dma((3,)),
        dma((2, 2)), dma((2, 2)),
        dma((2,)), dma((2,)),
        dma((3, 2)), dma((3, 2)),
        dma((4, 2)), dma((4, 2)),
        dma((8, 2)), dma((8, 2)),
        dma((2,)), dma((2,)),
        dma((2, 2, 2, 3)), dma((2, 2, 2, 3)),
        dma((2, 4)), dma((2, 4)),
        dma((2, 4)), dma((2, 4)),
    ]
    return pl.pallas_call(
        kernel,
        out_shape=jax.ShapeDtypeStruct((8, 2 * MINE), BF16),
        in_specs=[pl.BlockSpec(memory_space=pltpu.SMEM), vmem] + [anywhere] * 4,
        out_specs=vmem,
        scratch_shapes=scratch,
        compiler_params=pltpu.CompilerParams(
            collective_id=0, has_side_effects=True, vmem_limit_bytes=60 * 1024 * 1024
        ),
        cost_estimate=pl.CostEstimate(flops=3_500_000_000, bytes_accessed=3_000_000, transcendentals=1_048_576),
    )(block_order, latent, queries.transpose(1, 2, 0), key_up_weight, value_up_weight, w_o.T)


def solution(mesh):
    placed = (
        P("blk", "head", None),
        P(("blk", "head"), None),
        P("head", None, None),
        P("head", None, None),
        P("head", "blk"),
        P(),
    )
    return jax.shard_map(
        shards, mesh=mesh, in_specs=placed, out_specs=P(("blk", "head"), None), check_vma=False
    )
```

```python
import functools
import math

import jax
import jax.numpy as jnp
from jax import lax
from jax.experimental import pallas as pl
from jax.experimental.pallas import tpu as pltpu
from jax.sharding import PartitionSpec as P

NOPE = 128
ROT = 64
LAT = 512
WIDTH = LAT + ROT
VAL = 128
HEADS = 8
TOKENS = 128
HALF = 64
SPAN = 8
NBLK = 32
COLS = 112
MINE = 1792
WIDE = ((0, 512), (1024, 384))
GAIN = (NOPE + ROT) ** (-0.5) * math.log2(math.e)
HIDDEN = -1e30
F32 = jnp.float32
BF16 = jnp.bfloat16


def remote(src, dst, send, recv, device):
    return pltpu.make_async_remote_copy(
        src_ref=src, dst_ref=dst, send_sem=send, recv_sem=recv,
        device_id=device, device_id_type=pl.DeviceIdType.MESH,
    )


def kernel(
    order, latent, q_hbm, ku_hbm, vu_hbm, wo_hbm, out,
    q_raw, ku, vu, vu_t, q_t, bias, pack, keys, near_keys, keys_t, wt, vals,
    top, total, accum, score, prob, terms_a, terms_b, got_a, got_b, relay_a, relay_b, part_a, part_b, fin_a, fin_b,
    load_sem, ps, pr, lzs, lzr, lcs, lcr, lys, lyr, lds, ldr,
    wps, wpr, wms, wmr, wcs, wcr, vs, vr, xs, xr, yss, ysr, yos, yor,
):
    b = lax.axis_index("blk")
    h = lax.axis_index("head")
    z, c = b // 4, b % 4
    lo, core = c // 2, c % 2
    hi, x = h // 4, h % 4
    up = (b + 4) % NBLK
    down = (b + NBLK - 4) % NBLK
    mate = b + 1 - 2 * core
    side = b + 2 - 4 * lo
    c_mate = c + 1 - 2 * core
    c_side = c + 2 - 4 * lo
    c_diag = c_side + 1 - 2 * core

    loads = [
        pltpu.make_async_copy(src, dst, load_sem.at[i])
        for i, (src, dst) in enumerate(((q_hbm, q_raw), (ku_hbm, ku), (vu_hbm, vu)))
    ]
    mine = wt.at[pl.ds(pl.multiple_of((z * 2 + core) * COLS, 16), COLS)]
    loads.append(pltpu.make_async_copy(wo_hbm, mine, load_sem.at[3]))
    for load in loads[3:] + loads[:3]:
        load.start()

    rows = latent[...].astype(F32)
    second = jnp.concatenate([rows[:, 384:], jnp.zeros((8, 192), F32)], axis=1)
    pack[h] = jnp.concatenate([rows[:, :384], second], axis=0).astype(BF16)

    barrier = pltpu.get_barrier_semaphore()

    def greet(device):
        pl.semaphore_signal(barrier, inc=1, device_id=device, device_id_type=pl.DeviceIdType.MESH)

    @pl.loop(1, 16)
    def _(i):
        greet({"head": (h + i) % 16})

    @pl.loop(0, 4)
    def _(i):
        greet({"blk": side, "head": (hi + i) % 4 * 4 + x})

    greet({"blk": up})
    greet({"blk": down})
    greet({"blk": mate})
    pl.semaphore_wait(barrier, 22)

    def own_rows(i):
        return remote(pack.at[h], pack.at[h], ps.at[i], pr.at[i], {"head": (h + i) % 16})

    def shard(zz, cc, half):
        first = (zz * 2 + cc) * COLS + 64 * half
        return wt.at[pl.ds(pl.multiple_of(first, 16), (64, 48)[half])]

    def w_plus(k, half):
        ref = shard((z + 8 - k) % 8, core, half)
        return remote(ref, ref, wps.at[k, half], wpr.at[k, half], {"blk": up})

    def w_minus(k, half):
        ref = shard((z + k) % 8, core, half)
        return remote(ref, ref, wms.at[k, half], wmr.at[k, half], {"blk": down})

    def w_core(k, half):
        zz = (z + 8 - k) % 8 if k < 4 else (z + k - 3) % 8
        ref = shard(zz, core, half)
        return remote(ref, ref, wcs.at[k, half], wcr.at[k, half], {"blk": mate})

    def w_core_in(k, half):
        zz = (z + 8 - k) % 8 if k < 4 else (z + k - 3) % 8
        ref = shard(zz, 1 - core, half)
        return remote(ref, ref, wcs.at[k, half], wcr.at[k, half], {"blk": mate})

    def w_plus_in(k, half):
        ref = shard((z + 7 - k) % 8, core, half)
        return remote(ref, ref, wps.at[k, half], wpr.at[k, half], {"blk": up})

    def w_minus_in(k, half):
        ref = shard((z + 1 + k) % 8, core, half)
        return remote(ref, ref, wms.at[k, half], wmr.at[k, half], {"blk": down})

    def w_step_plus(k, half):
        w_plus_in(k - 1, half).wait_recv()
        if k < 3:
            w_plus(k, half).start()
        w_core(k, half).start()

    def w_step_minus(k, half):
        w_minus_in(k - 1, half).wait_recv()
        if k < 4:
            w_minus(k, half).start()
        w_core(3 + k, half).start()

    loads[3].wait()
    for half in range(2):
        w_plus(0, half).start()
        w_minus(0, half).start()

    @pl.loop(1, 16)
    def _(i):
        own_rows(i).start()

    for half in range(2):
        w_core(0, half).start()

    loads[0].wait()
    loads[1].wait()
    for n in range(HEADS):
        at = slice(n % 2 * TOKENS, (n % 2 + 1) * TOKENS)
        q_t[n // 2, :LAT, at] = lax.dot_general(
            ku[n], q_raw[n, :NOPE, :], (((0,), (0,)), ((), ())), preferred_element_type=F32
        ).astype(BF16)
        q_t[n // 2, LAT:, at] = q_raw[n, NOPE:, :]

    blocks = (
        (0, c), (1, c), (1, c_mate),
        (1 - lo, c_side), (1 - lo, c_diag), (2 - 2 * core, c_mate),
        (2 - lo, c_side), (2 - lo, c_diag),
    )
    row = lax.broadcasted_iota(jnp.int32, (TOKENS, TOKENS), 0)
    col = lax.broadcasted_iota(jnp.int32, (TOKENS, TOKENS), 1)
    q_pos = jnp.where(col < HALF, order[2 * b], order[2 * b + 1]) * HALF + col % HALF
    for j, (plane, cc) in enumerate(blocks):
        src = (z + 8 - plane) % 8 * 4 + cc
        k_pos = jnp.where(row < HALF, order[2 * src], order[2 * src + 1]) * HALF + row % HALF
        bias[j * TOKENS:(j + 1) * TOKENS, :] = jnp.where(k_pos <= q_pos, 0.0, HIDDEN)

    loads[2].wait()
    for n in range(HEADS):
        vu_t[n] = vu[n].astype(F32).T.astype(BF16)

    @pl.loop(1, 16)
    def _(i):
        ref = pack.at[(h + 16 - i) % 16]
        remote(ref, ref, ps.at[i], pr.at[i], {"head": (h + i) % 16}).wait_recv()

    def part_slot(plane, cc, half):
        first = (8 - 4 * plane + cc) * TOKENS + half * HALF
        return keys.at[pl.ds(pl.multiple_of(first, HALF), HALF)]

    def slot(plane, cc):
        return keys.at[pl.ds(pl.multiple_of((8 - 4 * plane + cc) * TOKENS, TOKENS), TOKENS)]

    gathered = pack[...].astype(F32)
    base = pl.multiple_of((8 + c) * TOKENS, TOKENS)
    keys[pl.ds(base, TOKENS), :384] = gathered[:, :8, :].reshape(TOKENS, 384).astype(BF16)
    keys[pl.ds(base, TOKENS), 384:] = gathered[:, 8:, :192].reshape(TOKENS, 192).astype(BF16)

    def l_up(k, half):
        src, dst = part_slot(k, c, half), part_slot(k + 1, c, half)
        return remote(src, dst, lzs.at[k, half], lzr.at[k, half], {"blk": up})

    def l_up_in(k, half):
        ref = part_slot(k + 1, c, half)
        return remote(ref, ref, lzs.at[k, half], lzr.at[k, half], {"blk": up})

    def l_core(p):
        return remote(slot(p, c), slot(p, c), lcs.at[p], lcr.at[p], {"blk": mate})

    def l_core_in(p):
        return remote(slot(p, c_mate), slot(p, c_mate), lcs.at[p], lcr.at[p], {"blk": mate})

    def l_side(j, half):
        ref = part_slot(j + lo, c, half)
        return remote(ref, ref, lys.at[j, half], lyr.at[j, half], {"blk": side})

    def l_side_in(j, half):
        ref = part_slot(j + 1 - lo, c_side, half)
        return remote(ref, ref, lys.at[j, half], lyr.at[j, half], {"blk": side})

    def l_diag(j):
        ref = slot(j + 1 - lo, c_side)
        return remote(ref, ref, lds.at[j], ldr.at[j], {"blk": mate})

    def l_diag_in(j):
        ref = slot(j + 1 - lo, c_diag)
        return remote(ref, ref, lds.at[j], ldr.at[j], {"blk": mate})

    l_up(0, 0).start()
    l_up(0, 1).start()

    @pl.when(lo == 0)
    def _():
        l_side(0, 0).start()
        l_side(0, 1).start()

    l_core(0).start()
    for half in range(2):
        w_step_minus(1, half)
        w_step_plus(1, half)

    def take(j):
        rows = slot(*blocks[j])[...]
        near_keys[j * TOKENS:(j + 1) * TOKENS, :] = rows
        keys_t[:, j * TOKENS:(j + 1) * TOKENS] = rows[:, :LAT].astype(F32).T.astype(BF16)

    take(0)
    for half in range(2):
        l_up_in(0, half).wait_recv()
        l_up(1, half).start()
        l_side(1 - lo, half).start()

    l_core(1).start()
    take(1)
    for half in range(2):
        w_step_minus(2, half)
        w_step_plus(2, half)
    l_core_in(1).wait_recv()
    take(2)

    def v_out(i):
        ref = vals.at[lo, pl.ds(pl.multiple_of(i * 256, 256), 256)]
        return remote(ref, ref, vs.at[i], vr.at[i], {"blk": side})

    def v_in(i):
        ref = vals.at[1 - lo, pl.ds(pl.multiple_of(i * 256, 256), 256)]
        return remote(ref, ref, vs.at[i], vr.at[i], {"blk": side})

    def attend(j, first, count, begins, ends):
        k = near_keys[first:first + count, :]
        k_t = keys_t[:, first:first + count]
        for g in range(2):
            score[g, :count] = jnp.dot(k, q_t[2 * j + g], preferred_element_type=F32)
        for g in range(2):
            i = 2 * j + g
            high = None
            for r in range(0, count, 64):
                mask = bias[first + r:first + r + 64, :]
                sc = score[g, r:r + 64] + jnp.concatenate([mask, mask], axis=1)
                score[g, r:r + 64] = sc
                part = jnp.max(sc.reshape(8, 8, 256), axis=0)
                high = part if high is None else jnp.maximum(high, part)
            m = jnp.max(high, axis=0, keepdims=True)
            if not begins:
                old = top[i, :1]
                m = jnp.maximum(m, old)
                shrink = jnp.exp2((old - m) * GAIN)
            add = None
            for r in range(0, count, 64):
                e = jnp.exp2((score[g, r:r + 64] - m) * GAIN)
                prob[g, r:r + 64] = e.astype(BF16)
                part = jnp.sum(e.reshape(8, 8, 256), axis=0)
                add = part if add is None else add + part
            tot = jnp.sum(add, axis=0, keepdims=True)
            if not begins:
                tot = tot + total[i, :1] * shrink
            if not ends:
                top[i] = jnp.broadcast_to(m, (8, 256))
                total[i] = jnp.broadcast_to(tot, (8, 256))
            got = jnp.dot(k_t, prob[g, :count], preferred_element_type=F32)
            if begins:
                accum[i] = got
            elif not ends:
                accum[i] = accum[i] * shrink + got
            else:
                inverse = 1.0 / tot
                ctx = (accum[i] * (shrink * inverse) + got * inverse).astype(BF16)
                for n in range(2):
                    v = jnp.dot(vu_t[2 * i + n], ctx[:, n * TOKENS:(n + 1) * TOKENS], preferred_element_type=F32)
                    vals[lo, pl.ds(pl.multiple_of(i * 256 + n * VAL, VAL), VAL), :] = v.astype(BF16)
                v_out(i).start()

    @pl.loop(0, 2)
    def _(j):
        attend(j, 0, 384, True, False)

        @pl.when(j == 0)
        def _():
            l_side_in(0, 0).wait_recv()
            l_side_in(0, 1).wait_recv()
            l_diag(0).start()
            for half in range(2):
                l_up_in(1, half).wait_recv()

                @pl.when(lo == 1)
                def _():
                    l_side(1, half).start()

            l_core(2).start()

    for half in range(2):
        w_step_minus(3, half)
    take(3)
    l_diag_in(0).wait_recv()
    take(4)
    l_core_in(0).wait_recv()
    l_core_in(2).wait_recv()
    take(5)

    @pl.loop(0, 2)
    def _(j):
        attend(j, 384, 384, False, False)

        @pl.when(j == 0)
        def _():
            l_side_in(1, 0).wait_recv()
            l_side_in(1, 1).wait_recv()
            l_diag(1).start()
            for half in range(2):
                w_step_plus(3, half)

    take(6)
    for half in range(2):
        w_step_minus(4, half)
    l_diag_in(1).wait_recv()
    take(7)

    @pl.loop(0, 2)
    def _(j):
        attend(j, 768, 256, False, True)

    for k in range(8):
        for half in range(2):
            w_core_in(k, half).wait_recv()

    def x_out(y, n, step, way, kind):
        terms, got, relay = ((terms_a, got_a, relay_a), (terms_b, got_b, relay_b))[n]
        xd = (x + 1 + 2 * way) % 4
        if kind == 0:
            src, dst = terms.at[y, way, :, (x + 2) % 4], relay.at[y, way]
        else:
            half = 1 - way if kind == 1 else way
            src, dst = terms.at[y, half, :, xd], got.at[y, way, half]
        sem = (n, step, way, kind)
        return remote(src, dst, xs.at[sem], xr.at[sem], {"head": hi * 4 + xd})

    def project(y, n, step):
        first, width = WIDE[n]
        terms = (terms_a, terms_b)[n]
        t = jnp.dot(wt[first:first + 2 * width, :], vals[y], preferred_element_type=F32).T
        left = t[:, :width].reshape(16, 8, width)
        right = t[:, width:].reshape(16, 8, width)
        both = jnp.concatenate([left, right], axis=1).astype(BF16)
        terms[y] = both.reshape(2, 2, 4, 16, width)
        for kind in range(2):
            for way in range(2):
                x_out(y, n, step, way, kind).start()

    def pass_on(y, n, step):
        terms, relay = ((terms_a, relay_a), (terms_b, relay_b))[n]
        for way in range(2):
            x_out(y, n, step, way, 0).wait_recv()
            xd = (x + 1 + 2 * way) % 4
            t = terms[y, way, :, xd].astype(F32) + relay[y, way].astype(F32)
            terms[y, way, :, xd] = t.astype(BF16)
            x_out(y, n, step, way, 2).start()

    def y_same(n, e):
        part, fin = ((part_a, fin_a), (part_b, fin_b))[n]
        yd = (hi + e) % 4
        return remote(
            part.at[lo, yd], fin.at[0, e], yss.at[n, e], ysr.at[n, e], {"head": yd * 4 + x}
        )

    def y_other(n, e):
        part, fin = ((part_a, fin_a), (part_b, fin_b))[n]
        yd = (hi + e) % 4
        return remote(
            part.at[1 - lo, yd], fin.at[1, e], yos.at[n, e], yor.at[n, e],
            {"blk": side, "head": yd * 4 + x},
        )

    def combine(y, n, step):
        terms, got, part = ((terms_a, got_a, part_a), (terms_b, got_b, part_b))[n]
        width = WIDE[n][1]
        for way in range(2):
            x_out(y, n, step, way, 1).wait_recv()
            x_out(y, n, step, way, 2).wait_recv()
        t = terms[y, :, :, x].astype(F32) + got[y, 0].astype(F32) + got[y, 1].astype(F32)
        part[y] = t.reshape(4, 16, width).astype(BF16)

    project(lo, 0, 0)
    project(lo, 1, 0)
    pass_on(lo, 0, 0)
    for i in range(4):
        v_in(i).wait_recv()
    project(1 - lo, 0, 1)
    pass_on(lo, 1, 0)
    project(1 - lo, 1, 1)
    pass_on(1 - lo, 0, 1)
    pass_on(1 - lo, 1, 1)
    for n in range(2):
        combine(lo, n, 0)
        for e in (2, 1, 3):
            y_same(n, e).start()
    for n in range(2):
        combine(1 - lo, n, 1)
        for e in (2, 1, 3, 0):
            y_other(n, e).start()
    same_cols, other_cols = [], []
    for n in range(2):
        part, fin = ((part_a, fin_a), (part_b, fin_b))[n]
        same = part[lo, hi].astype(F32)
        for e in (1, 2, 3):
            y_same(n, e).wait_recv()
            same = same + fin[0, e].astype(F32)
        y_other(n, 0).wait_recv()
        other = fin[1, 0].astype(F32)
        for e in (1, 2, 3):
            y_other(n, e).wait_recv()
            other = other + fin[1, e].astype(F32)
        same_cols += [same[:8], same[8:]]
        other_cols += [other[:8], other[8:]]
    same = jnp.concatenate(same_cols, axis=1)
    other = jnp.concatenate(other_cols, axis=1)
    by_y = (jnp.where(lo == 0, same, other), jnp.where(lo == 0, other, same))
    pair = 2 * COLS
    out[...] = jnp.concatenate(
        [by_y[i % 2][:, i // 2 * pair:(i // 2 + 1) * pair] for i in range(16)], axis=1
    ).astype(BF16)

    @pl.loop(1, 16)
    def _(i):
        own_rows(i).wait_send()

    for k in range(2):
        for half in range(2):
            l_up(k, half).wait_send()
            l_side(k, half).wait_send()
        l_diag(k).wait_send()
    for k in range(3):
        l_core(k).wait_send()
    for half in range(2):
        for k in range(3):
            w_plus(k, half).wait_send()
        for k in range(4):
            w_minus(k, half).wait_send()
        for k in range(8):
            w_core(k, half).wait_send()
    for i in range(4):
        v_out(i).wait_send()
    for n in range(2):
        for way in range(2):
            for kind in range(3):
                x_out(lo, n, 0, way, kind).wait_send()
                x_out(1 - lo, n, 1, way, kind).wait_send()
        for e in (1, 2, 3):
            y_same(n, e).wait_send()
        for e in range(4):
            y_other(n, e).wait_send()


def shards(queries, latent, key_up_weight, value_up_weight, w_o, block_order):
    vmem = pl.BlockSpec(memory_space=pltpu.VMEM)
    anywhere = pl.BlockSpec(memory_space=pl.ANY)
    dma = pltpu.SemaphoreType.DMA
    scratch = [
        pltpu.VMEM((HEADS, NOPE + ROT, TOKENS), BF16),
        pltpu.VMEM((HEADS, NOPE, LAT), BF16),
        pltpu.VMEM((HEADS, LAT, VAL), BF16),
        pltpu.VMEM((HEADS, VAL, LAT), BF16),
        pltpu.VMEM((4, WIDTH, 256), BF16),
        pltpu.VMEM((SPAN * TOKENS, TOKENS), F32),
        pltpu.VMEM((16, 16, 384), BF16),
        pltpu.VMEM((12 * TOKENS, WIDTH), BF16),
        pltpu.VMEM((SPAN * TOKENS, WIDTH), BF16),
        pltpu.VMEM((LAT, SPAN * TOKENS), BF16),
        pltpu.VMEM((MINE, HEADS * VAL), BF16),
        pltpu.VMEM((2, HEADS * VAL, TOKENS), BF16),
        pltpu.VMEM((4, 8, 256), F32),
        pltpu.VMEM((4, 8, 256), F32),
        pltpu.VMEM((4, LAT, 256), F32),
        pltpu.VMEM((2, 384, 256), F32),
        pltpu.VMEM((2, 384, 256), BF16),
        pltpu.VMEM((2, 2, 2, 4, 16, 512), BF16),
        pltpu.VMEM((2, 2, 2, 4, 16, 384), BF16),
        pltpu.VMEM((2, 2, 2, 2, 16, 512), BF16),
        pltpu.VMEM((2, 2, 2, 2, 16, 384), BF16),
        pltpu.VMEM((2, 2, 2, 16, 512), BF16),
        pltpu.VMEM((2, 2, 2, 16, 384), BF16),
        pltpu.VMEM((2, 4, 16, 512), BF16),
        pltpu.VMEM((2, 4, 16, 384), BF16),
        pltpu.VMEM((2, 4, 16, 512), BF16),
        pltpu.VMEM((2, 4, 16, 384), BF16),
        dma((4,)),
        dma((16,)), dma((16,)),
        dma((2, 2)), dma((2, 2)),
        dma((3,)), dma((3,)),
        dma((2, 2)), dma((2, 2)),
        dma((2,)), dma((2,)),
        dma((3, 2)), dma((3, 2)),
        dma((4, 2)), dma((4, 2)),
        dma((8, 2)), dma((8, 2)),
        dma((4,)), dma((4,)),
        dma((2, 2, 2, 3)), dma((2, 2, 2, 3)),
        dma((2, 4)), dma((2, 4)),
        dma((2, 4)), dma((2, 4)),
    ]
    return pl.pallas_call(
        kernel,
        out_shape=jax.ShapeDtypeStruct((8, 2 * MINE), BF16),
        in_specs=[pl.BlockSpec(memory_space=pltpu.SMEM), vmem] + [anywhere] * 4,
        out_specs=vmem,
        scratch_shapes=scratch,
        compiler_params=pltpu.CompilerParams(
            collective_id=0, has_side_effects=True, vmem_limit_bytes=60 * 1024 * 1024
        ),
        cost_estimate=pl.CostEstimate(flops=3_500_000_000, bytes_accessed=3_000_000, transcendentals=1_048_576),
    )(block_order, latent, queries.transpose(1, 2, 0), key_up_weight, value_up_weight, w_o.T)


def solution(mesh):
    placed = (
        P("blk", "head", None),
        P(("blk", "head"), None),
        P("head", None, None),
        P("head", None, None),
        P("head", "blk"),
        P(),
    )
    return jax.shard_map(
        shards, mesh=mesh, in_specs=placed, out_specs=P(("blk", "head"), None), check_vma=False
    )
```

```python
import functools
import math

import jax
import jax.numpy as jnp
from jax import lax
from jax.experimental import pallas as pl
from jax.experimental.pallas import tpu as pltpu
from jax.sharding import PartitionSpec as P

NOPE = 128
ROT = 64
LAT = 512
WIDTH = LAT + ROT
VAL = 128
HEADS = 8
TOKENS = 128
HALF = 64
SPAN = 8
NBLK = 32
COLS = 112
MINE = 896
GAIN = (NOPE + ROT) ** (-0.5) * math.log2(math.e)
HIDDEN = -1e30
F32 = jnp.float32
BF16 = jnp.bfloat16


def remote(src, dst, send, recv, device):
    return pltpu.make_async_remote_copy(
        src_ref=src, dst_ref=dst, send_sem=send, recv_sem=recv,
        device_id=device, device_id_type=pl.DeviceIdType.MESH,
    )


def kernel(
    order, latent, q_hbm, ku_hbm, vu_hbm, wo_hbm, out,
    q_raw, ku, vu, vu_t, q_t, bias, pack, keys, near_keys, keys_t, wt, vals,
    top, total, accum, score, prob, terms, got, relay, part, fin,
    load_sem, ps, pr, lzs, lzr, lcs, lcr, lys, lyr, lds, ldr,
    wps, wpr, wms, wmr, vs, vr, xs, xr, ys, yr,
):
    b = lax.axis_index("blk")
    h = lax.axis_index("head")
    z, c = b // 4, b % 4
    lo, core = c // 2, c % 2
    hi, x = h // 4, h % 4
    up = (b + 4) % NBLK
    down = (b + NBLK - 4) % NBLK
    mate = b + 1 - 2 * core
    side = b + 2 - 4 * lo
    diag = side + 1 - 2 * core
    c_mate = c + 1 - 2 * core
    c_side = c + 2 - 4 * lo
    c_diag = c_side + 1 - 2 * core

    loads = [
        pltpu.make_async_copy(src, dst, load_sem.at[i])
        for i, (src, dst) in enumerate(((q_hbm, q_raw), (ku_hbm, ku), (vu_hbm, vu)))
    ]
    mine = wt.at[pl.ds(pl.multiple_of(z * COLS, 16), COLS)]
    loads.append(pltpu.make_async_copy(wo_hbm, mine, load_sem.at[3]))
    for load in loads[3:] + loads[:3]:
        load.start()

    rows = latent[...].astype(F32)
    second = jnp.concatenate([rows[:, 384:], jnp.zeros((8, 192), F32)], axis=1)
    pack[h] = jnp.concatenate([rows[:, :384], second], axis=0).astype(BF16)

    barrier = pltpu.get_barrier_semaphore()

    def greet(device):
        pl.semaphore_signal(barrier, inc=1, device_id=device, device_id_type=pl.DeviceIdType.MESH)

    @pl.loop(1, 16)
    def _(i):
        greet({"head": (h + i) % 16})

    for other in (side, diag):
        @pl.loop(0, 4)
        def _(i):
            greet({"blk": other, "head": i * 4 + x})

    @pl.loop(0, 4)
    def _(i):
        greet({"blk": mate, "head": i * 4 + x})

    greet({"blk": up})
    greet({"blk": down})
    pl.semaphore_wait(barrier, 29)

    def own_rows(i):
        return remote(pack.at[h], pack.at[h], ps.at[i], pr.at[i], {"head": (h + i) % 16})

    def shard(zz):
        return wt.at[pl.ds(pl.multiple_of(zz * COLS, 16), COLS)]

    def w_plus(k):
        ref = shard((z + 8 - k) % 8)
        return remote(ref, ref, wps.at[k], wpr.at[k], {"blk": up})

    def w_minus(k):
        ref = shard((z + k) % 8)
        return remote(ref, ref, wms.at[k], wmr.at[k], {"blk": down})

    def w_plus_in(k):
        ref = shard((z + 7 - k) % 8)
        return remote(ref, ref, wps.at[k], wpr.at[k], {"blk": up})

    def w_minus_in(k):
        ref = shard((z + 1 + k) % 8)
        return remote(ref, ref, wms.at[k], wmr.at[k], {"blk": down})

    def w_step_plus(k):
        w_plus_in(k - 1).wait_recv()
        if k < 3:
            w_plus(k).start()

    def w_step_minus(k):
        w_minus_in(k - 1).wait_recv()
        if k < 4:
            w_minus(k).start()

    loads[3].wait()
    w_plus(0).start()
    w_minus(0).start()

    @pl.loop(1, 16)
    def _(i):
        own_rows(i).start()


    loads[0].wait()
    loads[1].wait()
    for n in range(HEADS):
        at = slice(n % 2 * TOKENS, (n % 2 + 1) * TOKENS)
        q_t[n // 2, :LAT, at] = lax.dot_general(
            ku[n], q_raw[n, :NOPE, :], (((0,), (0,)), ((), ())), preferred_element_type=F32
        ).astype(BF16)
        q_t[n // 2, LAT:, at] = q_raw[n, NOPE:, :]

    blocks = (
        (0, c), (1, c), (1, c_mate),
        (1 - lo, c_side), (1 - lo, c_diag), (2 - 2 * core, c_mate),
        (2 - lo, c_side), (2 - lo, c_diag),
    )
    row = lax.broadcasted_iota(jnp.int32, (TOKENS, TOKENS), 0)
    col = lax.broadcasted_iota(jnp.int32, (TOKENS, TOKENS), 1)
    q_pos = jnp.where(col < HALF, order[2 * b], order[2 * b + 1]) * HALF + col % HALF
    for j, (plane, cc) in enumerate(blocks):
        src = (z + 8 - plane) % 8 * 4 + cc
        k_pos = jnp.where(row < HALF, order[2 * src], order[2 * src + 1]) * HALF + row % HALF
        bias[j * TOKENS:(j + 1) * TOKENS, :] = jnp.where(k_pos <= q_pos, 0.0, HIDDEN)

    loads[2].wait()
    for n in range(HEADS):
        vu_t[n] = vu[n].astype(F32).T.astype(BF16)

    @pl.loop(1, 16)
    def _(i):
        ref = pack.at[(h + 16 - i) % 16]
        remote(ref, ref, ps.at[i], pr.at[i], {"head": (h + i) % 16}).wait_recv()

    def part_slot(plane, cc, half):
        first = (8 - 4 * plane + cc) * TOKENS + half * HALF
        return keys.at[pl.ds(pl.multiple_of(first, HALF), HALF)]

    def slot(plane, cc):
        return keys.at[pl.ds(pl.multiple_of((8 - 4 * plane + cc) * TOKENS, TOKENS), TOKENS)]

    gathered = pack[...].astype(F32)
    base = pl.multiple_of((8 + c) * TOKENS, TOKENS)
    keys[pl.ds(base, TOKENS), :384] = gathered[:, :8, :].reshape(TOKENS, 384).astype(BF16)
    keys[pl.ds(base, TOKENS), 384:] = gathered[:, 8:, :192].reshape(TOKENS, 192).astype(BF16)

    def l_up(k, half):
        src, dst = part_slot(k, c, half), part_slot(k + 1, c, half)
        return remote(src, dst, lzs.at[k, half], lzr.at[k, half], {"blk": up})

    def l_up_in(k, half):
        ref = part_slot(k + 1, c, half)
        return remote(ref, ref, lzs.at[k, half], lzr.at[k, half], {"blk": up})

    def l_core(p):
        return remote(slot(p, c), slot(p, c), lcs.at[p], lcr.at[p], {"blk": mate})

    def l_core_in(p):
        return remote(slot(p, c_mate), slot(p, c_mate), lcs.at[p], lcr.at[p], {"blk": mate})

    def l_side(j, half):
        ref = part_slot(j + lo, c, half)
        return remote(ref, ref, lys.at[j, half], lyr.at[j, half], {"blk": side})

    def l_side_in(j, half):
        ref = part_slot(j + 1 - lo, c_side, half)
        return remote(ref, ref, lys.at[j, half], lyr.at[j, half], {"blk": side})

    def l_diag(j):
        ref = slot(j + 1 - lo, c_side)
        return remote(ref, ref, lds.at[j], ldr.at[j], {"blk": mate})

    def l_diag_in(j):
        ref = slot(j + 1 - lo, c_diag)
        return remote(ref, ref, lds.at[j], ldr.at[j], {"blk": mate})

    l_up(0, 0).start()
    l_up(0, 1).start()

    @pl.when(lo == 0)
    def _():
        l_side(0, 0).start()
        l_side(0, 1).start()

    l_core(0).start()
    def take(j):
        rows = slot(*blocks[j])[...]
        near_keys[j * TOKENS:(j + 1) * TOKENS, :] = rows
        keys_t[:, j * TOKENS:(j + 1) * TOKENS] = rows[:, :LAT].astype(F32).T.astype(BF16)

    take(0)
    w_step_minus(1)
    for half in range(2):
        l_up_in(0, half).wait_recv()
        l_up(1, half).start()
        l_side(1 - lo, half).start()

    l_core(1).start()
    take(1)
    w_step_plus(1)
    l_core_in(1).wait_recv()
    take(2)

    def v_part(y, i, cc):
        rows = pl.ds(pl.multiple_of(i * 256, 256), 256)
        return vals.at[y, rows, pl.ds(pl.multiple_of(cc * TOKENS, TOKENS), TOKENS)]

    def v_mate(i):
        ref = v_part(lo, i, core)
        return remote(ref, ref, vs.at[0, i], vr.at[0, i], {"blk": mate})

    def v_mate_in(i):
        ref = v_part(lo, i, 1 - core)
        return remote(ref, ref, vs.at[0, i], vr.at[0, i], {"blk": mate})

    def v_side(i):
        ref = v_part(lo, i, core)
        return remote(ref, ref, vs.at[1, i], vr.at[1, i], {"blk": side})

    def v_side_in(i):
        ref = v_part(1 - lo, i, core)
        return remote(ref, ref, vs.at[1, i], vr.at[1, i], {"blk": side})

    def v_diag(i):
        ref = v_part(1 - lo, i, core)
        return remote(ref, ref, vs.at[2, i], vr.at[2, i], {"blk": mate})

    def v_diag_in(i):
        ref = v_part(1 - lo, i, 1 - core)
        return remote(ref, ref, vs.at[2, i], vr.at[2, i], {"blk": mate})

    def attend(j, first, count, begins, ends):
        k = near_keys[first:first + count, :]
        k_t = keys_t[:, first:first + count]
        for g in range(2):
            score[g, :count] = jnp.dot(k, q_t[2 * j + g], preferred_element_type=F32)
        for g in range(2):
            i = 2 * j + g
            high = None
            for r in range(0, count, 64):
                mask = bias[first + r:first + r + 64, :]
                sc = score[g, r:r + 64] + jnp.concatenate([mask, mask], axis=1)
                score[g, r:r + 64] = sc
                part = jnp.max(sc.reshape(8, 8, 256), axis=0)
                high = part if high is None else jnp.maximum(high, part)
            m = jnp.max(high, axis=0, keepdims=True)
            if not begins:
                old = top[i, :1]
                m = jnp.maximum(m, old)
                shrink = jnp.exp2((old - m) * GAIN)
            add = None
            for r in range(0, count, 64):
                e = jnp.exp2((score[g, r:r + 64] - m) * GAIN)
                prob[g, r:r + 64] = e.astype(BF16)
                part = jnp.sum(e.reshape(8, 8, 256), axis=0)
                add = part if add is None else add + part
            tot = jnp.sum(add, axis=0, keepdims=True)
            if not begins:
                tot = tot + total[i, :1] * shrink
            if not ends:
                top[i] = jnp.broadcast_to(m, (8, 256))
                total[i] = jnp.broadcast_to(tot, (8, 256))
            got = jnp.dot(k_t, prob[g, :count], preferred_element_type=F32)
            if begins:
                accum[i] = got
            elif not ends:
                accum[i] = accum[i] * shrink + got
            else:
                inverse = 1.0 / tot
                ctx = (accum[i] * (shrink * inverse) + got * inverse).astype(BF16)
                for n in range(2):
                    v = jnp.dot(vu_t[2 * i + n], ctx[:, n * TOKENS:(n + 1) * TOKENS], preferred_element_type=F32)
                    rows = pl.ds(pl.multiple_of(i * 256 + n * VAL, VAL), VAL)
                    vals[lo, rows, pl.ds(pl.multiple_of(core * TOKENS, TOKENS), TOKENS)] = v.astype(BF16)
                v_side(i).start()
                v_mate(i).start()

    @pl.loop(0, 2)
    def _(j):
        attend(j, 0, 384, True, False)

        @pl.when(j == 0)
        def _():
            l_side_in(0, 0).wait_recv()
            l_side_in(0, 1).wait_recv()
            l_diag(0).start()
            for half in range(2):
                l_up_in(1, half).wait_recv()

                @pl.when(lo == 1)
                def _():
                    l_side(1, half).start()

            l_core(2).start()
            w_step_minus(2)

    take(3)
    l_diag_in(0).wait_recv()
    take(4)
    l_core_in(0).wait_recv()
    l_core_in(2).wait_recv()
    take(5)
    w_step_plus(2)

    @pl.loop(0, 2)
    def _(j):
        attend(j, 384, 384, False, False)

        @pl.when(j == 0)
        def _():
            l_side_in(1, 0).wait_recv()
            l_side_in(1, 1).wait_recv()
            l_diag(1).start()
            w_step_minus(3)

    take(6)
    l_diag_in(1).wait_recv()
    take(7)

    @pl.loop(0, 2)
    def _(j):
        attend(j, 768, 256, False, True)

    w_step_plus(3)
    w_step_minus(4)

    def x_out(y, n, step, way, kind):
        xd = (x + 1 + 2 * way) % 4
        if kind == 0:
            src, dst = terms.at[n, y, way, :, (x + 2) % 4], relay.at[n, y, way]
        else:
            half = 1 - way if kind == 1 else way
            src, dst = terms.at[n, y, half, :, xd], got.at[n, y, way, half]
        sem = (n, step, way, kind)
        return remote(src, dst, xs.at[sem], xr.at[sem], {"head": hi * 4 + xd})

    def project(y, n, step):
        last = min(MINE, 512 * n + 512)
        t = jnp.dot(wt[512 * n:last, :], vals[y], preferred_element_type=F32).T
        if n == 1:
            t = jnp.concatenate([t, jnp.zeros((256, 128), F32)], axis=1)
        for cc in range(2):
            rows = t[cc * TOKENS:(cc + 1) * TOKENS]
            left = rows[:, :256].reshape(16, 8, 256)
            right = rows[:, 256:].reshape(16, 8, 256)
            both = jnp.concatenate([left, right], axis=1).astype(BF16)
            terms[n, y, :, :, :, cc] = both.reshape(2, 2, 4, 16, 256)
        for kind in range(2):
            for way in range(2):
                x_out(y, n, step, way, kind).start()

    def pass_on(y, n, step):
        for way in range(2):
            x_out(y, n, step, way, 0).wait_recv()
            xd = (x + 1 + 2 * way) % 4
            t = terms[n, y, way, :, xd].astype(F32) + relay[n, y, way].astype(F32)
            terms[n, y, way, :, xd] = t.astype(BF16)
            x_out(y, n, step, way, 2).start()

    def combine(y, n, step):
        for way in range(2):
            x_out(y, n, step, way, 1).wait_recv()
            x_out(y, n, step, way, 2).wait_recv()
        t = terms[n, y, :, :, x].astype(F32) + got[n, y, 0].astype(F32) + got[n, y, 1].astype(F32)
        part[y, :, :, n] = t.reshape(4, 2, 16, 256).astype(BF16)

    groups = ((b, lo, core), (mate, lo, 1 - core), (side, 1 - lo, core), (diag, 1 - lo, 1 - core))

    def y_out(g, e):
        blk, y, cc = groups[g]
        yd = (hi + e) % 4
        return remote(
            part.at[y, yd, cc], fin.at[g, e], ys.at[g, e], yr.at[g, e], {"blk": blk, "head": yd * 4 + x}
        )

    pairs = [(0, e) for e in (2, 1, 3)] + [(g, e) for g in (1, 2, 3) for e in (2, 1, 3, 0)]

    for i in range(4):
        v_mate_in(i).wait_recv()
    project(lo, 0, 0)
    for i in range(4):
        v_side_in(i).wait_recv()
        v_diag(i).start()
    project(lo, 1, 0)
    pass_on(lo, 0, 0)
    for i in range(4):
        v_diag_in(i).wait_recv()
    project(1 - lo, 0, 1)
    pass_on(lo, 1, 0)
    project(1 - lo, 1, 1)
    pass_on(1 - lo, 0, 1)
    combine(lo, 0, 0)
    combine(lo, 1, 0)
    for g, e in pairs[:7]:
        y_out(g, e).start()
    pass_on(1 - lo, 1, 1)
    combine(1 - lo, 0, 1)
    combine(1 - lo, 1, 1)
    for g, e in pairs[7:]:
        y_out(g, e).start()
    sums = [part[lo, hi, core].astype(F32), None, None, None]
    for g, e in pairs:
        y_out(g, e).wait_recv()
        v = fin[g, e].astype(F32)
        sums[g] = v if sums[g] is None else sums[g] + v
    flat = [
        jnp.concatenate([v[0, :8], v[0, 8:], v[1, :8], v[1, 8:, :128]], axis=1) for v in sums
    ]
    by_c = [
        jnp.where(c == a, flat[0], jnp.where(c_mate == a, flat[1], jnp.where(c_side == a, flat[2], flat[3])))
        for a in range(4)
    ]
    out[...] = jnp.concatenate(
        [by_c[i % 4][:, i // 4 * COLS:(i // 4 + 1) * COLS] for i in range(NBLK)], axis=1
    ).astype(BF16)

    @pl.loop(1, 16)
    def _(i):
        own_rows(i).wait_send()

    for k in range(2):
        for half in range(2):
            l_up(k, half).wait_send()
            l_side(k, half).wait_send()
        l_diag(k).wait_send()
    for k in range(3):
        l_core(k).wait_send()
    for k in range(3):
        w_plus(k).wait_send()
    for k in range(4):
        w_minus(k).wait_send()
    for i in range(4):
        v_side(i).wait_send()
        v_mate(i).wait_send()
        v_diag(i).wait_send()
    for n in range(2):
        for way in range(2):
            for kind in range(3):
                x_out(lo, n, 0, way, kind).wait_send()
                x_out(1 - lo, n, 1, way, kind).wait_send()
    for g, e in pairs:
        y_out(g, e).wait_send()


def shards(queries, latent, key_up_weight, value_up_weight, w_o, block_order):
    vmem = pl.BlockSpec(memory_space=pltpu.VMEM)
    anywhere = pl.BlockSpec(memory_space=pl.ANY)
    dma = pltpu.SemaphoreType.DMA
    scratch = [
        pltpu.VMEM((HEADS, NOPE + ROT, TOKENS), BF16),
        pltpu.VMEM((HEADS, NOPE, LAT), BF16),
        pltpu.VMEM((HEADS, LAT, VAL), BF16),
        pltpu.VMEM((HEADS, VAL, LAT), BF16),
        pltpu.VMEM((4, WIDTH, 256), BF16),
        pltpu.VMEM((SPAN * TOKENS, TOKENS), F32),
        pltpu.VMEM((16, 16, 384), BF16),
        pltpu.VMEM((12 * TOKENS, WIDTH), BF16),
        pltpu.VMEM((SPAN * TOKENS, WIDTH), BF16),
        pltpu.VMEM((LAT, SPAN * TOKENS), BF16),
        pltpu.VMEM((MINE, HEADS * VAL), BF16),
        pltpu.VMEM((2, HEADS * VAL, 2 * TOKENS), BF16),
        pltpu.VMEM((4, 8, 256), F32),
        pltpu.VMEM((4, 8, 256), F32),
        pltpu.VMEM((4, LAT, 256), F32),
        pltpu.VMEM((2, 384, 256), F32),
        pltpu.VMEM((2, 384, 256), BF16),
        pltpu.VMEM((2, 2, 2, 2, 4, 2, 16, 256), BF16),
        pltpu.VMEM((2, 2, 2, 2, 2, 2, 16, 256), BF16),
        pltpu.VMEM((2, 2, 2, 2, 2, 16, 256), BF16),
        pltpu.VMEM((2, 4, 2, 2, 16, 256), BF16),
        pltpu.VMEM((4, 4, 2, 16, 256), BF16),
        dma((4,)),
        dma((16,)), dma((16,)),
        dma((2, 2)), dma((2, 2)),
        dma((3,)), dma((3,)),
        dma((2, 2)), dma((2, 2)),
        dma((2,)), dma((2,)),
        dma((3,)), dma((3,)),
        dma((4,)), dma((4,)),
        dma((3, 4)), dma((3, 4)),
        dma((2, 2, 2, 3)), dma((2, 2, 2, 3)),
        dma((4, 4)), dma((4, 4)),
    ]
    return pl.pallas_call(
        kernel,
        out_shape=jax.ShapeDtypeStruct((8, NBLK * COLS), BF16),
        in_specs=[pl.BlockSpec(memory_space=pltpu.SMEM), vmem] + [anywhere] * 4,
        out_specs=vmem,
        scratch_shapes=scratch,
        compiler_params=pltpu.CompilerParams(
            collective_id=0, has_side_effects=True, vmem_limit_bytes=60 * 1024 * 1024
        ),
        cost_estimate=pl.CostEstimate(flops=3_500_000_000, bytes_accessed=3_000_000, transcendentals=1_048_576),
    )(block_order, latent, queries.transpose(1, 2, 0), key_up_weight, value_up_weight, w_o.T)


def solution(mesh):
    placed = (
        P("blk", "head", None),
        P(("blk", "head"), None),
        P("head", None, None),
        P("head", None, None),
        P("head", "blk"),
        P(),
    )
    return jax.shard_map(
        shards, mesh=mesh, in_specs=placed, out_specs=P(("blk", "head"), None), check_vma=False
    )
```

```python
import functools
import math

import jax
import jax.numpy as jnp
from jax import lax
from jax.experimental import pallas as pl
from jax.experimental.pallas import tpu as pltpu
from jax.sharding import PartitionSpec as P

NOPE = 128
ROT = 64
LAT = 512
WIDTH = LAT + ROT
PADDED = 640
VAL = 128
HEADS = 8
TOKENS = 128
HALF = 64
SPAN = 8
NBLK = 32
COLS = 112
MINE = 1792
WIDE = ((0, 512), (1024, 384))
GAIN = (NOPE + ROT) ** (-0.5) * math.log2(math.e)
HIDDEN = -1e30
NT = (((1,), (1,)), ((), ()))
F32 = jnp.float32
BF16 = jnp.bfloat16


def nt_dot(a, b):
    return lax.dot_general(a, b, NT, preferred_element_type=F32)


def remote(src, dst, send, recv, device):
    return pltpu.make_async_remote_copy(
        src_ref=src, dst_ref=dst, send_sem=send, recv_sem=recv,
        device_id=device, device_id_type=pl.DeviceIdType.MESH,
    )


def kernel(
    order, latent, q_hbm, ku_hbm, vu_hbm, wo_hbm, out,
    q_raw, ku, vu, q_full, bias, pack, keys, wt, vals,
    top, total, accum, score, prob, ctx, terms_a, terms_b, got_a, got_b, relay_a, relay_b, part_a, part_b, fin_a, fin_b,
    load_sem, ps, pr, lzs, lzr, lcs, lcr, lys, lyr, lds, ldr,
    wps, wpr, wms, wmr, wcs, wcr, vs, vr, xs, xr, yss, ysr, yos, yor,
):
    b = lax.axis_index("blk")
    h = lax.axis_index("head")
    z, c = b // 4, b % 4
    lo, core = c // 2, c % 2
    hi, x = h // 4, h % 4
    up = (b + 4) % NBLK
    down = (b + NBLK - 4) % NBLK
    mate = b + 1 - 2 * core
    side = b + 2 - 4 * lo
    c_mate = c + 1 - 2 * core
    c_side = c + 2 - 4 * lo
    c_diag = c_side + 1 - 2 * core

    loads = [
        pltpu.make_async_copy(src, dst, load_sem.at[i])
        for i, (src, dst) in enumerate(((q_hbm, q_raw), (ku_hbm, ku), (vu_hbm, vu)))
    ]
    mine = wt.at[pl.ds(pl.multiple_of((z * 2 + core) * COLS, 16), COLS)]
    loads.append(pltpu.make_async_copy(wo_hbm, mine, load_sem.at[3]))
    for load in loads[3:] + loads[:3]:
        load.start()

    rows = latent[...].astype(F32)
    second = jnp.concatenate([rows[:, 384:], jnp.zeros((8, 192), F32)], axis=1)
    pack[h] = jnp.concatenate([rows[:, :384], second], axis=0).astype(BF16)

    barrier = pltpu.get_barrier_semaphore()

    def greet(device):
        pl.semaphore_signal(barrier, inc=1, device_id=device, device_id_type=pl.DeviceIdType.MESH)

    @pl.loop(1, 16)
    def _(i):
        greet({"head": (h + i) % 16})

    @pl.loop(0, 4)
    def _(i):
        greet({"blk": side, "head": (hi + i) % 4 * 4 + x})

    greet({"blk": up})
    greet({"blk": down})
    greet({"blk": mate})
    pl.semaphore_wait(barrier, 22)

    def own_rows(i):
        return remote(pack.at[h], pack.at[h], ps.at[i], pr.at[i], {"head": (h + i) % 16})

    def shard(zz, cc):
        return wt.at[pl.ds(pl.multiple_of((zz * 2 + cc) * COLS, 16), COLS)]

    def w_plus(k):
        ref = shard((z + 8 - k) % 8, core)
        return remote(ref, ref, wps.at[k], wpr.at[k], {"blk": up})

    def w_minus(k):
        ref = shard((z + k) % 8, core)
        return remote(ref, ref, wms.at[k], wmr.at[k], {"blk": down})

    def w_core(k):
        zz = (z + 8 - k) % 8 if k < 4 else (z + k - 3) % 8
        ref = shard(zz, core)
        return remote(ref, ref, wcs.at[k], wcr.at[k], {"blk": mate})

    def w_core_in(k):
        zz = (z + 8 - k) % 8 if k < 4 else (z + k - 3) % 8
        ref = shard(zz, 1 - core)
        return remote(ref, ref, wcs.at[k], wcr.at[k], {"blk": mate})

    def w_plus_in(k):
        ref = shard((z + 7 - k) % 8, core)
        return remote(ref, ref, wps.at[k], wpr.at[k], {"blk": up})

    def w_minus_in(k):
        ref = shard((z + 1 + k) % 8, core)
        return remote(ref, ref, wms.at[k], wmr.at[k], {"blk": down})

    loads[3].wait()
    w_plus(0).start()
    w_minus(0).start()

    @pl.loop(1, 16)
    def _(i):
        own_rows(i).start()

    w_core(0).start()

    loads[0].wait()
    loads[1].wait()
    for n in range(HEADS):
        lat = lax.dot_general(
            q_raw[n, :NOPE, :], ku[n], (((0,), (0,)), ((), ())), preferred_element_type=F32
        ).astype(BF16)
        turned = q_raw[n, NOPE:, :].astype(F32).T.astype(BF16)
        for t in range(2):
            at = slice(t * 512 + n * HALF, t * 512 + (n + 1) * HALF)
            q_full[at, :LAT] = lat[t * HALF:(t + 1) * HALF]
            q_full[at, LAT:] = turned[t * HALF:(t + 1) * HALF]

    row = lax.broadcasted_iota(jnp.int32, (TOKENS, TOKENS), 0)
    col = lax.broadcasted_iota(jnp.int32, (TOKENS, TOKENS), 1)
    q_pos = jnp.where(row < HALF, order[2 * b], order[2 * b + 1]) * HALF + row % HALF
    for n in range(SPAN):
        src = (b + NBLK - 7 + n) % NBLK
        k_pos = jnp.where(col < HALF, order[2 * src], order[2 * src + 1]) * HALF + col % HALF
        bias[:, n * TOKENS:(n + 1) * TOKENS] = jnp.where(k_pos <= q_pos, 0.0, HIDDEN)

    @pl.loop(1, 16)
    def _(i):
        ref = pack.at[(h + 16 - i) % 16]
        remote(ref, ref, ps.at[i], pr.at[i], {"head": (h + i) % 16}).wait_recv()

    def part_slot(plane, cc, half):
        first = (8 - 4 * plane + cc) * TOKENS + half * HALF
        return keys.at[pl.ds(pl.multiple_of(first, HALF), HALF)]

    def slot(plane, cc):
        return keys.at[pl.ds(pl.multiple_of((8 - 4 * plane + cc) * TOKENS, TOKENS), TOKENS)]

    gathered = pack[...].astype(F32)
    base = pl.multiple_of((8 + c) * TOKENS, TOKENS)
    keys[pl.ds(base, TOKENS), :384] = gathered[:, :8, :].reshape(TOKENS, 384).astype(BF16)
    keys[pl.ds(base, TOKENS), 384:] = gathered[:, 8:, :256].reshape(TOKENS, 256).astype(BF16)

    def l_up(k, half):
        src, dst = part_slot(k, c, half), part_slot(k + 1, c, half)
        return remote(src, dst, lzs.at[k, half], lzr.at[k, half], {"blk": up})

    def l_up_in(k, half):
        ref = part_slot(k + 1, c, half)
        return remote(ref, ref, lzs.at[k, half], lzr.at[k, half], {"blk": up})

    def l_core(p):
        return remote(slot(p, c), slot(p, c), lcs.at[p], lcr.at[p], {"blk": mate})

    def l_core_in(p):
        return remote(slot(p, c_mate), slot(p, c_mate), lcs.at[p], lcr.at[p], {"blk": mate})

    def l_side(j, half):
        ref = part_slot(j + lo, c, half)
        return remote(ref, ref, lys.at[j, half], lyr.at[j, half], {"blk": side})

    def l_side_in(j, half):
        ref = part_slot(j + 1 - lo, c_side, half)
        return remote(ref, ref, lys.at[j, half], lyr.at[j, half], {"blk": side})

    def l_diag(j):
        ref = slot(j + 1 - lo, c_side)
        return remote(ref, ref, lds.at[j], ldr.at[j], {"blk": mate})

    def l_diag_in(j):
        ref = slot(j + 1 - lo, c_diag)
        return remote(ref, ref, lds.at[j], ldr.at[j], {"blk": mate})

    def w_step_plus(k):
        w_plus_in(k - 1).wait_recv()
        if k < 3:
            w_plus(k).start()
        w_core(k).start()

    def w_step_minus(k):
        w_minus_in(k - 1).wait_recv()
        if k < 4:
            w_minus(k).start()
        w_core(3 + k).start()

    l_up(0, 0).start()
    l_up(0, 1).start()

    @pl.when(lo == 0)
    def _():
        l_side(0, 0).start()
        l_side(0, 1).start()

    l_core(0).start()
    w_step_minus(1)
    for half in range(2):
        l_up_in(0, half).wait_recv()
        l_up(1, half).start()
        l_side(1 - lo, half).start()

    l_core(1).start()
    w_step_plus(1)
    l_side_in(0, 0).wait_recv()
    l_side_in(0, 1).wait_recv()
    l_diag(0).start()
    for half in range(2):
        l_up_in(1, half).wait_recv()

        @pl.when(lo == 1)
        def _():
            l_side(1, half).start()

    l_core(2).start()
    w_step_minus(2)
    l_core_in(0).wait_recv()
    l_core_in(1).wait_recv()
    l_diag_in(0).wait_recv()

    def v_out(t):
        ref = vals.at[t, lo]
        return remote(ref, ref, vs.at[t], vr.at[t], {"blk": side})

    def v_in(t):
        ref = vals.at[t, 1 - lo]
        return remote(ref, ref, vs.at[t], vr.at[t], {"blk": side})

    def rows_at(t, g, first, count):
        return pl.ds(pl.multiple_of(t * 512 + g * 256 + first, 32), count)

    def step(t, start, first, last):
        k = keys[pl.ds(pl.multiple_of(start, TOKENS), 512), :WIDTH]
        for g in range(2):
            score[g] = nt_dot(q_full[rows_at(t, g, 0, 256), :], k)
        for g in range(2):
            factors = []
            for r in range(8):
                at = rows_at(t, g, r * 32, 32)
                tok = pl.ds(pl.multiple_of(t * HALF + r % 2 * 32, 32), 32)
                sc = score[g, r * 32:(r + 1) * 32, :] + bias[tok, first:first + 512]
                m = jnp.max(sc, axis=1, keepdims=True)
                if last:
                    old = top[at, :][:, :1]
                    m = jnp.maximum(m, old)
                e = jnp.exp2((sc - m) * GAIN)
                add = jnp.sum(e, axis=1, keepdims=True)
                prob[g, r * 32:(r + 1) * 32, :] = e.astype(BF16)
                if last:
                    shrink = jnp.exp2((old - m) * GAIN)
                    inverse = 1.0 / (total[at, :][:, :1] * shrink + add)
                    factors.append((shrink * inverse, inverse))
                else:
                    top[at, :] = jnp.broadcast_to(m, (32, 128))
                    total[at, :] = jnp.broadcast_to(add, (32, 128))
            got = jnp.dot(prob[g], k[:, :LAT], preferred_element_type=F32)
            if not last:
                accum[rows_at(t, g, 0, 256), :] = got
                continue
            score[g] = got
            for r in range(8):
                old, new = factors[r]
                ctx[g, r * 32:(r + 1) * 32, :] = (
                    accum[rows_at(t, g, r * 32, 32), :] * old + score[g, r * 32:(r + 1) * 32, :] * new
                ).astype(BF16)
            for n in range(4):
                head = 4 * g + n
                v = jnp.dot(ctx[g, n * HALF:(n + 1) * HALF, :], vu[head], preferred_element_type=F32)
                vals[t, lo, :, head * VAL:(head + 1) * VAL] = v.astype(BF16)

    @pl.loop(0, 2)
    def _(t):
        step(t, (c + 5) * TOKENS, 512, False)

        @pl.when(t == 0)
        def _():
            w_step_plus(2)
            l_side_in(1, 0).wait_recv()
            l_side_in(1, 1).wait_recv()
            l_diag(1).start()

    w_step_minus(3)
    loads[2].wait()
    l_core_in(2).wait_recv()
    l_diag_in(1).wait_recv()

    @pl.loop(0, 2)
    def _(t):
        step(t, (c + 1) * TOKENS, 0, True)
        v_out(t).start()

        @pl.when(t == 0)
        def _():
            w_step_plus(3)

    w_step_minus(4)
    for k in range(8):
        w_core_in(k).wait_recv()

    def x_out(t, n, way, kind):
        terms, got, relay = ((terms_a, got_a, relay_a), (terms_b, got_b, relay_b))[n]
        xd = (x + 1 + 2 * way) % 4
        if kind == 0:
            src, dst = terms.at[t, way, (x + 2) % 4], relay.at[t, way]
        else:
            r = 1 - way if kind == 1 else way
            src, dst = terms.at[t, r, xd], got.at[t, way, r]
        sem = (t, n, way, kind)
        return remote(src, dst, xs.at[sem], xr.at[sem], {"head": hi * 4 + xd})

    def project(t, n):
        first, width = WIDE[n]
        terms = (terms_a, terms_b)[n]
        both = vals[t].reshape(TOKENS, HEADS * VAL)
        out = nt_dot(both, wt[first:first + 2 * width, :])
        for y in range(2):
            left = out[y * HALF:(y + 1) * HALF, :width].reshape(8, 8, width)
            right = out[y * HALF:(y + 1) * HALF, width:].reshape(8, 8, width)
            pair = jnp.concatenate([left, right], axis=1).astype(BF16)
            terms[t, :, :, y] = pair.reshape(2, 4, 16, width)
        for kind in range(2):
            for way in range(2):
                x_out(t, n, way, kind).start()

    def pass_on(t, n):
        terms, relay = ((terms_a, relay_a), (terms_b, relay_b))[n]
        for way in range(2):
            x_out(t, n, way, 0).wait_recv()
            xd = (x + 1 + 2 * way) % 4
            both = terms[t, way, xd].astype(F32) + relay[t, way].astype(F32)
            terms[t, way, xd] = both.astype(BF16)
            x_out(t, n, way, 2).start()

    def y_same(n, yd, src):
        part, fin = ((part_a, fin_a), (part_b, fin_b))[n]
        return remote(
            part.at[yd, lo], fin.at[0, src], yss.at[n, yd], ysr.at[n, src], {"head": yd * 4 + x}
        )

    def y_other(n, yd, src):
        part, fin = ((part_a, fin_a), (part_b, fin_b))[n]
        return remote(
            part.at[yd, 1 - lo], fin.at[1, src], yos.at[n, yd], yor.at[n, src],
            {"blk": side, "head": yd * 4 + x},
        )

    def combine(t, n):
        terms, got, part = ((terms_a, got_a, part_a), (terms_b, got_b, part_b))[n]
        for way in range(2):
            x_out(t, n, way, 1).wait_recv()
            x_out(t, n, way, 2).wait_recv()
        both = terms[t, :, x].astype(F32) + got[t, 0].astype(F32) + got[t, 1].astype(F32)
        part[2 * t:2 * t + 2] = both.astype(BF16)
        for yd in (2 * t, 2 * t + 1):
            y_other(n, yd, hi).start()

            @pl.when(hi != yd)
            def _():
                y_same(n, yd, hi).start()

    v_in(0).wait_recv()
    project(0, 0)
    project(0, 1)
    pass_on(0, 0)
    v_in(1).wait_recv()
    project(1, 0)
    pass_on(0, 1)
    project(1, 1)
    combine(0, 0)
    pass_on(1, 0)
    combine(0, 1)
    pass_on(1, 1)
    combine(1, 0)
    combine(1, 1)
    same_cols, other_cols = [], []
    for n in range(2):
        part, fin = ((part_a, fin_a), (part_b, fin_b))[n]
        same = part[hi, lo].astype(F32)
        other = jnp.zeros_like(same)
        for e in (1, 2, 3):
            src = (hi + e) % 4
            y_same(n, src, src).wait_recv()
            same = same + fin[0, src].astype(F32)
        for src in range(4):
            y_other(n, src, src).wait_recv()
            other = other + fin[1, src].astype(F32)
        same_cols += [same[:8], same[8:]]
        other_cols += [other[:8], other[8:]]
    same = jnp.concatenate(same_cols, axis=1)
    other = jnp.concatenate(other_cols, axis=1)
    by_y = (jnp.where(lo == 0, same, other), jnp.where(lo == 0, other, same))
    pair = 2 * COLS
    out[...] = jnp.concatenate(
        [by_y[i % 2][:, i // 2 * pair:(i // 2 + 1) * pair] for i in range(16)], axis=1
    ).astype(BF16)

    @pl.loop(1, 16)
    def _(i):
        own_rows(i).wait_send()

    for k in range(2):
        for half in range(2):
            l_up(k, half).wait_send()
            l_side(k, half).wait_send()
        l_diag(k).wait_send()
    for k in range(3):
        l_core(k).wait_send()
        w_plus(k).wait_send()
    for k in range(4):
        w_minus(k).wait_send()
    for k in range(8):
        w_core(k).wait_send()
    for t in range(2):
        v_out(t).wait_send()
    for n in range(2):
        for t in range(2):
            for way in range(2):
                for kind in range(3):
                    x_out(t, n, way, kind).wait_send()
        for yd in range(4):
            y_other(n, yd, hi).wait_send()
        for e in (1, 2, 3):
            y_same(n, (hi + e) % 4, hi).wait_send()


def shards(queries, latent, key_up_weight, value_up_weight, w_o, block_order):
    vmem = pl.BlockSpec(memory_space=pltpu.VMEM)
    anywhere = pl.BlockSpec(memory_space=pl.ANY)
    dma = pltpu.SemaphoreType.DMA
    rows = TOKENS * HEADS
    scratch = [
        pltpu.VMEM((HEADS, NOPE + ROT, TOKENS), BF16),
        pltpu.VMEM((HEADS, NOPE, LAT), BF16),
        pltpu.VMEM((HEADS, LAT, VAL), BF16),
        pltpu.VMEM((rows, WIDTH), BF16),
        pltpu.VMEM((TOKENS, SPAN * TOKENS), F32),
        pltpu.VMEM((16, 16, 384), BF16),
        pltpu.VMEM((12 * TOKENS, PADDED), BF16),
        pltpu.VMEM((MINE, HEADS * VAL), BF16),
        pltpu.VMEM((2, 2, HALF, HEADS * VAL), BF16),
        pltpu.VMEM((rows, 128), F32),
        pltpu.VMEM((rows, 128), F32),
        pltpu.VMEM((rows, LAT), F32),
        pltpu.VMEM((2, 256, LAT), F32),
        pltpu.VMEM((2, 256, LAT), BF16),
        pltpu.VMEM((2, 256, LAT), BF16),
        pltpu.VMEM((2, 2, 4, 2, 16, 512), BF16),
        pltpu.VMEM((2, 2, 4, 2, 16, 384), BF16),
        pltpu.VMEM((2, 2, 2, 2, 16, 512), BF16),
        pltpu.VMEM((2, 2, 2, 2, 16, 384), BF16),
        pltpu.VMEM((2, 2, 2, 16, 512), BF16),
        pltpu.VMEM((2, 2, 2, 16, 384), BF16),
        pltpu.VMEM((4, 2, 16, 512), BF16),
        pltpu.VMEM((4, 2, 16, 384), BF16),
        pltpu.VMEM((2, 4, 16, 512), BF16),
        pltpu.VMEM((2, 4, 16, 384), BF16),
        dma((4,)),
        dma((16,)), dma((16,)),
        dma((2, 2)), dma((2, 2)),
        dma((3,)), dma((3,)),
        dma((2, 2)), dma((2, 2)),
        dma((2,)), dma((2,)),
        dma((3,)), dma((3,)),
        dma((4,)), dma((4,)),
        dma((8,)), dma((8,)),
        dma((2,)), dma((2,)),
        dma((2, 2, 2, 3)), dma((2, 2, 2, 3)),
        dma((2, 4)), dma((2, 4)),
        dma((2, 4)), dma((2, 4)),
    ]
    return pl.pallas_call(
        kernel,
        out_shape=jax.ShapeDtypeStruct((8, 2 * MINE), BF16),
        in_specs=[pl.BlockSpec(memory_space=pltpu.SMEM), vmem] + [anywhere] * 4,
        out_specs=vmem,
        scratch_shapes=scratch,
        compiler_params=pltpu.CompilerParams(
            collective_id=0, has_side_effects=True, vmem_limit_bytes=60 * 1024 * 1024
        ),
        cost_estimate=pl.CostEstimate(flops=3_500_000_000, bytes_accessed=3_000_000, transcendentals=1_048_576),
    )(block_order, latent, queries.transpose(1, 2, 0), key_up_weight, value_up_weight, w_o.T)


def solution(mesh):
    placed = (
        P("blk", "head", None),
        P(("blk", "head"), None),
        P("head", None, None),
        P("head", None, None),
        P("head", "blk"),
        P(),
    )
    return jax.shard_map(
        shards, mesh=mesh, in_specs=placed, out_specs=P(("blk", "head"), None), check_vma=False
    )
```

```python
import functools
import math

import jax
import jax.numpy as jnp
from jax import lax
from jax.experimental import pallas as pl
from jax.experimental.pallas import tpu as pltpu
from jax.sharding import PartitionSpec as P

NOPE = 128
ROT = 64
LAT = 512
WIDTH = LAT + ROT
VAL = 128
HEADS = 8
TOKENS = 128
HALF = 64
SPAN = 8
NBLK = 32
COLS = 112
MINE = 1792
WIDE = ((0, 512), (1024, 384))
GAIN = (NOPE + ROT) ** (-0.5) * math.log2(math.e)
HIDDEN = -1e30
NT = (((1,), (1,)), ((), ()))
F32 = jnp.float32
BF16 = jnp.bfloat16


def nt_dot(a, b):
    return lax.dot_general(a, b, NT, preferred_element_type=F32)


def remote(src, dst, send, recv, device):
    return pltpu.make_async_remote_copy(
        src_ref=src, dst_ref=dst, send_sem=send, recv_sem=recv,
        device_id=device, device_id_type=pl.DeviceIdType.MESH,
    )


def kernel(
    order_hbm, latent_hbm, q_hbm, ku_hbm, vu_hbm, wo_hbm, out,
    order, latent, q_raw, ku, vu, q_full, bias, pack, keys, wt, vals,
    top, total, accum, score, prob, ctx, terms_a, terms_b, got_a, got_b, relay_a, relay_b, part_a, part_b, fin_a, fin_b,
    load_sem, ps, pr, lzs, lzr, lcs, lcr, lys, lyr, lds, ldr,
    wps, wpr, wms, wmr, wcs, wcr, vs, vr, xs, xr, yss, ysr, yos, yor,
):
    b = lax.axis_index("blk")
    h = lax.axis_index("head")
    z, c = b // 4, b % 4
    lo, core = c // 2, c % 2
    hi, x = h // 4, h % 4
    up = (b + 4) % NBLK
    down = (b + NBLK - 4) % NBLK
    mate = b + 1 - 2 * core
    side = b + 2 - 4 * lo
    up_side, down_side = (side + 4) % NBLK, (side + NBLK - 4) % NBLK
    c_mate = c + 1 - 2 * core
    c_side = c + 2 - 4 * lo
    c_diag = c_side + 1 - 2 * core

    loads = [
        pltpu.make_async_copy(src, dst, load_sem.at[i])
        for i, (src, dst) in enumerate(((q_hbm, q_raw), (ku_hbm, ku), (vu_hbm, vu)))
    ]
    mine = wt.at[pl.ds(pl.multiple_of((z * 2 + core) * COLS, 16), COLS)]
    loads.append(pltpu.make_async_copy(wo_hbm, mine, load_sem.at[3]))
    loads.append(pltpu.make_async_copy(latent_hbm, latent, load_sem.at[4]))
    loads.append(pltpu.make_async_copy(order_hbm, order, load_sem.at[5]))
    for load in loads[4:] + loads[3:4] + loads[:3]:
        load.start()

    barrier = pltpu.get_barrier_semaphore()

    def greet(device):
        pl.semaphore_signal(barrier, inc=1, device_id=device, device_id_type=pl.DeviceIdType.MESH)

    @pl.loop(1, 16)
    def _(i):
        greet({"head": (h + i) % 16})

    @pl.loop(0, 4)
    def _(i):
        greet({"blk": side, "head": (hi + i) % 4 * 4 + x})

    greet({"blk": up})
    greet({"blk": down})
    greet({"blk": mate})
    greet({"blk": up_side})
    greet({"blk": down_side})
    loads[4].wait()
    rows = latent[...].astype(F32)
    second = jnp.concatenate([rows[:, 384:], jnp.zeros((8, 192), F32)], axis=1)
    pack[h] = jnp.concatenate([rows[:, :384], second], axis=0).astype(BF16)
    pl.semaphore_wait(barrier, 24)

    def own_rows(i):
        return remote(pack.at[h], pack.at[h], ps.at[i], pr.at[i], {"head": (h + i) % 16})

    def shard(zz, cc):
        return wt.at[pl.ds(pl.multiple_of((zz * 2 + cc) * COLS, 16), COLS)]

    def w_plus(k):
        ref = shard((z + 8 - k) % 8, core)
        return remote(ref, ref, wps.at[k], wpr.at[k], {"blk": up})

    def w_minus(k):
        ref = shard((z + k) % 8, core)
        return remote(ref, ref, wms.at[k], wmr.at[k], {"blk": down})

    def w_core(k):
        zz = (z + 8 - k) % 8 if k < 4 else (z + k - 3) % 8
        ref = shard(zz, core)
        return remote(ref, ref, wcs.at[k], wcr.at[k], {"blk": mate})

    def w_core_in(k):
        zz = (z + 8 - k) % 8 if k < 4 else (z + k - 3) % 8
        ref = shard(zz, 1 - core)
        return remote(ref, ref, wcs.at[k], wcr.at[k], {"blk": mate})

    def w_plus_in(k):
        ref = shard((z + 7 - k) % 8, core)
        return remote(ref, ref, wps.at[k], wpr.at[k], {"blk": up})

    def w_minus_in(k):
        ref = shard((z + 1 + k) % 8, core)
        return remote(ref, ref, wms.at[k], wmr.at[k], {"blk": down})

    loads[3].wait()
    w_plus(0).start()
    w_minus(0).start()

    @pl.loop(1, 16)
    def _(i):
        own_rows(i).start()

    w_core(0).start()

    loads[0].wait()
    loads[1].wait()
    for n in range(HEADS):
        lat = lax.dot_general(
            q_raw[n, :NOPE, :], ku[n], (((0,), (0,)), ((), ())), preferred_element_type=F32
        ).astype(BF16)
        turned = q_raw[n, NOPE:, :].astype(F32).T.astype(BF16)
        for t in range(2):
            at = slice(t * 512 + n * HALF, t * 512 + (n + 1) * HALF)
            q_full[at, :LAT] = lat[t * HALF:(t + 1) * HALF]
            q_full[at, LAT:] = turned[t * HALF:(t + 1) * HALF]

    loads[5].wait()
    row = lax.broadcasted_iota(jnp.int32, (TOKENS, TOKENS), 0)
    col = lax.broadcasted_iota(jnp.int32, (TOKENS, TOKENS), 1)
    q_pos = jnp.where(row < HALF, order[2 * b], order[2 * b + 1]) * HALF + row % HALF
    for n in range(SPAN):
        src = (b + NBLK - 7 + n) % NBLK
        k_pos = jnp.where(col < HALF, order[2 * src], order[2 * src + 1]) * HALF + col % HALF
        bias[:, n * TOKENS:(n + 1) * TOKENS] = jnp.where(k_pos <= q_pos, 0.0, HIDDEN)

    @pl.loop(1, 16)
    def _(i):
        ref = pack.at[(h + 16 - i) % 16]
        remote(ref, ref, ps.at[i], pr.at[i], {"head": (h + i) % 16}).wait_recv()

    def part_slot(plane, cc, half):
        first = (8 - 4 * plane + cc) * TOKENS + half * HALF
        return keys.at[pl.ds(pl.multiple_of(first, HALF), HALF)]

    def slot(plane, cc):
        return keys.at[pl.ds(pl.multiple_of((8 - 4 * plane + cc) * TOKENS, TOKENS), TOKENS)]

    gathered = pack[...].astype(F32)
    base = pl.multiple_of((8 + c) * TOKENS, TOKENS)
    keys[pl.ds(base, TOKENS), :384] = gathered[:, :8, :].reshape(TOKENS, 384).astype(BF16)
    keys[pl.ds(base, TOKENS), 384:] = gathered[:, 8:, :192].reshape(TOKENS, 192).astype(BF16)

    def l_up(k, half):
        src, dst = part_slot(k, c, half), part_slot(k + 1, c, half)
        return remote(src, dst, lzs.at[k, half], lzr.at[k, half], {"blk": up})

    def l_up_in(k, half):
        ref = part_slot(k + 1, c, half)
        return remote(ref, ref, lzs.at[k, half], lzr.at[k, half], {"blk": up})

    def l_core(p):
        return remote(slot(p, c), slot(p, c), lcs.at[p], lcr.at[p], {"blk": mate})

    def l_core_in(p):
        return remote(slot(p, c_mate), slot(p, c_mate), lcs.at[p], lcr.at[p], {"blk": mate})

    def l_side(j, half):
        src = part_slot(j * lo, c, half)
        dst = part_slot(j + lo, c, half)
        blk = side * (1 - lo) + up_side * lo if j == 0 else up_side
        return remote(src, dst, lys.at[j, half], lyr.at[j, half], {"blk": blk})

    def l_side_in(j, half):
        ref = part_slot(j + 1 - lo, c_side, half)
        return remote(ref, ref, lys.at[j, half], lyr.at[j, half], {"blk": side})

    def l_diag(j):
        ref = slot(j + 1 - lo, c_side)
        return remote(ref, ref, lds.at[j], ldr.at[j], {"blk": mate})

    def l_diag_in(j):
        ref = slot(j + 1 - lo, c_diag)
        return remote(ref, ref, lds.at[j], ldr.at[j], {"blk": mate})

    def w_step_plus(k):
        w_plus_in(k - 1).wait_recv()
        if k < 3:
            w_plus(k).start()
        w_core(k).start()

    def w_step_minus(k):
        w_minus_in(k - 1).wait_recv()
        if k < 4:
            w_minus(k).start()
        w_core(3 + k).start()

    l_up(0, 0).start()
    l_up(0, 1).start()

    l_side(0, 0).start()
    l_side(0, 1).start()

    @pl.when(lo == 0)
    def _():
        l_side(1, 0).start()
        l_side(1, 1).start()

    l_core(0).start()
    w_step_minus(1)
    for half in range(2):
        l_up_in(0, half).wait_recv()
        l_up(1, half).start()

        @pl.when(lo == 1)
        def _():
            l_side(1, half).start()

    l_core(1).start()
    w_step_plus(1)
    l_side_in(0, 0).wait_recv()
    l_side_in(0, 1).wait_recv()
    l_diag(0).start()
    for half in range(2):
        l_up_in(1, half).wait_recv()

    l_core(2).start()
    w_step_minus(2)
    l_core_in(0).wait_recv()
    l_core_in(1).wait_recv()
    l_diag_in(0).wait_recv()

    def v_out(t):
        ref = vals.at[t, lo]
        return remote(ref, ref, vs.at[t], vr.at[t], {"blk": side})

    def v_in(t):
        ref = vals.at[t, 1 - lo]
        return remote(ref, ref, vs.at[t], vr.at[t], {"blk": side})

    def rows_at(t, g, first, count):
        return pl.ds(pl.multiple_of(t * 512 + g * 256 + first, 32), count)

    def step(t, start, first, last):
        k = keys[pl.ds(pl.multiple_of(start, TOKENS), 512), :]
        for g in range(2):
            score[g] = nt_dot(q_full[rows_at(t, g, 0, 256), :], k)
        for g in range(2):
            factors = []
            for r in range(8):
                at = rows_at(t, g, r * 32, 32)
                tok = pl.ds(pl.multiple_of(t * HALF + r % 2 * 32, 32), 32)
                sc = score[g, r * 32:(r + 1) * 32, :] + bias[tok, first:first + 512]
                m = jnp.max(sc, axis=1, keepdims=True)
                if last:
                    old = top[at, :][:, :1]
                    m = jnp.maximum(m, old)
                e = jnp.exp2((sc - m) * GAIN)
                add = jnp.sum(e, axis=1, keepdims=True)
                prob[g, r * 32:(r + 1) * 32, :] = e.astype(BF16)
                if last:
                    shrink = jnp.exp2((old - m) * GAIN)
                    inverse = 1.0 / (total[at, :][:, :1] * shrink + add)
                    factors.append((shrink * inverse, inverse))
                else:
                    top[at, :] = jnp.broadcast_to(m, (32, 128))
                    total[at, :] = jnp.broadcast_to(add, (32, 128))
            got = jnp.dot(prob[g], k[:, :LAT], preferred_element_type=F32)
            if not last:
                accum[rows_at(t, g, 0, 256), :] = got
                continue
            score[g] = got
            for r in range(8):
                old, new = factors[r]
                ctx[g, r * 32:(r + 1) * 32, :] = (
                    accum[rows_at(t, g, r * 32, 32), :] * old + score[g, r * 32:(r + 1) * 32, :] * new
                ).astype(BF16)
            for n in range(4):
                head = 4 * g + n
                v = jnp.dot(ctx[g, n * HALF:(n + 1) * HALF, :], vu[head], preferred_element_type=F32)
                vals[t, lo, :, head * VAL:(head + 1) * VAL] = v.astype(BF16)

    @pl.loop(0, 2)
    def _(t):
        step(t, (c + 5) * TOKENS, 512, False)

        @pl.when(t == 0)
        def _():
            w_step_plus(2)
            l_side_in(1, 0).wait_recv()
            l_side_in(1, 1).wait_recv()
            l_diag(1).start()

    w_step_minus(3)
    loads[2].wait()
    l_core_in(2).wait_recv()
    l_diag_in(1).wait_recv()

    @pl.loop(0, 2)
    def _(t):
        step(t, (c + 1) * TOKENS, 0, True)
        v_out(t).start()

        @pl.when(t == 0)
        def _():
            w_step_plus(3)

    w_step_minus(4)
    for k in range(8):
        w_core_in(k).wait_recv()

    def x_out(t, n, way, kind):
        terms, got, relay = ((terms_a, got_a, relay_a), (terms_b, got_b, relay_b))[n]
        xd = (x + 1 + 2 * way) % 4
        if kind == 0:
            src, dst = terms.at[t, way, (x + 2) % 4], relay.at[t, way]
        else:
            r = 1 - way if kind == 1 else way
            src, dst = terms.at[t, r, xd], got.at[t, way, r]
        sem = (t, n, way, kind)
        return remote(src, dst, xs.at[sem], xr.at[sem], {"head": hi * 4 + xd})

    def project(t, n):
        first, width = WIDE[n]
        terms = (terms_a, terms_b)[n]
        both = vals[t].reshape(TOKENS, HEADS * VAL)
        out = nt_dot(both, wt[first:first + 2 * width, :])
        for y in range(2):
            left = out[y * HALF:(y + 1) * HALF, :width].reshape(8, 8, width)
            right = out[y * HALF:(y + 1) * HALF, width:].reshape(8, 8, width)
            pair = jnp.concatenate([left, right], axis=1).astype(BF16)
            terms[t, :, :, y] = pair.reshape(2, 4, 16, width)
        for kind in range(2):
            for way in range(2):
                x_out(t, n, way, kind).start()

    def pass_on(t, n):
        terms, relay = ((terms_a, relay_a), (terms_b, relay_b))[n]
        for way in range(2):
            x_out(t, n, way, 0).wait_recv()
            xd = (x + 1 + 2 * way) % 4
            both = terms[t, way, xd].astype(F32) + relay[t, way].astype(F32)
            terms[t, way, xd] = both.astype(BF16)
            x_out(t, n, way, 2).start()

    def y_same(n, yd, src):
        part, fin = ((part_a, fin_a), (part_b, fin_b))[n]
        return remote(
            part.at[yd, lo], fin.at[0, src], yss.at[n, yd], ysr.at[n, src], {"head": yd * 4 + x}
        )

    def y_other(n, yd, src):
        part, fin = ((part_a, fin_a), (part_b, fin_b))[n]
        return remote(
            part.at[yd, 1 - lo], fin.at[1, src], yos.at[n, yd], yor.at[n, src],
            {"blk": side, "head": yd * 4 + x},
        )

    def combine(t, n):
        terms, got, part = ((terms_a, got_a, part_a), (terms_b, got_b, part_b))[n]
        for way in range(2):
            x_out(t, n, way, 1).wait_recv()
            x_out(t, n, way, 2).wait_recv()
        both = terms[t, :, x].astype(F32) + got[t, 0].astype(F32) + got[t, 1].astype(F32)
        part[2 * t:2 * t + 2] = both.astype(BF16)
        for yd in (2 * t, 2 * t + 1):
            y_other(n, yd, hi).start()

            @pl.when(hi != yd)
            def _():
                y_same(n, yd, hi).start()

    v_in(0).wait_recv()
    project(0, 0)
    project(0, 1)
    pass_on(0, 0)
    v_in(1).wait_recv()
    project(1, 0)
    pass_on(0, 1)
    project(1, 1)
    combine(0, 0)
    pass_on(1, 0)
    combine(0, 1)
    pass_on(1, 1)
    combine(1, 0)
    combine(1, 1)
    same_cols, other_cols = [], []
    for n in range(2):
        part, fin = ((part_a, fin_a), (part_b, fin_b))[n]
        same = part[hi, lo].astype(F32)
        other = jnp.zeros_like(same)
        for e in (1, 2, 3):
            src = (hi + e) % 4
            y_same(n, src, src).wait_recv()
            same = same + fin[0, src].astype(F32)
        for src in range(4):
            y_other(n, src, src).wait_recv()
            other = other + fin[1, src].astype(F32)
        same_cols += [same[:8], same[8:]]
        other_cols += [other[:8], other[8:]]
    same = jnp.concatenate(same_cols, axis=1)
    other = jnp.concatenate(other_cols, axis=1)
    by_y = (jnp.where(lo == 0, same, other), jnp.where(lo == 0, other, same))
    pair = 2 * COLS
    out[...] = jnp.concatenate(
        [by_y[i % 2][:, i // 2 * pair:(i // 2 + 1) * pair] for i in range(16)], axis=1
    ).astype(BF16)

    @pl.loop(1, 16)
    def _(i):
        own_rows(i).wait_send()

    for k in range(2):
        for half in range(2):
            l_up(k, half).wait_send()
            l_side(k, half).wait_send()
        l_diag(k).wait_send()
    for k in range(3):
        l_core(k).wait_send()
        w_plus(k).wait_send()
    for k in range(4):
        w_minus(k).wait_send()
    for k in range(8):
        w_core(k).wait_send()
    for t in range(2):
        v_out(t).wait_send()
    for n in range(2):
        for t in range(2):
            for way in range(2):
                for kind in range(3):
                    x_out(t, n, way, kind).wait_send()
        for yd in range(4):
            y_other(n, yd, hi).wait_send()
        for e in (1, 2, 3):
            y_same(n, (hi + e) % 4, hi).wait_send()


def shards(queries, latent, key_up_weight, value_up_weight, w_o, block_order):
    vmem = pl.BlockSpec(memory_space=pltpu.VMEM)
    anywhere = pl.BlockSpec(memory_space=pl.ANY)
    dma = pltpu.SemaphoreType.DMA
    rows = TOKENS * HEADS
    scratch = [
        pltpu.SMEM((64,), jnp.int32),
        pltpu.VMEM((8, WIDTH), BF16),
        pltpu.VMEM((HEADS, NOPE + ROT, TOKENS), BF16),
        pltpu.VMEM((HEADS, NOPE, LAT), BF16),
        pltpu.VMEM((HEADS, LAT, VAL), BF16),
        pltpu.VMEM((rows, WIDTH), BF16),
        pltpu.VMEM((TOKENS, SPAN * TOKENS), F32),
        pltpu.VMEM((16, 16, 384), BF16),
        pltpu.VMEM((12 * TOKENS, WIDTH), BF16),
        pltpu.VMEM((MINE, HEADS * VAL), BF16),
        pltpu.VMEM((2, 2, HALF, HEADS * VAL), BF16),
        pltpu.VMEM((rows, 128), F32),
        pltpu.VMEM((rows, 128), F32),
        pltpu.VMEM((rows, LAT), F32),
        pltpu.VMEM((2, 256, LAT), F32),
        pltpu.VMEM((2, 256, LAT), BF16),
        pltpu.VMEM((2, 256, LAT), BF16),
        pltpu.VMEM((2, 2, 4, 2, 16, 512), BF16),
        pltpu.VMEM((2, 2, 4, 2, 16, 384), BF16),
        pltpu.VMEM((2, 2, 2, 2, 16, 512), BF16),
        pltpu.VMEM((2, 2, 2, 2, 16, 384), BF16),
        pltpu.VMEM((2, 2, 2, 16, 512), BF16),
        pltpu.VMEM((2, 2, 2, 16, 384), BF16),
        pltpu.VMEM((4, 2, 16, 512), BF16),
        pltpu.VMEM((4, 2, 16, 384), BF16),
        pltpu.VMEM((2, 4, 16, 512), BF16),
        pltpu.VMEM((2, 4, 16, 384), BF16),
        dma((6,)),
        dma((16,)), dma((16,)),
        dma((2, 2)), dma((2, 2)),
        dma((3,)), dma((3,)),
        dma((2, 2)), dma((2, 2)),
        dma((2,)), dma((2,)),
        dma((3,)), dma((3,)),
        dma((4,)), dma((4,)),
        dma((8,)), dma((8,)),
        dma((2,)), dma((2,)),
        dma((2, 2, 2, 3)), dma((2, 2, 2, 3)),
        dma((2, 4)), dma((2, 4)),
        dma((2, 4)), dma((2, 4)),
    ]
    return pl.pallas_call(
        kernel,
        out_shape=jax.ShapeDtypeStruct((8, 2 * MINE), BF16),
        in_specs=[anywhere] * 6,
        out_specs=vmem,
        scratch_shapes=scratch,
        compiler_params=pltpu.CompilerParams(
            collective_id=0, has_side_effects=True, vmem_limit_bytes=60 * 1024 * 1024
        ),
        cost_estimate=pl.CostEstimate(flops=3_500_000_000, bytes_accessed=3_000_000, transcendentals=1_048_576),
    )(block_order, latent, queries.transpose(1, 2, 0), key_up_weight, value_up_weight, w_o.T)


def solution(mesh):
    placed = (
        P("blk", "head", None),
        P(("blk", "head"), None),
        P("head", None, None),
        P("head", None, None),
        P("head", "blk"),
        P(),
    )
    return jax.shard_map(
        shards, mesh=mesh, in_specs=placed, out_specs=P(("blk", "head"), None), check_vma=False
    )
```

```python
import functools
import math

import jax
import jax.numpy as jnp
from jax import lax
from jax.experimental import pallas as pl
from jax.experimental.pallas import tpu as pltpu
from jax.sharding import PartitionSpec as P

NOPE = 128
ROT = 64
LAT = 512
WIDTH = LAT + ROT
VAL = 128
HEADS = 8
TOKENS = 128
HALF = 64
SPAN = 8
NBLK = 32
COLS = 112
MINE = 1792
WIDE = ((0, 512), (1024, 384))
GAIN = (NOPE + ROT) ** (-0.5) * math.log2(math.e)
HIDDEN = -1e30
NT = (((1,), (1,)), ((), ()))
F32 = jnp.float32
BF16 = jnp.bfloat16


def nt_dot(a, b):
    return lax.dot_general(a, b, NT, preferred_element_type=F32)


def remote(src, dst, send, recv, device):
    return pltpu.make_async_remote_copy(
        src_ref=src, dst_ref=dst, send_sem=send, recv_sem=recv,
        device_id=device, device_id_type=pl.DeviceIdType.MESH,
    )


def kernel(
    order, latent, q_hbm, ku_hbm, vu_hbm, wo_hbm, out,
    q_raw, ku, vu, q_full, bias, pack, keys, wt, vals,
    top, total, accum, score, prob, ctx, terms_a, terms_b, got_a, got_b, relay_a, relay_b, part_a, part_b, fin_a, fin_b,
    load_sem, ps, pr, lzs, lzr, lcs, lcr, lys, lyr, lds, ldr,
    wps, wpr, wms, wmr, wcs, wcr, vs, vr, xs, xr, yss, ysr, yos, yor,
):
    b = lax.axis_index("blk")
    h = lax.axis_index("head")
    z, c = b // 4, b % 4
    lo, core = c // 2, c % 2
    hi, x = h // 4, h % 4
    up = (b + 4) % NBLK
    down = (b + NBLK - 4) % NBLK
    mate = b + 1 - 2 * core
    side = b + 2 - 4 * lo
    c_mate = c + 1 - 2 * core
    c_side = c + 2 - 4 * lo
    c_diag = c_side + 1 - 2 * core

    loads = [
        pltpu.make_async_copy(src, dst, load_sem.at[i])
        for i, (src, dst) in enumerate(((q_hbm, q_raw), (ku_hbm, ku), (vu_hbm, vu)))
    ]
    mine = wt.at[pl.ds(pl.multiple_of((z * 2 + core) * COLS, 16), COLS)]
    loads.append(pltpu.make_async_copy(wo_hbm, mine, load_sem.at[3]))
    for load in loads[3:] + loads[:3]:
        load.start()

    rows = latent[...].astype(F32)
    second = jnp.concatenate([rows[:, 384:], jnp.zeros((8, 192), F32)], axis=1)
    pack[h] = jnp.concatenate([rows[:, :384], second], axis=0).astype(BF16)

    barrier = pltpu.get_barrier_semaphore()

    def greet(device):
        pl.semaphore_signal(barrier, inc=1, device_id=device, device_id_type=pl.DeviceIdType.MESH)

    @pl.loop(1, 16)
    def _(i):
        greet({"head": (h + i) % 16})

    @pl.loop(0, 4)
    def _(i):
        greet({"blk": side, "head": (hi + i) % 4 * 4 + x})

    greet({"blk": up})
    greet({"blk": down})
    greet({"blk": mate})
    pl.semaphore_wait(barrier, 22)

    def own_rows(i):
        return remote(pack.at[h], pack.at[h], ps.at[i], pr.at[i], {"head": (h + i) % 16})

    def shard(zz, cc, half):
        first = (zz * 2 + cc) * COLS + 64 * half
        return wt.at[pl.ds(pl.multiple_of(first, 16), (64, 48)[half])]

    def w_plus(k, half):
        ref = shard((z + 8 - k) % 8, core, half)
        return remote(ref, ref, wps.at[k, half], wpr.at[k, half], {"blk": up})

    def w_minus(k, half):
        ref = shard((z + k) % 8, core, half)
        return remote(ref, ref, wms.at[k, half], wmr.at[k, half], {"blk": down})

    def w_core(k, half):
        zz = (z + 8 - k) % 8 if k < 4 else (z + k - 3) % 8
        ref = shard(zz, core, half)
        return remote(ref, ref, wcs.at[k, half], wcr.at[k, half], {"blk": mate})

    def w_core_in(k, half):
        zz = (z + 8 - k) % 8 if k < 4 else (z + k - 3) % 8
        ref = shard(zz, 1 - core, half)
        return remote(ref, ref, wcs.at[k, half], wcr.at[k, half], {"blk": mate})

    def w_plus_in(k, half):
        ref = shard((z + 7 - k) % 8, core, half)
        return remote(ref, ref, wps.at[k, half], wpr.at[k, half], {"blk": up})

    def w_minus_in(k, half):
        ref = shard((z + 1 + k) % 8, core, half)
        return remote(ref, ref, wms.at[k, half], wmr.at[k, half], {"blk": down})

    def w_step_plus(k, half):
        w_plus_in(k - 1, half).wait_recv()
        if k < 3:
            w_plus(k, half).start()
        w_core(k, half).start()

    def w_step_minus(k, half):
        w_minus_in(k - 1, half).wait_recv()
        if k < 4:
            w_minus(k, half).start()
        w_core(3 + k, half).start()

    loads[3].wait()
    for half in range(2):
        w_plus(0, half).start()
        w_minus(0, half).start()

    @pl.loop(1, 16)
    def _(i):
        own_rows(i).start()

    for half in range(2):
        w_core(0, half).start()

    loads[0].wait()
    loads[1].wait()
    for n in range(HEADS):
        lat = lax.dot_general(
            q_raw[n, :NOPE, :], ku[n], (((0,), (0,)), ((), ())), preferred_element_type=F32
        ).astype(BF16)
        turned = q_raw[n, NOPE:, :].astype(F32).T.astype(BF16)
        for t in range(2):
            at = slice(t * 512 + n * HALF, t * 512 + (n + 1) * HALF)
            q_full[at, :LAT] = lat[t * HALF:(t + 1) * HALF]
            q_full[at, LAT:] = turned[t * HALF:(t + 1) * HALF]

    row = lax.broadcasted_iota(jnp.int32, (TOKENS, TOKENS), 0)
    col = lax.broadcasted_iota(jnp.int32, (TOKENS, TOKENS), 1)
    q_pos = jnp.where(row < HALF, order[2 * b], order[2 * b + 1]) * HALF + row % HALF
    for n in range(SPAN):
        src = (b + NBLK - 7 + n) % NBLK
        k_pos = jnp.where(col < HALF, order[2 * src], order[2 * src + 1]) * HALF + col % HALF
        bias[:, n * TOKENS:(n + 1) * TOKENS] = jnp.where(k_pos <= q_pos, 0.0, HIDDEN)

    @pl.loop(1, 16)
    def _(i):
        ref = pack.at[(h + 16 - i) % 16]
        remote(ref, ref, ps.at[i], pr.at[i], {"head": (h + i) % 16}).wait_recv()

    def part_slot(plane, cc, half):
        first = (8 - 4 * plane + cc) * TOKENS + half * HALF
        return keys.at[pl.ds(pl.multiple_of(first, HALF), HALF)]

    def slot(plane, cc):
        return keys.at[pl.ds(pl.multiple_of((8 - 4 * plane + cc) * TOKENS, TOKENS), TOKENS)]

    gathered = pack[...].astype(F32)
    base = pl.multiple_of((8 + c) * TOKENS, TOKENS)
    keys[pl.ds(base, TOKENS), :384] = gathered[:, :8, :].reshape(TOKENS, 384).astype(BF16)
    keys[pl.ds(base, TOKENS), 384:] = gathered[:, 8:, :192].reshape(TOKENS, 192).astype(BF16)

    def l_up(k, half):
        src, dst = part_slot(k, c, half), part_slot(k + 1, c, half)
        return remote(src, dst, lzs.at[k, half], lzr.at[k, half], {"blk": up})

    def l_up_in(k, half):
        ref = part_slot(k + 1, c, half)
        return remote(ref, ref, lzs.at[k, half], lzr.at[k, half], {"blk": up})

    def l_core(p):
        return remote(slot(p, c), slot(p, c), lcs.at[p], lcr.at[p], {"blk": mate})

    def l_core_in(p):
        return remote(slot(p, c_mate), slot(p, c_mate), lcs.at[p], lcr.at[p], {"blk": mate})

    def l_side(j, half):
        ref = part_slot(j + lo, c, half)
        return remote(ref, ref, lys.at[j, half], lyr.at[j, half], {"blk": side})

    def l_side_in(j, half):
        ref = part_slot(j + 1 - lo, c_side, half)
        return remote(ref, ref, lys.at[j, half], lyr.at[j, half], {"blk": side})

    def l_diag(j):
        ref = slot(j + 1 - lo, c_side)
        return remote(ref, ref, lds.at[j], ldr.at[j], {"blk": mate})

    def l_diag_in(j):
        ref = slot(j + 1 - lo, c_diag)
        return remote(ref, ref, lds.at[j], ldr.at[j], {"blk": mate})

    l_up(0, 0).start()
    l_up(0, 1).start()

    @pl.when(lo == 0)
    def _():
        l_side(0, 0).start()
        l_side(0, 1).start()

    l_core(0).start()
    for half in range(2):
        w_step_minus(1, half)
    for half in range(2):
        l_up_in(0, half).wait_recv()
        l_up(1, half).start()
        l_side(1 - lo, half).start()

    l_core(1).start()
    w_step_minus(2, 0)
    for half in range(2):
        w_step_plus(1, half)
    w_step_minus(2, 1)
    l_side_in(0, 0).wait_recv()
    l_side_in(0, 1).wait_recv()
    l_diag(0).start()
    for half in range(2):
        l_up_in(1, half).wait_recv()

        @pl.when(lo == 1)
        def _():
            l_side(1, half).start()

    l_core(2).start()
    l_core_in(0).wait_recv()
    l_core_in(1).wait_recv()
    l_diag_in(0).wait_recv()

    def v_out(t):
        ref = vals.at[t, lo]
        return remote(ref, ref, vs.at[t], vr.at[t], {"blk": side})

    def v_in(t):
        ref = vals.at[t, 1 - lo]
        return remote(ref, ref, vs.at[t], vr.at[t], {"blk": side})

    def rows_at(t, g, first, count):
        return pl.ds(pl.multiple_of(t * 512 + g * 256 + first, 32), count)

    def step(t, start, first, last):
        k = keys[pl.ds(pl.multiple_of(start, TOKENS), 512), :]
        for g in range(2):
            score[g] = nt_dot(q_full[rows_at(t, g, 0, 256), :], k)
        for g in range(2):
            factors = []
            for r in range(8):
                at = rows_at(t, g, r * 32, 32)
                tok = pl.ds(pl.multiple_of(t * HALF + r % 2 * 32, 32), 32)
                sc = score[g, r * 32:(r + 1) * 32, :] + bias[tok, first:first + 512]
                m = jnp.max(sc, axis=1, keepdims=True)
                if last:
                    old = top[at, :][:, :1]
                    m = jnp.maximum(m, old)
                e = jnp.exp2((sc - m) * GAIN)
                add = jnp.sum(e, axis=1, keepdims=True)
                prob[g, r * 32:(r + 1) * 32, :] = e.astype(BF16)
                if last:
                    shrink = jnp.exp2((old - m) * GAIN)
                    inverse = 1.0 / (total[at, :][:, :1] * shrink + add)
                    factors.append((shrink * inverse, inverse))
                else:
                    top[at, :] = jnp.broadcast_to(m, (32, 128))
                    total[at, :] = jnp.broadcast_to(add, (32, 128))
            got = jnp.dot(prob[g], k[:, :LAT], preferred_element_type=F32)
            if not last:
                accum[rows_at(t, g, 0, 256), :] = got
                continue
            score[g] = got
            for r in range(8):
                old, new = factors[r]
                ctx[g, r * 32:(r + 1) * 32, :] = (
                    accum[rows_at(t, g, r * 32, 32), :] * old + score[g, r * 32:(r + 1) * 32, :] * new
                ).astype(BF16)
            for n in range(4):
                head = 4 * g + n
                v = jnp.dot(ctx[g, n * HALF:(n + 1) * HALF, :], vu[head], preferred_element_type=F32)
                vals[t, lo, :, head * VAL:(head + 1) * VAL] = v.astype(BF16)

    @pl.loop(0, 2)
    def _(t):
        step(t, (c + 5) * TOKENS, 512, False)

        @pl.when(t == 0)
        def _():
            l_side_in(1, 0).wait_recv()
            l_side_in(1, 1).wait_recv()
            l_diag(1).start()
            for half in range(2):
                w_step_minus(3, half)
            for half in range(2):
                w_step_plus(2, half)

    loads[2].wait()
    l_core_in(2).wait_recv()
    l_diag_in(1).wait_recv()

    @pl.loop(0, 2)
    def _(t):
        step(t, (c + 1) * TOKENS, 0, True)
        v_out(t).start()

        @pl.when(t == 0)
        def _():
            for half in range(2):
                w_step_plus(3, half)

    for half in range(2):
        w_step_minus(4, half)
    for k in range(8):
        for half in range(2):
            w_core_in(k, half).wait_recv()

    def x_out(t, n, way, kind):
        terms, got, relay = ((terms_a, got_a, relay_a), (terms_b, got_b, relay_b))[n]
        xd = (x + 1 + 2 * way) % 4
        if kind == 0:
            src, dst = terms.at[t, way, (x + 2) % 4], relay.at[t, way]
        else:
            r = 1 - way if kind == 1 else way
            src, dst = terms.at[t, r, xd], got.at[t, way, r]
        sem = (t, n, way, kind)
        return remote(src, dst, xs.at[sem], xr.at[sem], {"head": hi * 4 + xd})

    def project(t, n):
        first, width = WIDE[n]
        terms = (terms_a, terms_b)[n]
        both = vals[t].reshape(TOKENS, HEADS * VAL)
        out = nt_dot(both, wt[first:first + 2 * width, :])
        for y in range(2):
            left = out[y * HALF:(y + 1) * HALF, :width].reshape(8, 8, width)
            right = out[y * HALF:(y + 1) * HALF, width:].reshape(8, 8, width)
            pair = jnp.concatenate([left, right], axis=1).astype(BF16)
            terms[t, :, :, y] = pair.reshape(2, 4, 16, width)
        for kind in range(2):
            for way in range(2):
                x_out(t, n, way, kind).start()

    def pass_on(t, n):
        terms, relay = ((terms_a, relay_a), (terms_b, relay_b))[n]
        for way in range(2):
            x_out(t, n, way, 0).wait_recv()
            xd = (x + 1 + 2 * way) % 4
            both = terms[t, way, xd].astype(F32) + relay[t, way].astype(F32)
            terms[t, way, xd] = both.astype(BF16)
            x_out(t, n, way, 2).start()

    def y_same(n, yd, src):
        part, fin = ((part_a, fin_a), (part_b, fin_b))[n]
        return remote(
            part.at[yd, lo], fin.at[0, src], yss.at[n, yd], ysr.at[n, src], {"head": yd * 4 + x}
        )

    def y_other(n, yd, src):
        part, fin = ((part_a, fin_a), (part_b, fin_b))[n]
        return remote(
            part.at[yd, 1 - lo], fin.at[1, src], yos.at[n, yd], yor.at[n, src],
            {"blk": side, "head": yd * 4 + x},
        )

    def combine(t, n):
        terms, got, part = ((terms_a, got_a, part_a), (terms_b, got_b, part_b))[n]
        for way in range(2):
            x_out(t, n, way, 1).wait_recv()
            x_out(t, n, way, 2).wait_recv()
        both = terms[t, :, x].astype(F32) + got[t, 0].astype(F32) + got[t, 1].astype(F32)
        part[2 * t:2 * t + 2] = both.astype(BF16)
        for yd in (2 * t, 2 * t + 1):
            y_other(n, yd, hi).start()

            @pl.when(hi != yd)
            def _():
                y_same(n, yd, hi).start()

    v_in(0).wait_recv()
    project(0, 0)
    project(0, 1)
    pass_on(0, 0)
    v_in(1).wait_recv()
    project(1, 0)
    pass_on(0, 1)
    project(1, 1)
    combine(0, 0)
    pass_on(1, 0)
    combine(0, 1)
    pass_on(1, 1)
    combine(1, 0)
    combine(1, 1)
    same_cols, other_cols = [], []
    for n in range(2):
        part, fin = ((part_a, fin_a), (part_b, fin_b))[n]
        same = part[hi, lo].astype(F32)
        other = jnp.zeros_like(same)
        for e in (1, 2, 3):
            src = (hi + e) % 4
            y_same(n, src, src).wait_recv()
            same = same + fin[0, src].astype(F32)
        for src in range(4):
            y_other(n, src, src).wait_recv()
            other = other + fin[1, src].astype(F32)
        same_cols += [same[:8], same[8:]]
        other_cols += [other[:8], other[8:]]
    same = jnp.concatenate(same_cols, axis=1)
    other = jnp.concatenate(other_cols, axis=1)
    by_y = (jnp.where(lo == 0, same, other), jnp.where(lo == 0, other, same))
    pair = 2 * COLS
    out[...] = jnp.concatenate(
        [by_y[i % 2][:, i // 2 * pair:(i // 2 + 1) * pair] for i in range(16)], axis=1
    ).astype(BF16)

    @pl.loop(1, 16)
    def _(i):
        own_rows(i).wait_send()

    for k in range(2):
        for half in range(2):
            l_up(k, half).wait_send()
            l_side(k, half).wait_send()
        l_diag(k).wait_send()
    for k in range(3):
        l_core(k).wait_send()
    for half in range(2):
        for k in range(3):
            w_plus(k, half).wait_send()
        for k in range(4):
            w_minus(k, half).wait_send()
        for k in range(8):
            w_core(k, half).wait_send()
    for t in range(2):
        v_out(t).wait_send()
    for n in range(2):
        for t in range(2):
            for way in range(2):
                for kind in range(3):
                    x_out(t, n, way, kind).wait_send()
        for yd in range(4):
            y_other(n, yd, hi).wait_send()
        for e in (1, 2, 3):
            y_same(n, (hi + e) % 4, hi).wait_send()


def shards(queries, latent, key_up_weight, value_up_weight, w_o, block_order):
    vmem = pl.BlockSpec(memory_space=pltpu.VMEM)
    anywhere = pl.BlockSpec(memory_space=pl.ANY)
    dma = pltpu.SemaphoreType.DMA
    rows = TOKENS * HEADS
    scratch = [
        pltpu.VMEM((HEADS, NOPE + ROT, TOKENS), BF16),
        pltpu.VMEM((HEADS, NOPE, LAT), BF16),
        pltpu.VMEM((HEADS, LAT, VAL), BF16),
        pltpu.VMEM((rows, WIDTH), BF16),
        pltpu.VMEM((TOKENS, SPAN * TOKENS), F32),
        pltpu.VMEM((16, 16, 384), BF16),
        pltpu.VMEM((12 * TOKENS, WIDTH), BF16),
        pltpu.VMEM((MINE, HEADS * VAL), BF16),
        pltpu.VMEM((2, 2, HALF, HEADS * VAL), BF16),
        pltpu.VMEM((rows, 128), F32),
        pltpu.VMEM((rows, 128), F32),
        pltpu.VMEM((rows, LAT), F32),
        pltpu.VMEM((2, 256, LAT), F32),
        pltpu.VMEM((2, 256, LAT), BF16),
        pltpu.VMEM((2, 256, LAT), BF16),
        pltpu.VMEM((2, 2, 4, 2, 16, 512), BF16),
        pltpu.VMEM((2, 2, 4, 2, 16, 384), BF16),
        pltpu.VMEM((2, 2, 2, 2, 16, 512), BF16),
        pltpu.VMEM((2, 2, 2, 2, 16, 384), BF16),
        pltpu.VMEM((2, 2, 2, 16, 512), BF16),
        pltpu.VMEM((2, 2, 2, 16, 384), BF16),
        pltpu.VMEM((4, 2, 16, 512), BF16),
        pltpu.VMEM((4, 2, 16, 384), BF16),
        pltpu.VMEM((2, 4, 16, 512), BF16),
        pltpu.VMEM((2, 4, 16, 384), BF16),
        dma((4,)),
        dma((16,)), dma((16,)),
        dma((2, 2)), dma((2, 2)),
        dma((3,)), dma((3,)),
        dma((2, 2)), dma((2, 2)),
        dma((2,)), dma((2,)),
        dma((3, 2)), dma((3, 2)),
        dma((4, 2)), dma((4, 2)),
        dma((8, 2)), dma((8, 2)),
        dma((2,)), dma((2,)),
        dma((2, 2, 2, 3)), dma((2, 2, 2, 3)),
        dma((2, 4)), dma((2, 4)),
        dma((2, 4)), dma((2, 4)),
    ]
    return pl.pallas_call(
        kernel,
        out_shape=jax.ShapeDtypeStruct((8, 2 * MINE), BF16),
        in_specs=[pl.BlockSpec(memory_space=pltpu.SMEM), vmem] + [anywhere] * 4,
        out_specs=vmem,
        scratch_shapes=scratch,
        compiler_params=pltpu.CompilerParams(
            collective_id=0, has_side_effects=True, vmem_limit_bytes=60 * 1024 * 1024
        ),
        cost_estimate=pl.CostEstimate(flops=3_500_000_000, bytes_accessed=3_000_000, transcendentals=1_048_576),
    )(block_order, latent, queries.transpose(1, 2, 0), key_up_weight, value_up_weight, w_o.T)


def solution(mesh):
    placed = (
        P("blk", "head", None),
        P(("blk", "head"), None),
        P("head", None, None),
        P("head", None, None),
        P("head", "blk"),
        P(),
    )
    return jax.shard_map(
        shards, mesh=mesh, in_specs=placed, out_specs=P(("blk", "head"), None), check_vma=False
    )
```

```python
import functools
import math

import jax
import jax.numpy as jnp
from jax import lax
from jax.experimental import pallas as pl
from jax.experimental.pallas import tpu as pltpu
from jax.sharding import PartitionSpec as P

NOPE = 128
ROT = 64
LAT = 512
WIDTH = LAT + ROT
VAL = 128
HEADS = 8
TOKENS = 128
HALF = 64
SPAN = 8
NBLK = 32
COLS = 112
MINE = 1792
WIDE = ((0, 512), (1024, 384))
BELOW = (0, 1, 3, 6)
ABOVE = (0, 2, 4, 5, 7)
OFFSET = (0, 7, 1, 6, 2, 3, 5, 4)
GAIN = (NOPE + ROT) ** (-0.5) * math.log2(math.e)
HIDDEN = -1e30
NT = (((1,), (1,)), ((), ()))
F32 = jnp.float32
BF16 = jnp.bfloat16


def nt_dot(a, b):
    return lax.dot_general(a, b, NT, preferred_element_type=F32)


def remote(src, dst, send, recv, device):
    return pltpu.make_async_remote_copy(
        src_ref=src, dst_ref=dst, send_sem=send, recv_sem=recv,
        device_id=device, device_id_type=pl.DeviceIdType.MESH,
    )


def kernel(
    order, latent, q_hbm, ku_hbm, vu_hbm, wo_hbm, out,
    q_raw, ku, vu, q_full, bias, pack, keys, wt, vals,
    top, total, accum, score, prob, ctx, terms_a, terms_b, got_a, got_b, relay_a, relay_b, part_a, part_b, fin_a, fin_b,
    load_sem, ps, pr, lzs, lzr, lcs, lcr, lys, lyr, lds, ldr,
    wps, wpr, wms, wmr, wcs, wcr, vs, vr, xs, xr, yss, ysr, yos, yor,
):
    b = lax.axis_index("blk")
    h = lax.axis_index("head")
    z, c = b // 4, b % 4
    lo, core = c // 2, c % 2
    hi, x = h // 4, h % 4
    up = (b + 4) % NBLK
    down = (b + NBLK - 4) % NBLK
    mate = b + 1 - 2 * core
    side = b + 2 - 4 * lo
    c_mate = c + 1 - 2 * core
    c_side = c + 2 - 4 * lo
    c_diag = c_side + 1 - 2 * core

    loads = [
        pltpu.make_async_copy(src, dst, load_sem.at[i])
        for i, (src, dst) in enumerate(((q_hbm, q_raw), (ku_hbm, ku), (vu_hbm, vu)))
    ]
    mine = wt.at[pl.ds(pl.multiple_of(core * COLS, 16), COLS)]
    loads.append(pltpu.make_async_copy(wo_hbm, mine, load_sem.at[3]))
    for load in loads[3:] + loads[:3]:
        load.start()

    rows = latent[...].astype(F32)
    second = jnp.concatenate([rows[:, 384:], jnp.zeros((8, 192), F32)], axis=1)
    pack[h] = jnp.concatenate([rows[:, :384], second], axis=0).astype(BF16)

    barrier = pltpu.get_barrier_semaphore()

    def greet(device):
        pl.semaphore_signal(barrier, inc=1, device_id=device, device_id_type=pl.DeviceIdType.MESH)

    @pl.loop(1, 16)
    def _(i):
        greet({"head": (h + i) % 16})

    @pl.loop(0, 4)
    def _(i):
        greet({"blk": side, "head": (hi + i) % 4 * 4 + x})

    greet({"blk": up})
    greet({"blk": down})
    greet({"blk": mate})
    pl.semaphore_wait(barrier, 22)

    def own_rows(i):
        return remote(pack.at[h], pack.at[h], ps.at[i], pr.at[i], {"head": (h + i) % 16})

    def shard(place, cc, half):
        first = (place * 2 + cc) * COLS + 64 * half
        return wt.at[pl.ds(pl.multiple_of(first, 16), (64, 48)[half])]

    def w_plus(k, half):
        src, dst = shard(BELOW[k], core, half), shard(BELOW[k + 1], core, half)
        return remote(src, dst, wps.at[k, half], wpr.at[k, half], {"blk": up})

    def w_minus(k, half):
        src, dst = shard(ABOVE[k], core, half), shard(ABOVE[k + 1], core, half)
        return remote(src, dst, wms.at[k, half], wmr.at[k, half], {"blk": down})

    def w_core(k, half):
        ref = shard(BELOW[k] if k < 4 else ABOVE[k - 3], core, half)
        return remote(ref, ref, wcs.at[k, half], wcr.at[k, half], {"blk": mate})

    def w_core_in(k, half):
        ref = shard(BELOW[k] if k < 4 else ABOVE[k - 3], 1 - core, half)
        return remote(ref, ref, wcs.at[k, half], wcr.at[k, half], {"blk": mate})

    def w_plus_in(k, half):
        ref = shard(BELOW[k + 1], core, half)
        return remote(ref, ref, wps.at[k, half], wpr.at[k, half], {"blk": up})

    def w_minus_in(k, half):
        ref = shard(ABOVE[k + 1], core, half)
        return remote(ref, ref, wms.at[k, half], wmr.at[k, half], {"blk": down})

    def w_step_plus(k, half):
        w_plus_in(k - 1, half).wait_recv()
        if k < 3:
            w_plus(k, half).start()
        w_core(k, half).start()

    def w_step_minus(k, half):
        w_minus_in(k - 1, half).wait_recv()
        if k < 4:
            w_minus(k, half).start()
        w_core(3 + k, half).start()

    loads[3].wait()
    for half in range(2):
        w_plus(0, half).start()
        w_minus(0, half).start()

    @pl.loop(1, 16)
    def _(i):
        own_rows(i).start()

    for half in range(2):
        w_core(0, half).start()

    loads[0].wait()
    loads[1].wait()
    for n in range(HEADS):
        lat = lax.dot_general(
            q_raw[n, :NOPE, :], ku[n], (((0,), (0,)), ((), ())), preferred_element_type=F32
        ).astype(BF16)
        turned = q_raw[n, NOPE:, :].astype(F32).T.astype(BF16)
        for t in range(2):
            at = slice(t * 512 + n * HALF, t * 512 + (n + 1) * HALF)
            q_full[at, :LAT] = lat[t * HALF:(t + 1) * HALF]
            q_full[at, LAT:] = turned[t * HALF:(t + 1) * HALF]

    row = lax.broadcasted_iota(jnp.int32, (TOKENS, TOKENS), 0)
    col = lax.broadcasted_iota(jnp.int32, (TOKENS, TOKENS), 1)
    q_pos = jnp.where(row < HALF, order[2 * b], order[2 * b + 1]) * HALF + row % HALF
    for n in range(SPAN):
        src = (b + NBLK - 7 + n) % NBLK
        k_pos = jnp.where(col < HALF, order[2 * src], order[2 * src + 1]) * HALF + col % HALF
        bias[:, n * TOKENS:(n + 1) * TOKENS] = jnp.where(k_pos <= q_pos, 0.0, HIDDEN)

    @pl.loop(1, 16)
    def _(i):
        ref = pack.at[(h + 16 - i) % 16]
        remote(ref, ref, ps.at[i], pr.at[i], {"head": (h + i) % 16}).wait_recv()

    def part_slot(plane, cc, half):
        first = (8 - 4 * plane + cc) * TOKENS + half * HALF
        return keys.at[pl.ds(pl.multiple_of(first, HALF), HALF)]

    def slot(plane, cc):
        return keys.at[pl.ds(pl.multiple_of((8 - 4 * plane + cc) * TOKENS, TOKENS), TOKENS)]

    gathered = pack[...].astype(F32)
    base = pl.multiple_of((8 + c) * TOKENS, TOKENS)
    keys[pl.ds(base, TOKENS), :384] = gathered[:, :8, :].reshape(TOKENS, 384).astype(BF16)
    keys[pl.ds(base, TOKENS), 384:] = gathered[:, 8:, :192].reshape(TOKENS, 192).astype(BF16)

    def l_up(k, half):
        src, dst = part_slot(k, c, half), part_slot(k + 1, c, half)
        return remote(src, dst, lzs.at[k, half], lzr.at[k, half], {"blk": up})

    def l_up_in(k, half):
        ref = part_slot(k + 1, c, half)
        return remote(ref, ref, lzs.at[k, half], lzr.at[k, half], {"blk": up})

    def l_core(p):
        return remote(slot(p, c), slot(p, c), lcs.at[p], lcr.at[p], {"blk": mate})

    def l_core_in(p):
        return remote(slot(p, c_mate), slot(p, c_mate), lcs.at[p], lcr.at[p], {"blk": mate})

    def l_side(j, half):
        ref = part_slot(j + lo, c, half)
        return remote(ref, ref, lys.at[j, half], lyr.at[j, half], {"blk": side})

    def l_side_in(j, half):
        ref = part_slot(j + 1 - lo, c_side, half)
        return remote(ref, ref, lys.at[j, half], lyr.at[j, half], {"blk": side})

    def l_diag(j):
        ref = slot(j + 1 - lo, c_side)
        return remote(ref, ref, lds.at[j], ldr.at[j], {"blk": mate})

    def l_diag_in(j):
        ref = slot(j + 1 - lo, c_diag)
        return remote(ref, ref, lds.at[j], ldr.at[j], {"blk": mate})

    l_up(0, 0).start()
    l_up(0, 1).start()

    @pl.when(lo == 0)
    def _():
        l_side(0, 0).start()
        l_side(0, 1).start()

    l_core(0).start()
    for half in range(2):
        w_step_minus(1, half)
    for half in range(2):
        l_up_in(0, half).wait_recv()
        l_up(1, half).start()
        l_side(1 - lo, half).start()

    l_core(1).start()
    w_step_minus(2, 0)
    for half in range(2):
        w_step_plus(1, half)
    w_step_minus(2, 1)
    l_side_in(0, 0).wait_recv()
    l_side_in(0, 1).wait_recv()
    l_diag(0).start()
    for half in range(2):
        l_up_in(1, half).wait_recv()

        @pl.when(lo == 1)
        def _():
            l_side(1, half).start()

    l_core(2).start()
    l_core_in(0).wait_recv()
    l_core_in(1).wait_recv()
    l_diag_in(0).wait_recv()

    def v_out(t):
        ref = vals.at[t, lo]
        return remote(ref, ref, vs.at[t], vr.at[t], {"blk": side})

    def v_in(t):
        ref = vals.at[t, 1 - lo]
        return remote(ref, ref, vs.at[t], vr.at[t], {"blk": side})

    def rows_at(t, g, first, count):
        return pl.ds(pl.multiple_of(t * 512 + g * 256 + first, 32), count)

    def step(t, start, first, last):
        k = keys[pl.ds(pl.multiple_of(start, TOKENS), 512), :]
        for g in range(2):
            score[g] = nt_dot(q_full[rows_at(t, g, 0, 256), :], k)
        for g in range(2):
            factors = []
            for r in range(8):
                at = rows_at(t, g, r * 32, 32)
                tok = pl.ds(pl.multiple_of(t * HALF + r % 2 * 32, 32), 32)
                sc = score[g, r * 32:(r + 1) * 32, :] + bias[tok, first:first + 512]
                m = jnp.max(sc, axis=1, keepdims=True)
                if last:
                    old = top[at, :][:, :1]
                    m = jnp.maximum(m, old)
                e = jnp.exp2((sc - m) * GAIN)
                add = jnp.sum(e, axis=1, keepdims=True)
                prob[g, r * 32:(r + 1) * 32, :] = e.astype(BF16)
                if last:
                    shrink = jnp.exp2((old - m) * GAIN)
                    inverse = 1.0 / (total[at, :][:, :1] * shrink + add)
                    factors.append((shrink * inverse, inverse))
                else:
                    top[at, :] = jnp.broadcast_to(m, (32, 128))
                    total[at, :] = jnp.broadcast_to(add, (32, 128))
            got = jnp.dot(prob[g], k[:, :LAT], preferred_element_type=F32)
            if not last:
                accum[rows_at(t, g, 0, 256), :] = got
                continue
            score[g] = got
            for r in range(8):
                old, new = factors[r]
                ctx[g, r * 32:(r + 1) * 32, :] = (
                    accum[rows_at(t, g, r * 32, 32), :] * old + score[g, r * 32:(r + 1) * 32, :] * new
                ).astype(BF16)
            for n in range(4):
                head = 4 * g + n
                v = jnp.dot(ctx[g, n * HALF:(n + 1) * HALF, :], vu[head], preferred_element_type=F32)
                vals[t, lo, :, head * VAL:(head + 1) * VAL] = v.astype(BF16)

    @pl.loop(0, 2)
    def _(t):
        step(t, (c + 5) * TOKENS, 512, False)

        @pl.when(t == 0)
        def _():
            l_side_in(1, 0).wait_recv()
            l_side_in(1, 1).wait_recv()
            l_diag(1).start()
            for half in range(2):
                w_step_minus(3, half)
            for half in range(2):
                w_step_plus(2, half)

    loads[2].wait()
    l_core_in(2).wait_recv()
    l_diag_in(1).wait_recv()

    @pl.loop(0, 2)
    def _(t):
        step(t, (c + 1) * TOKENS, 0, True)
        v_out(t).start()

    def x_out(t, n, way, kind):
        terms, got, relay = ((terms_a, got_a, relay_a), (terms_b, got_b, relay_b))[n]
        xd = (x + 1 + 2 * way) % 4
        if kind == 0:
            src, dst = terms.at[t, way, (x + 2) % 4], relay.at[t, way]
        else:
            r = 1 - way if kind == 1 else way
            src, dst = terms.at[t, r, xd], got.at[t, way, r]
        sem = (t, n, way, kind)
        return remote(src, dst, xs.at[sem], xr.at[sem], {"head": hi * 4 + xd})

    def project(t, n):
        first, width = WIDE[n]
        terms = (terms_a, terms_b)[n]
        both = vals[t].reshape(TOKENS, HEADS * VAL)
        out = nt_dot(both, wt[first:first + 2 * width, :])
        for y in range(2):
            left = out[y * HALF:(y + 1) * HALF, :width].reshape(8, 8, width)
            right = out[y * HALF:(y + 1) * HALF, width:].reshape(8, 8, width)
            pair = jnp.concatenate([left, right], axis=1).astype(BF16)
            terms[t, :, :, y] = pair.reshape(2, 4, 16, width)
        for kind in range(2):
            for way in range(2):
                x_out(t, n, way, kind).start()

    def pass_on(t, n):
        terms, relay = ((terms_a, relay_a), (terms_b, relay_b))[n]
        for way in range(2):
            x_out(t, n, way, 0).wait_recv()
            xd = (x + 1 + 2 * way) % 4
            both = terms[t, way, xd].astype(F32) + relay[t, way].astype(F32)
            terms[t, way, xd] = both.astype(BF16)
            x_out(t, n, way, 2).start()

    def y_same(n, yd, src):
        part, fin = ((part_a, fin_a), (part_b, fin_b))[n]
        return remote(
            part.at[yd, lo], fin.at[0, src], yss.at[n, yd], ysr.at[n, src], {"head": yd * 4 + x}
        )

    def y_other(n, yd, src):
        part, fin = ((part_a, fin_a), (part_b, fin_b))[n]
        return remote(
            part.at[yd, 1 - lo], fin.at[1, src], yos.at[n, yd], yor.at[n, src],
            {"blk": side, "head": yd * 4 + x},
        )

    def combine(t, n):
        terms, got, part = ((terms_a, got_a, part_a), (terms_b, got_b, part_b))[n]
        for way in range(2):
            x_out(t, n, way, 1).wait_recv()
            x_out(t, n, way, 2).wait_recv()
        both = terms[t, :, x].astype(F32) + got[t, 0].astype(F32) + got[t, 1].astype(F32)
        part[2 * t:2 * t + 2] = both.astype(BF16)
        for yd in (2 * t, 2 * t + 1):
            y_other(n, yd, hi).start()

            @pl.when(hi != yd)
            def _():
                y_same(n, yd, hi).start()

    def w_ready(ks):
        for k in ks:
            for half in range(2):
                w_core_in(k, half).wait_recv()

    w_ready((0, 1, 2, 4, 5))
    v_in(0).wait_recv()
    project(0, 0)
    for half in range(2):
        w_step_plus(3, half)
        w_step_minus(4, half)
    v_in(1).wait_recv()
    project(1, 0)
    pass_on(0, 0)
    w_ready((3, 6, 7))
    project(0, 1)
    pass_on(1, 0)
    project(1, 1)
    combine(0, 0)
    pass_on(0, 1)
    combine(1, 0)
    pass_on(1, 1)
    combine(0, 1)
    combine(1, 1)
    same_cols, other_cols = [], []
    for n in range(2):
        part, fin = ((part_a, fin_a), (part_b, fin_b))[n]
        same = part[hi, lo].astype(F32)
        other = jnp.zeros_like(same)
        for e in (1, 2, 3):
            src = (hi + e) % 4
            y_same(n, src, src).wait_recv()
            same = same + fin[0, src].astype(F32)
        for src in range(4):
            y_other(n, src, src).wait_recv()
            other = other + fin[1, src].astype(F32)
        same_cols += [same[:8], same[8:]]
        other_cols += [other[:8], other[8:]]
    same = jnp.concatenate(same_cols, axis=1)
    other = jnp.concatenate(other_cols, axis=1)
    by_y = (jnp.where(lo == 0, same, other), jnp.where(lo == 0, other, same))
    pair = 2 * COLS
    pieces = []
    for i in range(16):
        places = [by_y[i % 2][:, n * pair:(n + 1) * pair] for n in range(8)]
        piece = places[0]
        for n in range(1, 8):
            piece = jnp.where((z + OFFSET[n]) % 8 == i // 2, places[n], piece)
        pieces.append(piece)
    out[...] = jnp.concatenate(pieces, axis=1).astype(BF16)

    @pl.loop(1, 16)
    def _(i):
        own_rows(i).wait_send()

    for k in range(2):
        for half in range(2):
            l_up(k, half).wait_send()
            l_side(k, half).wait_send()
        l_diag(k).wait_send()
    for k in range(3):
        l_core(k).wait_send()
    for half in range(2):
        for k in range(3):
            w_plus(k, half).wait_send()
        for k in range(4):
            w_minus(k, half).wait_send()
        for k in range(8):
            w_core(k, half).wait_send()
    for t in range(2):
        v_out(t).wait_send()
    for n in range(2):
        for t in range(2):
            for way in range(2):
                for kind in range(3):
                    x_out(t, n, way, kind).wait_send()
        for yd in range(4):
            y_other(n, yd, hi).wait_send()
        for e in (1, 2, 3):
            y_same(n, (hi + e) % 4, hi).wait_send()


def shards(queries, latent, key_up_weight, value_up_weight, w_o, block_order):
    vmem = pl.BlockSpec(memory_space=pltpu.VMEM)
    anywhere = pl.BlockSpec(memory_space=pl.ANY)
    dma = pltpu.SemaphoreType.DMA
    rows = TOKENS * HEADS
    scratch = [
        pltpu.VMEM((HEADS, NOPE + ROT, TOKENS), BF16),
        pltpu.VMEM((HEADS, NOPE, LAT), BF16),
        pltpu.VMEM((HEADS, LAT, VAL), BF16),
        pltpu.VMEM((rows, WIDTH), BF16),
        pltpu.VMEM((TOKENS, SPAN * TOKENS), F32),
        pltpu.VMEM((16, 16, 384), BF16),
        pltpu.VMEM((12 * TOKENS, WIDTH), BF16),
        pltpu.VMEM((MINE, HEADS * VAL), BF16),
        pltpu.VMEM((2, 2, HALF, HEADS * VAL), BF16),
        pltpu.VMEM((rows, 128), F32),
        pltpu.VMEM((rows, 128), F32),
        pltpu.VMEM((rows, LAT), F32),
        pltpu.VMEM((2, 256, LAT), F32),
        pltpu.VMEM((2, 256, LAT), BF16),
        pltpu.VMEM((2, 256, LAT), BF16),
        pltpu.VMEM((2, 2, 4, 2, 16, 512), BF16),
        pltpu.VMEM((2, 2, 4, 2, 16, 384), BF16),
        pltpu.VMEM((2, 2, 2, 2, 16, 512), BF16),
        pltpu.VMEM((2, 2, 2, 2, 16, 384), BF16),
        pltpu.VMEM((2, 2, 2, 16, 512), BF16),
        pltpu.VMEM((2, 2, 2, 16, 384), BF16),
        pltpu.VMEM((4, 2, 16, 512), BF16),
        pltpu.VMEM((4, 2, 16, 384), BF16),
        pltpu.VMEM((2, 4, 16, 512), BF16),
        pltpu.VMEM((2, 4, 16, 384), BF16),
        dma((4,)),
        dma((16,)), dma((16,)),
        dma((2, 2)), dma((2, 2)),
        dma((3,)), dma((3,)),
        dma((2, 2)), dma((2, 2)),
        dma((2,)), dma((2,)),
        dma((3, 2)), dma((3, 2)),
        dma((4, 2)), dma((4, 2)),
        dma((8, 2)), dma((8, 2)),
        dma((2,)), dma((2,)),
        dma((2, 2, 2, 3)), dma((2, 2, 2, 3)),
        dma((2, 4)), dma((2, 4)),
        dma((2, 4)), dma((2, 4)),
    ]
    return pl.pallas_call(
        kernel,
        out_shape=jax.ShapeDtypeStruct((8, 2 * MINE), BF16),
        in_specs=[pl.BlockSpec(memory_space=pltpu.SMEM), vmem] + [anywhere] * 4,
        out_specs=vmem,
        scratch_shapes=scratch,
        compiler_params=pltpu.CompilerParams(
            collective_id=0, has_side_effects=True, vmem_limit_bytes=60 * 1024 * 1024
        ),
        cost_estimate=pl.CostEstimate(flops=3_500_000_000, bytes_accessed=3_000_000, transcendentals=1_048_576),
    )(block_order, latent, queries.transpose(1, 2, 0), key_up_weight, value_up_weight, w_o.T)


def solution(mesh):
    placed = (
        P("blk", "head", None),
        P(("blk", "head"), None),
        P("head", None, None),
        P("head", None, None),
        P("head", "blk"),
        P(),
    )
    return jax.shard_map(
        shards, mesh=mesh, in_specs=placed, out_specs=P(("blk", "head"), None), check_vma=False
    )
```

```python
import functools
import math

import jax
import jax.numpy as jnp
from jax import lax
from jax.experimental import pallas as pl
from jax.experimental.pallas import tpu as pltpu
from jax.sharding import PartitionSpec as P

NOPE = 128
ROT = 64
LAT = 512
WIDTH = LAT + ROT
VAL = 128
HEADS = 8
TOKENS = 128
HALF = 64
SPAN = 8
NBLK = 32
COLS = 112
MINE = 1792
WIDE = ((0, 512), (1024, 384))
GAIN = (NOPE + ROT) ** (-0.5) * math.log2(math.e)
HIDDEN = -1e30
NT = (((1,), (1,)), ((), ()))
F32 = jnp.float32
BF16 = jnp.bfloat16


def nt_dot(a, b):
    return lax.dot_general(a, b, NT, preferred_element_type=F32)


def remote(src, dst, send, recv, device):
    return pltpu.make_async_remote_copy(
        src_ref=src, dst_ref=dst, send_sem=send, recv_sem=recv,
        device_id=device, device_id_type=pl.DeviceIdType.MESH,
    )


def kernel(
    order_hbm, latent_hbm, q_hbm, ku_hbm, vu_hbm, wo_hbm, out,
    order, latent, q_raw, ku, vu, q_full, bias, pack, keys, wt, vals,
    top, total, accum, score, prob, ctx, terms_a, terms_b, got_a, got_b, relay_a, relay_b, part_a, part_b, fin_a, fin_b,
    load_sem, ps, pr, lzs, lzr, lcs, lcr, lys, lyr, lds, ldr,
    wps, wpr, wms, wmr, wcs, wcr, vs, vr, xs, xr, yss, ysr, yos, yor,
):
    b = lax.axis_index("blk")
    h = lax.axis_index("head")
    z, c = b // 4, b % 4
    lo, core = c // 2, c % 2
    hi, x = h // 4, h % 4
    up = (b + 4) % NBLK
    down = (b + NBLK - 4) % NBLK
    mate = b + 1 - 2 * core
    side = b + 2 - 4 * lo
    c_mate = c + 1 - 2 * core
    c_side = c + 2 - 4 * lo
    c_diag = c_side + 1 - 2 * core

    loads = [
        pltpu.make_async_copy(src, dst, load_sem.at[i])
        for i, (src, dst) in enumerate(((q_hbm, q_raw), (ku_hbm, ku), (vu_hbm, vu)))
    ]
    mine = wt.at[pl.ds(pl.multiple_of((z * 2 + core) * COLS, 16), COLS)]
    loads.append(pltpu.make_async_copy(wo_hbm, mine, load_sem.at[3]))
    loads.append(pltpu.make_async_copy(latent_hbm, latent, load_sem.at[4]))
    loads.append(pltpu.make_async_copy(order_hbm, order, load_sem.at[5]))
    loads[4].start()

    barrier = pltpu.get_barrier_semaphore()

    def greet(device):
        pl.semaphore_signal(barrier, inc=1, device_id=device, device_id_type=pl.DeviceIdType.MESH)

    @pl.loop(1, 16)
    def _(i):
        greet({"head": (h + i) % 16})

    @pl.loop(0, 4)
    def _(i):
        greet({"blk": side, "head": (hi + i) % 4 * 4 + x})

    greet({"blk": up})
    greet({"blk": down})
    greet({"blk": mate})
    for load in loads[3:4] + loads[:3] + loads[5:]:
        load.start()
    loads[4].wait()
    rows = latent[...].astype(F32)
    second = jnp.concatenate([rows[:, 384:], jnp.zeros((8, 192), F32)], axis=1)
    pack[h] = jnp.concatenate([rows[:, :384], second], axis=0).astype(BF16)
    pl.semaphore_wait(barrier, 22)

    def own_rows(i):
        return remote(pack.at[h], pack.at[h], ps.at[i], pr.at[i], {"head": (h + i) % 16})

    @pl.loop(1, 16)
    def _(i):
        own_rows(i).start()

    def shard(zz, cc, half):
        first = (zz * 2 + cc) * COLS + 64 * half
        return wt.at[pl.ds(pl.multiple_of(first, 16), (64, 48)[half])]

    def w_plus(k, half):
        ref = shard((z + 8 - k) % 8, core, half)
        return remote(ref, ref, wps.at[k, half], wpr.at[k, half], {"blk": up})

    def w_minus(k, half):
        ref = shard((z + k) % 8, core, half)
        return remote(ref, ref, wms.at[k, half], wmr.at[k, half], {"blk": down})

    def w_core(k, half):
        zz = (z + 8 - k) % 8 if k < 4 else (z + k - 3) % 8
        ref = shard(zz, core, half)
        return remote(ref, ref, wcs.at[k, half], wcr.at[k, half], {"blk": mate})

    def w_core_in(k, half):
        zz = (z + 8 - k) % 8 if k < 4 else (z + k - 3) % 8
        ref = shard(zz, 1 - core, half)
        return remote(ref, ref, wcs.at[k, half], wcr.at[k, half], {"blk": mate})

    def w_plus_in(k, half):
        ref = shard((z + 7 - k) % 8, core, half)
        return remote(ref, ref, wps.at[k, half], wpr.at[k, half], {"blk": up})

    def w_minus_in(k, half):
        ref = shard((z + 1 + k) % 8, core, half)
        return remote(ref, ref, wms.at[k, half], wmr.at[k, half], {"blk": down})

    def w_step_plus(k, half):
        w_plus_in(k - 1, half).wait_recv()
        if k < 3:
            w_plus(k, half).start()
        w_core(k, half).start()

    def w_step_minus(k, half):
        w_minus_in(k - 1, half).wait_recv()
        if k < 4:
            w_minus(k, half).start()
        w_core(3 + k, half).start()

    loads[3].wait()
    for half in range(2):
        w_plus(0, half).start()
        w_minus(0, half).start()

    for half in range(2):
        w_core(0, half).start()

    loads[0].wait()
    loads[1].wait()
    for n in range(HEADS):
        lat = lax.dot_general(
            q_raw[n, :NOPE, :], ku[n], (((0,), (0,)), ((), ())), preferred_element_type=F32
        ).astype(BF16)
        turned = q_raw[n, NOPE:, :].astype(F32).T.astype(BF16)
        for t in range(2):
            at = slice(t * 512 + n * HALF, t * 512 + (n + 1) * HALF)
            q_full[at, :LAT] = lat[t * HALF:(t + 1) * HALF]
            q_full[at, LAT:] = turned[t * HALF:(t + 1) * HALF]

    loads[5].wait()
    row = lax.broadcasted_iota(jnp.int32, (TOKENS, TOKENS), 0)
    col = lax.broadcasted_iota(jnp.int32, (TOKENS, TOKENS), 1)
    q_pos = jnp.where(row < HALF, order[2 * b], order[2 * b + 1]) * HALF + row % HALF
    for n in range(SPAN):
        src = (b + NBLK - 7 + n) % NBLK
        k_pos = jnp.where(col < HALF, order[2 * src], order[2 * src + 1]) * HALF + col % HALF
        bias[:, n * TOKENS:(n + 1) * TOKENS] = jnp.where(k_pos <= q_pos, 0.0, HIDDEN)

    @pl.loop(1, 16)
    def _(i):
        ref = pack.at[(h + 16 - i) % 16]
        remote(ref, ref, ps.at[i], pr.at[i], {"head": (h + i) % 16}).wait_recv()

    def part_slot(plane, cc, half):
        first = (8 - 4 * plane + cc) * TOKENS + half * HALF
        return keys.at[pl.ds(pl.multiple_of(first, HALF), HALF)]

    def slot(plane, cc):
        return keys.at[pl.ds(pl.multiple_of((8 - 4 * plane + cc) * TOKENS, TOKENS), TOKENS)]

    gathered = pack[...].astype(F32)
    base = pl.multiple_of((8 + c) * TOKENS, TOKENS)
    keys[pl.ds(base, TOKENS), :384] = gathered[:, :8, :].reshape(TOKENS, 384).astype(BF16)
    keys[pl.ds(base, TOKENS), 384:] = gathered[:, 8:, :192].reshape(TOKENS, 192).astype(BF16)

    def l_up(k, half):
        src, dst = part_slot(k, c, half), part_slot(k + 1, c, half)
        return remote(src, dst, lzs.at[k, half], lzr.at[k, half], {"blk": up})

    def l_up_in(k, half):
        ref = part_slot(k + 1, c, half)
        return remote(ref, ref, lzs.at[k, half], lzr.at[k, half], {"blk": up})

    def l_core(p):
        return remote(slot(p, c), slot(p, c), lcs.at[p], lcr.at[p], {"blk": mate})

    def l_core_in(p):
        return remote(slot(p, c_mate), slot(p, c_mate), lcs.at[p], lcr.at[p], {"blk": mate})

    def l_side(j, half):
        ref = part_slot(j + lo, c, half)
        return remote(ref, ref, lys.at[j, half], lyr.at[j, half], {"blk": side})

    def l_side_in(j, half):
        ref = part_slot(j + 1 - lo, c_side, half)
        return remote(ref, ref, lys.at[j, half], lyr.at[j, half], {"blk": side})

    def l_diag(j):
        ref = slot(j + 1 - lo, c_side)
        return remote(ref, ref, lds.at[j], ldr.at[j], {"blk": mate})

    def l_diag_in(j):
        ref = slot(j + 1 - lo, c_diag)
        return remote(ref, ref, lds.at[j], ldr.at[j], {"blk": mate})

    l_up(0, 0).start()
    l_up(0, 1).start()

    @pl.when(lo == 0)
    def _():
        l_side(0, 0).start()
        l_side(0, 1).start()

    l_core(0).start()
    for half in range(2):
        w_step_minus(1, half)
    for half in range(2):
        l_up_in(0, half).wait_recv()
        l_up(1, half).start()
        l_side(1 - lo, half).start()

    l_core(1).start()
    w_step_minus(2, 0)
    for half in range(2):
        w_step_plus(1, half)
    w_step_minus(2, 1)
    l_side_in(0, 0).wait_recv()
    l_side_in(0, 1).wait_recv()
    l_diag(0).start()
    for half in range(2):
        l_up_in(1, half).wait_recv()

        @pl.when(lo == 1)
        def _():
            l_side(1, half).start()

    l_core(2).start()
    l_core_in(0).wait_recv()
    l_core_in(1).wait_recv()
    l_diag_in(0).wait_recv()

    def v_out(t):
        ref = vals.at[t, lo]
        return remote(ref, ref, vs.at[t], vr.at[t], {"blk": side})

    def v_in(t):
        ref = vals.at[t, 1 - lo]
        return remote(ref, ref, vs.at[t], vr.at[t], {"blk": side})

    def rows_at(t, g, first, count):
        return pl.ds(pl.multiple_of(t * 512 + g * 256 + first, 32), count)

    def step(t, start, first, last):
        k = keys[pl.ds(pl.multiple_of(start, TOKENS), 512), :]
        for g in range(2):
            score[g] = nt_dot(q_full[rows_at(t, g, 0, 256), :], k)
        for g in range(2):
            factors = []
            for r in range(8):
                at = rows_at(t, g, r * 32, 32)
                tok = pl.ds(pl.multiple_of(t * HALF + r % 2 * 32, 32), 32)
                sc = score[g, r * 32:(r + 1) * 32, :] + bias[tok, first:first + 512]
                m = jnp.max(sc, axis=1, keepdims=True)
                if last:
                    old = top[at, :][:, :1]
                    m = jnp.maximum(m, old)
                e = jnp.exp2((sc - m) * GAIN)
                add = jnp.sum(e, axis=1, keepdims=True)
                prob[g, r * 32:(r + 1) * 32, :] = e.astype(BF16)
                if last:
                    shrink = jnp.exp2((old - m) * GAIN)
                    inverse = 1.0 / (total[at, :][:, :1] * shrink + add)
                    factors.append((shrink * inverse, inverse))
                else:
                    top[at, :] = jnp.broadcast_to(m, (32, 128))
                    total[at, :] = jnp.broadcast_to(add, (32, 128))
            got = jnp.dot(prob[g], k[:, :LAT], preferred_element_type=F32)
            if not last:
                accum[rows_at(t, g, 0, 256), :] = got
                continue
            score[g] = got
            for r in range(8):
                old, new = factors[r]
                ctx[g, r * 32:(r + 1) * 32, :] = (
                    accum[rows_at(t, g, r * 32, 32), :] * old + score[g, r * 32:(r + 1) * 32, :] * new
                ).astype(BF16)
            for n in range(4):
                head = 4 * g + n
                v = jnp.dot(ctx[g, n * HALF:(n + 1) * HALF, :], vu[head], preferred_element_type=F32)
                vals[t, lo, :, head * VAL:(head + 1) * VAL] = v.astype(BF16)

    @pl.loop(0, 2)
    def _(t):
        step(t, (c + 5) * TOKENS, 512, False)

        @pl.when(t == 0)
        def _():
            l_side_in(1, 0).wait_recv()
            l_side_in(1, 1).wait_recv()
            l_diag(1).start()
            for half in range(2):
                w_step_minus(3, half)
            for half in range(2):
                w_step_plus(2, half)

    loads[2].wait()
    l_core_in(2).wait_recv()
    l_diag_in(1).wait_recv()

    @pl.loop(0, 2)
    def _(t):
        step(t, (c + 1) * TOKENS, 0, True)
        v_out(t).start()

        @pl.when(t == 0)
        def _():
            for half in range(2):
                w_step_plus(3, half)

    for half in range(2):
        w_step_minus(4, half)
    for k in range(8):
        for half in range(2):
            w_core_in(k, half).wait_recv()

    def x_out(t, n, way, kind):
        terms, got, relay = ((terms_a, got_a, relay_a), (terms_b, got_b, relay_b))[n]
        xd = (x + 1 + 2 * way) % 4
        if kind == 0:
            src, dst = terms.at[t, way, (x + 2) % 4], relay.at[t, way]
        else:
            r = 1 - way if kind == 1 else way
            src, dst = terms.at[t, r, xd], got.at[t, way, r]
        sem = (t, n, way, kind)
        return remote(src, dst, xs.at[sem], xr.at[sem], {"head": hi * 4 + xd})

    def project(t, n):
        first, width = WIDE[n]
        terms = (terms_a, terms_b)[n]
        both = vals[t].reshape(TOKENS, HEADS * VAL)
        out = nt_dot(both, wt[first:first + 2 * width, :])
        for y in range(2):
            left = out[y * HALF:(y + 1) * HALF, :width].reshape(8, 8, width)
            right = out[y * HALF:(y + 1) * HALF, width:].reshape(8, 8, width)
            pair = jnp.concatenate([left, right], axis=1).astype(BF16)
            terms[t, :, :, y] = pair.reshape(2, 4, 16, width)
        for kind in range(2):
            for way in range(2):
                x_out(t, n, way, kind).start()

    def pass_on(t, n):
        terms, relay = ((terms_a, relay_a), (terms_b, relay_b))[n]
        for way in range(2):
            x_out(t, n, way, 0).wait_recv()
            xd = (x + 1 + 2 * way) % 4
            both = terms[t, way, xd].astype(F32) + relay[t, way].astype(F32)
            terms[t, way, xd] = both.astype(BF16)
            x_out(t, n, way, 2).start()

    def y_same(n, yd, src):
        part, fin = ((part_a, fin_a), (part_b, fin_b))[n]
        return remote(
            part.at[yd, lo], fin.at[0, src], yss.at[n, yd], ysr.at[n, src], {"head": yd * 4 + x}
        )

    def y_other(n, yd, src):
        part, fin = ((part_a, fin_a), (part_b, fin_b))[n]
        return remote(
            part.at[yd, 1 - lo], fin.at[1, src], yos.at[n, yd], yor.at[n, src],
            {"blk": side, "head": yd * 4 + x},
        )

    def combine(t, n):
        terms, got, part = ((terms_a, got_a, part_a), (terms_b, got_b, part_b))[n]
        for way in range(2):
            x_out(t, n, way, 1).wait_recv()
            x_out(t, n, way, 2).wait_recv()
        both = terms[t, :, x].astype(F32) + got[t, 0].astype(F32) + got[t, 1].astype(F32)
        part[2 * t:2 * t + 2] = both.astype(BF16)
        for yd in (2 * t, 2 * t + 1):
            y_other(n, yd, hi).start()

            @pl.when(hi != yd)
            def _():
                y_same(n, yd, hi).start()

    v_in(0).wait_recv()
    project(0, 0)
    project(0, 1)
    pass_on(0, 0)
    v_in(1).wait_recv()
    project(1, 0)
    pass_on(0, 1)
    project(1, 1)
    combine(0, 0)
    pass_on(1, 0)
    combine(0, 1)
    pass_on(1, 1)
    combine(1, 0)
    combine(1, 1)
    same_cols, other_cols = [], []
    for n in range(2):
        part, fin = ((part_a, fin_a), (part_b, fin_b))[n]
        same = part[hi, lo].astype(F32)
        other = jnp.zeros_like(same)
        for e in (1, 2, 3):
            src = (hi + e) % 4
            y_same(n, src, src).wait_recv()
            same = same + fin[0, src].astype(F32)
        for src in range(4):
            y_other(n, src, src).wait_recv()
            other = other + fin[1, src].astype(F32)
        same_cols += [same[:8], same[8:]]
        other_cols += [other[:8], other[8:]]
    same = jnp.concatenate(same_cols, axis=1)
    other = jnp.concatenate(other_cols, axis=1)
    by_y = (jnp.where(lo == 0, same, other), jnp.where(lo == 0, other, same))
    pair = 2 * COLS
    out[...] = jnp.concatenate(
        [by_y[i % 2][:, i // 2 * pair:(i // 2 + 1) * pair] for i in range(16)], axis=1
    ).astype(BF16)

    @pl.loop(1, 16)
    def _(i):
        own_rows(i).wait_send()

    for k in range(2):
        for half in range(2):
            l_up(k, half).wait_send()
            l_side(k, half).wait_send()
        l_diag(k).wait_send()
    for k in range(3):
        l_core(k).wait_send()
    for half in range(2):
        for k in range(3):
            w_plus(k, half).wait_send()
        for k in range(4):
            w_minus(k, half).wait_send()
        for k in range(8):
            w_core(k, half).wait_send()
    for t in range(2):
        v_out(t).wait_send()
    for n in range(2):
        for t in range(2):
            for way in range(2):
                for kind in range(3):
                    x_out(t, n, way, kind).wait_send()
        for yd in range(4):
            y_other(n, yd, hi).wait_send()
        for e in (1, 2, 3):
            y_same(n, (hi + e) % 4, hi).wait_send()


def shards(queries, latent, key_up_weight, value_up_weight, w_o, block_order):
    vmem = pl.BlockSpec(memory_space=pltpu.VMEM)
    anywhere = pl.BlockSpec(memory_space=pl.ANY)
    dma = pltpu.SemaphoreType.DMA
    rows = TOKENS * HEADS
    scratch = [
        pltpu.SMEM((64,), jnp.int32),
        pltpu.VMEM((8, WIDTH), BF16),
        pltpu.VMEM((HEADS, NOPE + ROT, TOKENS), BF16),
        pltpu.VMEM((HEADS, NOPE, LAT), BF16),
        pltpu.VMEM((HEADS, LAT, VAL), BF16),
        pltpu.VMEM((rows, WIDTH), BF16),
        pltpu.VMEM((TOKENS, SPAN * TOKENS), F32),
        pltpu.VMEM((16, 16, 384), BF16),
        pltpu.VMEM((12 * TOKENS, WIDTH), BF16),
        pltpu.VMEM((MINE, HEADS * VAL), BF16),
        pltpu.VMEM((2, 2, HALF, HEADS * VAL), BF16),
        pltpu.VMEM((rows, 128), F32),
        pltpu.VMEM((rows, 128), F32),
        pltpu.VMEM((rows, LAT), F32),
        pltpu.VMEM((2, 256, LAT), F32),
        pltpu.VMEM((2, 256, LAT), BF16),
        pltpu.VMEM((2, 256, LAT), BF16),
        pltpu.VMEM((2, 2, 4, 2, 16, 512), BF16),
        pltpu.VMEM((2, 2, 4, 2, 16, 384), BF16),
        pltpu.VMEM((2, 2, 2, 2, 16, 512), BF16),
        pltpu.VMEM((2, 2, 2, 2, 16, 384), BF16),
        pltpu.VMEM((2, 2, 2, 16, 512), BF16),
        pltpu.VMEM((2, 2, 2, 16, 384), BF16),
        pltpu.VMEM((4, 2, 16, 512), BF16),
        pltpu.VMEM((4, 2, 16, 384), BF16),
        pltpu.VMEM((2, 4, 16, 512), BF16),
        pltpu.VMEM((2, 4, 16, 384), BF16),
        dma((6,)),
        dma((16,)), dma((16,)),
        dma((2, 2)), dma((2, 2)),
        dma((3,)), dma((3,)),
        dma((2, 2)), dma((2, 2)),
        dma((2,)), dma((2,)),
        dma((3, 2)), dma((3, 2)),
        dma((4, 2)), dma((4, 2)),
        dma((8, 2)), dma((8, 2)),
        dma((2,)), dma((2,)),
        dma((2, 2, 2, 3)), dma((2, 2, 2, 3)),
        dma((2, 4)), dma((2, 4)),
        dma((2, 4)), dma((2, 4)),
    ]
    return pl.pallas_call(
        kernel,
        out_shape=jax.ShapeDtypeStruct((8, 2 * MINE), BF16),
        in_specs=[anywhere] * 6,
        out_specs=vmem,
        scratch_shapes=scratch,
        compiler_params=pltpu.CompilerParams(
            collective_id=0, has_side_effects=True, vmem_limit_bytes=60 * 1024 * 1024
        ),
        cost_estimate=pl.CostEstimate(flops=3_500_000_000, bytes_accessed=3_000_000, transcendentals=1_048_576),
    )(block_order, latent, queries.transpose(1, 2, 0), key_up_weight, value_up_weight, w_o.T)


def solution(mesh):
    placed = (
        P("blk", "head", None),
        P(("blk", "head"), None),
        P("head", None, None),
        P("head", None, None),
        P("head", "blk"),
        P(),
    )
    return jax.shard_map(
        shards, mesh=mesh, in_specs=placed, out_specs=P(("blk", "head"), None), check_vma=False
    )
```

```python
import functools
import math

import jax
import jax.numpy as jnp
from jax import lax
from jax.experimental import pallas as pl
from jax.experimental.pallas import tpu as pltpu
from jax.sharding import PartitionSpec as P

NOPE = 128
ROT = 64
LAT = 512
WIDTH = LAT + ROT
VAL = 128
HEADS = 8
TOKENS = 128
HALF = 64
SPAN = 8
NBLK = 32
COLS = 112
MINE = 1792
WIDE = ((0, 512), (1024, 384))
GAIN = (NOPE + ROT) ** (-0.5) * math.log2(math.e)
HIDDEN = -1e30
NT = (((1,), (1,)), ((), ()))
F32 = jnp.float32
BF16 = jnp.bfloat16


def nt_dot(a, b):
    return lax.dot_general(a, b, NT, preferred_element_type=F32)


def remote(src, dst, send, recv, device):
    return pltpu.make_async_remote_copy(
        src_ref=src, dst_ref=dst, send_sem=send, recv_sem=recv,
        device_id=device, device_id_type=pl.DeviceIdType.MESH,
    )


def kernel(
    order_hbm, latent_hbm, q_hbm, ku_hbm, vu_hbm, wo_hbm, out,
    order, latent, q_raw, ku, vu, q_full, bias, pack, keys, wt, vals,
    top, total, accum, score, prob, ctx, terms_a, terms_b, got_a, got_b, part_a, part_b, fin_a, fin_b,
    load_sem, ps, pr, lzs, lzr, lcs, lcr, lys, lyr, lds, ldr,
    wps, wpr, wms, wmr, wcs, wcr, vs, vr, xs, xr, yss, ysr, yos, yor,
):
    b = lax.axis_index("blk")
    h = lax.axis_index("head")
    z, c = b // 4, b % 4
    lo, core = c // 2, c % 2
    hi, x = h // 4, h % 4
    up = (b + 4) % NBLK
    down = (b + NBLK - 4) % NBLK
    mate = b + 1 - 2 * core
    side = b + 2 - 4 * lo
    c_mate = c + 1 - 2 * core
    c_side = c + 2 - 4 * lo
    c_diag = c_side + 1 - 2 * core

    loads = [
        pltpu.make_async_copy(src, dst, load_sem.at[i])
        for i, (src, dst) in enumerate(((q_hbm, q_raw), (ku_hbm, ku), (vu_hbm, vu)))
    ]
    mine = wt.at[pl.ds(pl.multiple_of((z * 2 + core) * COLS, 16), COLS)]
    loads.append(pltpu.make_async_copy(wo_hbm, mine, load_sem.at[3]))
    loads.append(pltpu.make_async_copy(latent_hbm, latent, load_sem.at[4]))
    loads.append(pltpu.make_async_copy(order_hbm, order, load_sem.at[5]))
    loads[4].start()

    barrier = pltpu.get_barrier_semaphore()

    def greet(device):
        pl.semaphore_signal(barrier, inc=1, device_id=device, device_id_type=pl.DeviceIdType.MESH)

    @pl.loop(1, 16)
    def _(i):
        greet({"head": (h + i) % 16})

    @pl.loop(0, 4)
    def _(i):
        greet({"blk": side, "head": (hi + i) % 4 * 4 + x})

    greet({"blk": up})
    greet({"blk": down})
    greet({"blk": mate})
    for load in loads[3:4] + loads[:3] + loads[5:]:
        load.start()
    loads[4].wait()
    rows = latent[...].astype(F32)
    second = jnp.concatenate([rows[:, 384:], jnp.zeros((8, 192), F32)], axis=1)
    pack[h] = jnp.concatenate([rows[:, :384], second], axis=0).astype(BF16)
    pl.semaphore_wait(barrier, 22)

    def own_rows(i):
        return remote(pack.at[h], pack.at[h], ps.at[i], pr.at[i], {"head": (h + i) % 16})

    @pl.loop(1, 16)
    def _(i):
        own_rows(i).start()

    def shard(zz, cc, half):
        first = (zz * 2 + cc) * COLS + 64 * half
        return wt.at[pl.ds(pl.multiple_of(first, 16), (64, 48)[half])]

    def w_plus(k, half):
        ref = shard((z + 8 - k) % 8, core, half)
        return remote(ref, ref, wps.at[k, half], wpr.at[k, half], {"blk": up})

    def w_minus(k, half):
        ref = shard((z + k) % 8, core, half)
        return remote(ref, ref, wms.at[k, half], wmr.at[k, half], {"blk": down})

    def w_core(k, half):
        zz = (z + 8 - k) % 8 if k < 4 else (z + k - 3) % 8
        ref = shard(zz, core, half)
        return remote(ref, ref, wcs.at[k, half], wcr.at[k, half], {"blk": mate})

    def w_core_in(k, half):
        zz = (z + 8 - k) % 8 if k < 4 else (z + k - 3) % 8
        ref = shard(zz, 1 - core, half)
        return remote(ref, ref, wcs.at[k, half], wcr.at[k, half], {"blk": mate})

    def w_plus_in(k, half):
        ref = shard((z + 7 - k) % 8, core, half)
        return remote(ref, ref, wps.at[k, half], wpr.at[k, half], {"blk": up})

    def w_minus_in(k, half):
        ref = shard((z + 1 + k) % 8, core, half)
        return remote(ref, ref, wms.at[k, half], wmr.at[k, half], {"blk": down})

    def w_step_plus(k, half):
        w_plus_in(k - 1, half).wait_recv()
        if k < 3:
            w_plus(k, half).start()
        w_core(k, half).start()

    def w_step_minus(k, half):
        w_minus_in(k - 1, half).wait_recv()
        if k < 4:
            w_minus(k, half).start()
        w_core(3 + k, half).start()

    loads[3].wait()
    for half in range(2):
        w_plus(0, half).start()
        w_minus(0, half).start()

    for half in range(2):
        w_core(0, half).start()

    loads[0].wait()
    loads[1].wait()
    for n in range(HEADS):
        lat = lax.dot_general(
            q_raw[n, :NOPE, :], ku[n], (((0,), (0,)), ((), ())), preferred_element_type=F32
        ).astype(BF16)
        turned = q_raw[n, NOPE:, :].astype(F32).T.astype(BF16)
        for t in range(2):
            at = slice(t * 512 + n * HALF, t * 512 + (n + 1) * HALF)
            q_full[at, :LAT] = lat[t * HALF:(t + 1) * HALF]
            q_full[at, LAT:] = turned[t * HALF:(t + 1) * HALF]

    loads[5].wait()
    row = lax.broadcasted_iota(jnp.int32, (TOKENS, TOKENS), 0)
    col = lax.broadcasted_iota(jnp.int32, (TOKENS, TOKENS), 1)
    q_pos = jnp.where(row < HALF, order[2 * b], order[2 * b + 1]) * HALF + row % HALF
    for n in range(SPAN):
        src = (b + NBLK - 7 + n) % NBLK
        k_pos = jnp.where(col < HALF, order[2 * src], order[2 * src + 1]) * HALF + col % HALF
        bias[:, n * TOKENS:(n + 1) * TOKENS] = jnp.where(k_pos <= q_pos, 0.0, HIDDEN)

    @pl.loop(1, 16)
    def _(i):
        ref = pack.at[(h + 16 - i) % 16]
        remote(ref, ref, ps.at[i], pr.at[i], {"head": (h + i) % 16}).wait_recv()

    def part_slot(plane, cc, half):
        first = (8 - 4 * plane + cc) * TOKENS + half * HALF
        return keys.at[pl.ds(pl.multiple_of(first, HALF), HALF)]

    def slot(plane, cc):
        return keys.at[pl.ds(pl.multiple_of((8 - 4 * plane + cc) * TOKENS, TOKENS), TOKENS)]

    gathered = pack[...].astype(F32)
    base = pl.multiple_of((8 + c) * TOKENS, TOKENS)
    keys[pl.ds(base, TOKENS), :384] = gathered[:, :8, :].reshape(TOKENS, 384).astype(BF16)
    keys[pl.ds(base, TOKENS), 384:] = gathered[:, 8:, :192].reshape(TOKENS, 192).astype(BF16)

    def l_up(k, half):
        src, dst = part_slot(k, c, half), part_slot(k + 1, c, half)
        return remote(src, dst, lzs.at[k, half], lzr.at[k, half], {"blk": up})

    def l_up_in(k, half):
        ref = part_slot(k + 1, c, half)
        return remote(ref, ref, lzs.at[k, half], lzr.at[k, half], {"blk": up})

    def l_core(p):
        return remote(slot(p, c), slot(p, c), lcs.at[p], lcr.at[p], {"blk": mate})

    def l_core_in(p):
        return remote(slot(p, c_mate), slot(p, c_mate), lcs.at[p], lcr.at[p], {"blk": mate})

    def l_side(j, half):
        ref = part_slot(j + lo, c, half)
        return remote(ref, ref, lys.at[j, half], lyr.at[j, half], {"blk": side})

    def l_side_in(j, half):
        ref = part_slot(j + 1 - lo, c_side, half)
        return remote(ref, ref, lys.at[j, half], lyr.at[j, half], {"blk": side})

    def l_diag(j):
        ref = slot(j + 1 - lo, c_side)
        return remote(ref, ref, lds.at[j], ldr.at[j], {"blk": mate})

    def l_diag_in(j):
        ref = slot(j + 1 - lo, c_diag)
        return remote(ref, ref, lds.at[j], ldr.at[j], {"blk": mate})

    l_up(0, 0).start()
    l_up(0, 1).start()

    @pl.when(lo == 0)
    def _():
        l_side(0, 0).start()
        l_side(0, 1).start()

    l_core(0).start()
    for half in range(2):
        w_step_minus(1, half)
    for half in range(2):
        l_up_in(0, half).wait_recv()
        l_up(1, half).start()
        l_side(1 - lo, half).start()

    l_core(1).start()
    w_step_minus(2, 0)
    for half in range(2):
        w_step_plus(1, half)
    w_step_minus(2, 1)
    l_side_in(0, 0).wait_recv()
    l_side_in(0, 1).wait_recv()
    l_diag(0).start()
    for half in range(2):
        l_up_in(1, half).wait_recv()

        @pl.when(lo == 1)
        def _():
            l_side(1, half).start()

    l_core(2).start()
    l_core_in(0).wait_recv()
    l_core_in(1).wait_recv()
    l_diag_in(0).wait_recv()

    def v_out(t):
        ref = vals.at[t, lo]
        return remote(ref, ref, vs.at[t], vr.at[t], {"blk": side})

    def v_in(t):
        ref = vals.at[t, 1 - lo]
        return remote(ref, ref, vs.at[t], vr.at[t], {"blk": side})

    def rows_at(t, g, first, count):
        return pl.ds(pl.multiple_of(t * 512 + g * 256 + first, 32), count)

    def step(t, start, first, last):
        k = keys[pl.ds(pl.multiple_of(start, TOKENS), 512), :]
        for g in range(2):
            score[g] = nt_dot(q_full[rows_at(t, g, 0, 256), :], k)
        for g in range(2):
            factors = []
            for r in range(8):
                at = rows_at(t, g, r * 32, 32)
                tok = pl.ds(pl.multiple_of(t * HALF + r % 2 * 32, 32), 32)
                sc = score[g, r * 32:(r + 1) * 32, :] + bias[tok, first:first + 512]
                m = jnp.max(sc, axis=1, keepdims=True)
                if last:
                    old = top[at, :][:, :1]
                    m = jnp.maximum(m, old)
                e = jnp.exp2((sc - m) * GAIN)
                add = jnp.sum(e, axis=1, keepdims=True)
                prob[g, r * 32:(r + 1) * 32, :] = e.astype(BF16)
                if last:
                    shrink = jnp.exp2((old - m) * GAIN)
                    inverse = 1.0 / (total[at, :][:, :1] * shrink + add)
                    factors.append((shrink * inverse, inverse))
                else:
                    top[at, :] = jnp.broadcast_to(m, (32, 128))
                    total[at, :] = jnp.broadcast_to(add, (32, 128))
            got = jnp.dot(prob[g], k[:, :LAT], preferred_element_type=F32)
            if not last:
                accum[rows_at(t, g, 0, 256), :] = got
                continue
            score[g] = got
            for r in range(8):
                old, new = factors[r]
                ctx[g, r * 32:(r + 1) * 32, :] = (
                    accum[rows_at(t, g, r * 32, 32), :] * old + score[g, r * 32:(r + 1) * 32, :] * new
                ).astype(BF16)
            for n in range(4):
                head = 4 * g + n
                v = jnp.dot(ctx[g, n * HALF:(n + 1) * HALF, :], vu[head], preferred_element_type=F32)
                vals[t, lo, :, head * VAL:(head + 1) * VAL] = v.astype(BF16)

    @pl.loop(0, 2)
    def _(t):
        step(t, (c + 5) * TOKENS, 512, False)

        @pl.when(t == 0)
        def _():
            l_side_in(1, 0).wait_recv()
            l_side_in(1, 1).wait_recv()
            l_diag(1).start()
            for half in range(2):
                w_step_minus(3, half)
            for half in range(2):
                w_step_plus(2, half)

    loads[2].wait()
    l_core_in(2).wait_recv()
    l_diag_in(1).wait_recv()

    @pl.loop(0, 2)
    def _(t):
        step(t, (c + 1) * TOKENS, 0, True)
        v_out(t).start()

        @pl.when(t == 0)
        def _():
            for half in range(2):
                w_step_plus(3, half)

    for half in range(2):
        w_step_minus(4, half)
    for k in range(8):
        for half in range(2):
            w_core_in(k, half).wait_recv()

    def x_out(t, n, d):
        terms, got = ((terms_a, got_a), (terms_b, got_b))[n]
        xd = (x + d) % 4
        return remote(
            terms.at[t, :, xd], got.at[t, d - 1],
            xs.at[t, n, d - 1], xr.at[t, n, d - 1], {"head": hi * 4 + xd},
        )

    def project(t, n):
        first, width = WIDE[n]
        terms = (terms_a, terms_b)[n]
        both = vals[t].reshape(TOKENS, HEADS * VAL)
        out = nt_dot(both, wt[first:first + 2 * width, :])
        for y in range(2):
            left = out[y * HALF:(y + 1) * HALF, :width].reshape(8, 8, width)
            right = out[y * HALF:(y + 1) * HALF, width:].reshape(8, 8, width)
            pair = jnp.concatenate([left, right], axis=1).astype(BF16)
            terms[t, :, :, y] = pair.reshape(2, 4, 16, width)
        for d in (2, 1, 3):
            x_out(t, n, d).start()

    def y_same(n, yd, src):
        part, fin = ((part_a, fin_a), (part_b, fin_b))[n]
        return remote(
            part.at[yd, lo], fin.at[0, src], yss.at[n, yd], ysr.at[n, src], {"head": yd * 4 + x}
        )

    def y_other(n, yd, src):
        part, fin = ((part_a, fin_a), (part_b, fin_b))[n]
        return remote(
            part.at[yd, 1 - lo], fin.at[1, src], yos.at[n, yd], yor.at[n, src],
            {"blk": side, "head": yd * 4 + x},
        )

    def combine(t, n):
        terms, got, part = ((terms_a, got_a, part_a), (terms_b, got_b, part_b))[n]
        both = terms[t, :, x].astype(F32)
        for d in (1, 3, 2):
            x_out(t, n, d).wait_recv()
            both = both + got[t, d - 1].astype(F32)
        part[2 * t:2 * t + 2] = both.astype(BF16)
        for yd in (2 * t, 2 * t + 1):
            y_other(n, yd, hi).start()

            @pl.when(hi != yd)
            def _():
                y_same(n, yd, hi).start()

    v_in(0).wait_recv()
    project(0, 0)
    project(0, 1)
    v_in(1).wait_recv()
    project(1, 0)
    project(1, 1)
    combine(0, 0)
    combine(0, 1)
    combine(1, 0)
    combine(1, 1)
    same_cols, other_cols = [], []
    for n in range(2):
        part, fin = ((part_a, fin_a), (part_b, fin_b))[n]
        same = part[hi, lo].astype(F32)
        other = jnp.zeros_like(same)
        for e in (1, 2, 3):
            src = (hi + e) % 4
            y_same(n, src, src).wait_recv()
            same = same + fin[0, src].astype(F32)
        for src in range(4):
            y_other(n, src, src).wait_recv()
            other = other + fin[1, src].astype(F32)
        same_cols += [same[:8], same[8:]]
        other_cols += [other[:8], other[8:]]
    same = jnp.concatenate(same_cols, axis=1)
    other = jnp.concatenate(other_cols, axis=1)
    by_y = (jnp.where(lo == 0, same, other), jnp.where(lo == 0, other, same))
    pair = 2 * COLS
    out[...] = jnp.concatenate(
        [by_y[i % 2][:, i // 2 * pair:(i // 2 + 1) * pair] for i in range(16)], axis=1
    ).astype(BF16)

    @pl.loop(1, 16)
    def _(i):
        own_rows(i).wait_send()

    for k in range(2):
        for half in range(2):
            l_up(k, half).wait_send()
            l_side(k, half).wait_send()
        l_diag(k).wait_send()
    for k in range(3):
        l_core(k).wait_send()
    for half in range(2):
        for k in range(3):
            w_plus(k, half).wait_send()
        for k in range(4):
            w_minus(k, half).wait_send()
        for k in range(8):
            w_core(k, half).wait_send()
    for t in range(2):
        v_out(t).wait_send()
    for n in range(2):
        for t in range(2):
            for d in (1, 2, 3):
                x_out(t, n, d).wait_send()
        for yd in range(4):
            y_other(n, yd, hi).wait_send()
        for e in (1, 2, 3):
            y_same(n, (hi + e) % 4, hi).wait_send()


def shards(queries, latent, key_up_weight, value_up_weight, w_o, block_order):
    vmem = pl.BlockSpec(memory_space=pltpu.VMEM)
    anywhere = pl.BlockSpec(memory_space=pl.ANY)
    dma = pltpu.SemaphoreType.DMA
    rows = TOKENS * HEADS
    scratch = [
        pltpu.SMEM((64,), jnp.int32),
        pltpu.VMEM((8, WIDTH), BF16),
        pltpu.VMEM((HEADS, NOPE + ROT, TOKENS), BF16),
        pltpu.VMEM((HEADS, NOPE, LAT), BF16),
        pltpu.VMEM((HEADS, LAT, VAL), BF16),
        pltpu.VMEM((rows, WIDTH), BF16),
        pltpu.VMEM((TOKENS, SPAN * TOKENS), F32),
        pltpu.VMEM((16, 16, 384), BF16),
        pltpu.VMEM((12 * TOKENS, WIDTH), BF16),
        pltpu.VMEM((MINE, HEADS * VAL), BF16),
        pltpu.VMEM((2, 2, HALF, HEADS * VAL), BF16),
        pltpu.VMEM((rows, 128), F32),
        pltpu.VMEM((rows, 128), F32),
        pltpu.VMEM((rows, LAT), F32),
        pltpu.VMEM((2, 256, LAT), F32),
        pltpu.VMEM((2, 256, LAT), BF16),
        pltpu.VMEM((2, 256, LAT), BF16),
        pltpu.VMEM((2, 2, 4, 2, 16, 512), BF16),
        pltpu.VMEM((2, 2, 4, 2, 16, 384), BF16),
        pltpu.VMEM((2, 3, 2, 2, 16, 512), BF16),
        pltpu.VMEM((2, 3, 2, 2, 16, 384), BF16),
        pltpu.VMEM((4, 2, 16, 512), BF16),
        pltpu.VMEM((4, 2, 16, 384), BF16),
        pltpu.VMEM((2, 4, 16, 512), BF16),
        pltpu.VMEM((2, 4, 16, 384), BF16),
        dma((6,)),
        dma((16,)), dma((16,)),
        dma((2, 2)), dma((2, 2)),
        dma((3,)), dma((3,)),
        dma((2, 2)), dma((2, 2)),
        dma((2,)), dma((2,)),
        dma((3, 2)), dma((3, 2)),
        dma((4, 2)), dma((4, 2)),
        dma((8, 2)), dma((8, 2)),
        dma((2,)), dma((2,)),
        dma((2, 2, 3)), dma((2, 2, 3)),
        dma((2, 4)), dma((2, 4)),
        dma((2, 4)), dma((2, 4)),
    ]
    return pl.pallas_call(
        kernel,
        out_shape=jax.ShapeDtypeStruct((8, 2 * MINE), BF16),
        in_specs=[anywhere] * 6,
        out_specs=vmem,
        scratch_shapes=scratch,
        compiler_params=pltpu.CompilerParams(
            collective_id=0, has_side_effects=True, vmem_limit_bytes=60 * 1024 * 1024
        ),
        cost_estimate=pl.CostEstimate(flops=3_500_000_000, bytes_accessed=3_000_000, transcendentals=1_048_576),
    )(block_order, latent, queries.transpose(1, 2, 0), key_up_weight, value_up_weight, w_o.T)


def solution(mesh):
    placed = (
        P("blk", "head", None),
        P(("blk", "head"), None),
        P("head", None, None),
        P("head", None, None),
        P("head", "blk"),
        P(),
    )
    return jax.shard_map(
        shards, mesh=mesh, in_specs=placed, out_specs=P(("blk", "head"), None), check_vma=False
    )
```

```python
import functools
import math

import jax
import jax.numpy as jnp
from jax import lax
from jax.experimental import pallas as pl
from jax.experimental.pallas import tpu as pltpu
from jax.sharding import PartitionSpec as P

NOPE = 128
ROT = 64
LAT = 512
WIDTH = LAT + ROT
VAL = 128
HEADS = 8
TOKENS = 128
HALF = 64
SPAN = 8
NBLK = 32
COLS = 112
MINE = 1792
WIDE = ((0, 512), (1024, 384))
GAIN = (NOPE + ROT) ** (-0.5) * math.log2(math.e)
HIDDEN = -1e30
NT = (((1,), (1,)), ((), ()))
F32 = jnp.float32
BF16 = jnp.bfloat16


def nt_dot(a, b):
    return lax.dot_general(a, b, NT, preferred_element_type=F32)


def remote(src, dst, send, recv, device):
    return pltpu.make_async_remote_copy(
        src_ref=src, dst_ref=dst, send_sem=send, recv_sem=recv,
        device_id=device, device_id_type=pl.DeviceIdType.MESH,
    )


def kernel(
    order_hbm, latent_hbm, q_hbm, ku_hbm, vu_hbm, wo_hbm, out,
    order, latent, q_raw, ku, vu, q_full, bias, pack, keys, wt, vals,
    top, total, accum, score, prob, ctx, terms_a, terms_b, got_a, got_b, relay_a, relay_b, part_a, part_b, fin_a, fin_b,
    load_sem, ps, pr, lzs, lzr, lcs, lcr, lys, lyr, lds, ldr,
    wps, wpr, wms, wmr, wcs, wcr, vs, vr, xs, xr, yss, ysr, yos, yor,
):
    b = lax.axis_index("blk")
    h = lax.axis_index("head")
    z, c = b // 4, b % 4
    lo, core = c // 2, c % 2
    hi, x = h // 4, h % 4
    up = (b + 4) % NBLK
    down = (b + NBLK - 4) % NBLK
    mate = b + 1 - 2 * core
    side = b + 2 - 4 * lo
    c_mate = c + 1 - 2 * core
    c_side = c + 2 - 4 * lo
    c_diag = c_side + 1 - 2 * core

    loads = [
        pltpu.make_async_copy(src, dst, load_sem.at[i])
        for i, (src, dst) in enumerate(((q_hbm, q_raw), (ku_hbm, ku), (vu_hbm, vu)))
    ]
    mine = wt.at[pl.ds(pl.multiple_of((z * 2 + core) * COLS, 16), COLS)]
    loads.append(pltpu.make_async_copy(wo_hbm, mine, load_sem.at[3]))
    loads.append(pltpu.make_async_copy(latent_hbm, latent, load_sem.at[4]))
    loads.append(pltpu.make_async_copy(order_hbm, order, load_sem.at[5]))
    loads[4].start()

    barrier = pltpu.get_barrier_semaphore()

    def greet(device):
        pl.semaphore_signal(barrier, inc=1, device_id=device, device_id_type=pl.DeviceIdType.MESH)

    @pl.loop(1, 16)
    def _(i):
        greet({"head": (h + i) % 16})

    @pl.loop(0, 4)
    def _(i):
        greet({"blk": side, "head": (hi + i) % 4 * 4 + x})

    greet({"blk": up})
    greet({"blk": down})
    greet({"blk": mate})
    for load in loads[3:4] + loads[:3] + loads[5:]:
        load.start()
    loads[4].wait()
    rows = latent[...].astype(F32)
    second = jnp.concatenate([rows[:, 384:], jnp.zeros((8, 192), F32)], axis=1)
    pack[h] = jnp.concatenate([rows[:, :384], second], axis=0).astype(BF16)
    pl.semaphore_wait(barrier, 22)

    def own_rows(i):
        return remote(pack.at[h], pack.at[h], ps.at[i], pr.at[i], {"head": (h + i) % 16})

    @pl.loop(1, 16)
    def _(i):
        own_rows(i).start()

    def shard(zz, cc, half):
        first = (zz * 2 + cc) * COLS + 64 * half
        return wt.at[pl.ds(pl.multiple_of(first, 16), (64, 48)[half])]

    def w_plus(k, half):
        ref = shard((z + 8 - k) % 8, core, half)
        return remote(ref, ref, wps.at[k, half], wpr.at[k, half], {"blk": up})

    def w_minus(k, half):
        ref = shard((z + k) % 8, core, half)
        return remote(ref, ref, wms.at[k, half], wmr.at[k, half], {"blk": down})

    def w_core(k, half):
        zz = (z + 8 - k) % 8 if k < 4 else (z + k - 3) % 8
        ref = shard(zz, core, half)
        return remote(ref, ref, wcs.at[k, half], wcr.at[k, half], {"blk": mate})

    def w_core_in(k, half):
        zz = (z + 8 - k) % 8 if k < 4 else (z + k - 3) % 8
        ref = shard(zz, 1 - core, half)
        return remote(ref, ref, wcs.at[k, half], wcr.at[k, half], {"blk": mate})

    def w_plus_in(k, half):
        ref = shard((z + 7 - k) % 8, core, half)
        return remote(ref, ref, wps.at[k, half], wpr.at[k, half], {"blk": up})

    def w_minus_in(k, half):
        ref = shard((z + 1 + k) % 8, core, half)
        return remote(ref, ref, wms.at[k, half], wmr.at[k, half], {"blk": down})

    def w_step_plus(k, half):
        w_plus_in(k - 1, half).wait_recv()
        if k < 3:
            w_plus(k, half).start()
        w_core(k, half).start()

    def w_step_minus(k, half):
        w_minus_in(k - 1, half).wait_recv()
        if k < 4:
            w_minus(k, half).start()
        w_core(3 + k, half).start()

    loads[3].wait()
    for half in range(2):
        w_plus(0, half).start()
        w_minus(0, half).start()

    for half in range(2):
        w_core(0, half).start()

    loads[0].wait()
    loads[1].wait()
    for n in range(HEADS):
        lat = lax.dot_general(
            q_raw[n, :NOPE, :], ku[n], (((0,), (0,)), ((), ())), preferred_element_type=F32
        ).astype(BF16)
        turned = q_raw[n, NOPE:, :].astype(F32).T.astype(BF16)
        for t in range(2):
            at = slice(t * 512 + n * HALF, t * 512 + (n + 1) * HALF)
            q_full[at, :LAT] = lat[t * HALF:(t + 1) * HALF]
            q_full[at, LAT:] = turned[t * HALF:(t + 1) * HALF]

    loads[5].wait()
    row = lax.broadcasted_iota(jnp.int32, (TOKENS, TOKENS), 0)
    col = lax.broadcasted_iota(jnp.int32, (TOKENS, TOKENS), 1)
    q_pos = jnp.where(row < HALF, order[2 * b], order[2 * b + 1]) * HALF + row % HALF
    for n in range(SPAN):
        src = (b + NBLK - 7 + n) % NBLK
        k_pos = jnp.where(col < HALF, order[2 * src], order[2 * src + 1]) * HALF + col % HALF
        bias[:, n * TOKENS:(n + 1) * TOKENS] = jnp.where(k_pos <= q_pos, 0.0, HIDDEN)

    @pl.loop(1, 16)
    def _(i):
        ref = pack.at[(h + 16 - i) % 16]
        remote(ref, ref, ps.at[i], pr.at[i], {"head": (h + i) % 16}).wait_recv()

    def part_slot(plane, cc, half):
        first = (8 - 4 * plane + cc) * TOKENS + half * HALF
        return keys.at[pl.ds(pl.multiple_of(first, HALF), HALF)]

    def slot(plane, cc):
        return keys.at[pl.ds(pl.multiple_of((8 - 4 * plane + cc) * TOKENS, TOKENS), TOKENS)]

    gathered = pack[...].astype(F32)
    base = pl.multiple_of((8 + c) * TOKENS, TOKENS)
    keys[pl.ds(base, TOKENS), :384] = gathered[:, :8, :].reshape(TOKENS, 384).astype(BF16)
    keys[pl.ds(base, TOKENS), 384:] = gathered[:, 8:, :192].reshape(TOKENS, 192).astype(BF16)

    def l_up(k, half):
        src, dst = part_slot(k, c, half), part_slot(k + 1, c, half)
        return remote(src, dst, lzs.at[k, half], lzr.at[k, half], {"blk": up})

    def l_up_in(k, half):
        ref = part_slot(k + 1, c, half)
        return remote(ref, ref, lzs.at[k, half], lzr.at[k, half], {"blk": up})

    def l_core(p):
        return remote(slot(p, c), slot(p, c), lcs.at[p], lcr.at[p], {"blk": mate})

    def l_core_in(p):
        return remote(slot(p, c_mate), slot(p, c_mate), lcs.at[p], lcr.at[p], {"blk": mate})

    def l_side(j, half):
        ref = part_slot(j + lo, c, half)
        return remote(ref, ref, lys.at[j, half], lyr.at[j, half], {"blk": side})

    def l_side_in(j, half):
        ref = part_slot(j + 1 - lo, c_side, half)
        return remote(ref, ref, lys.at[j, half], lyr.at[j, half], {"blk": side})

    def l_diag(j):
        ref = slot(j + 1 - lo, c_side)
        return remote(ref, ref, lds.at[j], ldr.at[j], {"blk": mate})

    def l_diag_in(j):
        ref = slot(j + 1 - lo, c_diag)
        return remote(ref, ref, lds.at[j], ldr.at[j], {"blk": mate})

    l_up(0, 0).start()
    l_up(0, 1).start()

    @pl.when(lo == 0)
    def _():
        l_side(0, 0).start()
        l_side(0, 1).start()

    l_core(0).start()
    for half in range(2):
        w_step_minus(1, half)
    for half in range(2):
        l_up_in(0, half).wait_recv()
        l_up(1, half).start()
        l_side(1 - lo, half).start()

    l_core(1).start()
    w_step_minus(2, 0)
    w_step_minus(2, 1)
    l_side_in(0, 0).wait_recv()
    l_side_in(0, 1).wait_recv()
    l_diag(0).start()
    for half in range(2):
        l_up_in(1, half).wait_recv()

        @pl.when(lo == 1)
        def _():
            l_side(1, half).start()

    l_core(2).start()
    for half in range(2):
        w_step_plus(1, half)
    l_core_in(0).wait_recv()
    l_core_in(1).wait_recv()
    l_diag_in(0).wait_recv()

    def v_out(t):
        ref = vals.at[t, lo]
        return remote(ref, ref, vs.at[t], vr.at[t], {"blk": side})

    def v_in(t):
        ref = vals.at[t, 1 - lo]
        return remote(ref, ref, vs.at[t], vr.at[t], {"blk": side})

    def rows_at(t, g, first, count):
        return pl.ds(pl.multiple_of(t * 512 + g * 256 + first, 32), count)

    def step(t, start, first, last):
        k = keys[pl.ds(pl.multiple_of(start, TOKENS), 512), :]
        for g in range(2):
            score[g] = nt_dot(q_full[rows_at(t, g, 0, 256), :], k)
        for g in range(2):
            factors = []
            for r in range(8):
                at = rows_at(t, g, r * 32, 32)
                tok = pl.ds(pl.multiple_of(t * HALF + r % 2 * 32, 32), 32)
                sc = score[g, r * 32:(r + 1) * 32, :] + bias[tok, first:first + 512]
                m = jnp.max(sc, axis=1, keepdims=True)
                if last:
                    old = top[at, :][:, :1]
                    m = jnp.maximum(m, old)
                e = jnp.exp2((sc - m) * GAIN)
                add = jnp.sum(e, axis=1, keepdims=True)
                prob[g, r * 32:(r + 1) * 32, :] = e.astype(BF16)
                if last:
                    shrink = jnp.exp2((old - m) * GAIN)
                    inverse = 1.0 / (total[at, :][:, :1] * shrink + add)
                    factors.append((shrink * inverse, inverse))
                else:
                    top[at, :] = jnp.broadcast_to(m, (32, 128))
                    total[at, :] = jnp.broadcast_to(add, (32, 128))
            got = jnp.dot(prob[g], k[:, :LAT], preferred_element_type=F32)
            if not last:
                accum[rows_at(t, g, 0, 256), :] = got
                continue
            score[g] = got
            for r in range(8):
                old, new = factors[r]
                ctx[g, r * 32:(r + 1) * 32, :] = (
                    accum[rows_at(t, g, r * 32, 32), :] * old + score[g, r * 32:(r + 1) * 32, :] * new
                ).astype(BF16)
            for n in range(4):
                head = 4 * g + n
                v = jnp.dot(ctx[g, n * HALF:(n + 1) * HALF, :], vu[head], preferred_element_type=F32)
                vals[t, lo, :, head * VAL:(head + 1) * VAL] = v.astype(BF16)

    @pl.loop(0, 2)
    def _(t):
        step(t, (c + 5) * TOKENS, 512, False)

        @pl.when(t == 0)
        def _():
            l_side_in(1, 0).wait_recv()
            l_side_in(1, 1).wait_recv()
            l_diag(1).start()
            for half in range(2):
                w_step_minus(3, half)

    for half in range(2):
        w_step_plus(2, half)
    loads[2].wait()
    l_core_in(2).wait_recv()
    l_diag_in(1).wait_recv()

    @pl.loop(0, 2)
    def _(t):
        step(t, (c + 1) * TOKENS, 0, True)
        v_out(t).start()

    for half in range(2):
        w_step_minus(4, half)
    for half in range(2):
        w_step_plus(3, half)
    for k in range(8):
        for half in range(2):
            w_core_in(k, half).wait_recv()

    def x_out(t, n, way, kind):
        terms, got, relay = ((terms_a, got_a, relay_a), (terms_b, got_b, relay_b))[n]
        xd = (x + 1 + 2 * way) % 4
        if kind == 0:
            src, dst = terms.at[t, way, (x + 2) % 4], relay.at[t, way]
        else:
            r = 1 - way if kind == 1 else way
            src, dst = terms.at[t, r, xd], got.at[t, way, r]
        sem = (t, n, way, kind)
        return remote(src, dst, xs.at[sem], xr.at[sem], {"head": hi * 4 + xd})

    def project(t, n):
        first, width = WIDE[n]
        terms = (terms_a, terms_b)[n]
        both = vals[t].reshape(TOKENS, HEADS * VAL)
        out = nt_dot(both, wt[first:first + 2 * width, :])
        for y in range(2):
            left = out[y * HALF:(y + 1) * HALF, :width].reshape(8, 8, width)
            right = out[y * HALF:(y + 1) * HALF, width:].reshape(8, 8, width)
            pair = jnp.concatenate([left, right], axis=1).astype(BF16)
            terms[t, :, :, y] = pair.reshape(2, 4, 16, width)
        for kind in range(2):
            for way in range(2):
                x_out(t, n, way, kind).start()

    def pass_on(t, n):
        terms, relay = ((terms_a, relay_a), (terms_b, relay_b))[n]
        for way in range(2):
            x_out(t, n, way, 0).wait_recv()
            xd = (x + 1 + 2 * way) % 4
            both = terms[t, way, xd].astype(F32) + relay[t, way].astype(F32)
            terms[t, way, xd] = both.astype(BF16)
            x_out(t, n, way, 2).start()

    def y_same(n, yd, src):
        part, fin = ((part_a, fin_a), (part_b, fin_b))[n]
        return remote(
            part.at[yd, lo], fin.at[0, src], yss.at[n, yd], ysr.at[n, src], {"head": yd * 4 + x}
        )

    def y_other(n, yd, src):
        part, fin = ((part_a, fin_a), (part_b, fin_b))[n]
        return remote(
            part.at[yd, 1 - lo], fin.at[1, src], yos.at[n, yd], yor.at[n, src],
            {"blk": side, "head": yd * 4 + x},
        )

    def combine(t, n):
        terms, got, part = ((terms_a, got_a, part_a), (terms_b, got_b, part_b))[n]
        for way in range(2):
            x_out(t, n, way, 1).wait_recv()
            x_out(t, n, way, 2).wait_recv()
        both = terms[t, :, x].astype(F32) + got[t, 0].astype(F32) + got[t, 1].astype(F32)
        part[2 * t:2 * t + 2] = both.astype(BF16)
        for yd in (2 * t, 2 * t + 1):
            y_other(n, yd, hi).start()

            @pl.when(hi != yd)
            def _():
                y_same(n, yd, hi).start()

    v_in(0).wait_recv()
    project(0, 0)
    project(0, 1)
    pass_on(0, 0)
    v_in(1).wait_recv()
    project(1, 0)
    pass_on(0, 1)
    project(1, 1)
    combine(0, 0)
    pass_on(1, 0)
    combine(0, 1)
    pass_on(1, 1)
    combine(1, 0)
    combine(1, 1)
    same_cols, other_cols = [], []
    for n in range(2):
        part, fin = ((part_a, fin_a), (part_b, fin_b))[n]
        same = part[hi, lo].astype(F32)
        other = jnp.zeros_like(same)
        for e in (1, 2, 3):
            src = (hi + e) % 4
            y_same(n, src, src).wait_recv()
            same = same + fin[0, src].astype(F32)
        for src in range(4):
            y_other(n, src, src).wait_recv()
            other = other + fin[1, src].astype(F32)
        same_cols += [same[:8], same[8:]]
        other_cols += [other[:8], other[8:]]
    same = jnp.concatenate(same_cols, axis=1)
    other = jnp.concatenate(other_cols, axis=1)
    by_y = (jnp.where(lo == 0, same, other), jnp.where(lo == 0, other, same))
    pair = 2 * COLS
    out[...] = jnp.concatenate(
        [by_y[i % 2][:, i // 2 * pair:(i // 2 + 1) * pair] for i in range(16)], axis=1
    ).astype(BF16)

    @pl.loop(1, 16)
    def _(i):
        own_rows(i).wait_send()

    for k in range(2):
        for half in range(2):
            l_up(k, half).wait_send()
            l_side(k, half).wait_send()
        l_diag(k).wait_send()
    for k in range(3):
        l_core(k).wait_send()
    for half in range(2):
        for k in range(3):
            w_plus(k, half).wait_send()
        for k in range(4):
            w_minus(k, half).wait_send()
        for k in range(8):
            w_core(k, half).wait_send()
    for t in range(2):
        v_out(t).wait_send()
    for n in range(2):
        for t in range(2):
            for way in range(2):
                for kind in range(3):
                    x_out(t, n, way, kind).wait_send()
        for yd in range(4):
            y_other(n, yd, hi).wait_send()
        for e in (1, 2, 3):
            y_same(n, (hi + e) % 4, hi).wait_send()


def shards(queries, latent, key_up_weight, value_up_weight, w_o, block_order):
    vmem = pl.BlockSpec(memory_space=pltpu.VMEM)
    anywhere = pl.BlockSpec(memory_space=pl.ANY)
    dma = pltpu.SemaphoreType.DMA
    rows = TOKENS * HEADS
    scratch = [
        pltpu.SMEM((64,), jnp.int32),
        pltpu.VMEM((8, WIDTH), BF16),
        pltpu.VMEM((HEADS, NOPE + ROT, TOKENS), BF16),
        pltpu.VMEM((HEADS, NOPE, LAT), BF16),
        pltpu.VMEM((HEADS, LAT, VAL), BF16),
        pltpu.VMEM((rows, WIDTH), BF16),
        pltpu.VMEM((TOKENS, SPAN * TOKENS), F32),
        pltpu.VMEM((16, 16, 384), BF16),
        pltpu.VMEM((12 * TOKENS, WIDTH), BF16),
        pltpu.VMEM((MINE, HEADS * VAL), BF16),
        pltpu.VMEM((2, 2, HALF, HEADS * VAL), BF16),
        pltpu.VMEM((rows, 128), F32),
        pltpu.VMEM((rows, 128), F32),
        pltpu.VMEM((rows, LAT), F32),
        pltpu.VMEM((2, 256, LAT), F32),
        pltpu.VMEM((2, 256, LAT), BF16),
        pltpu.VMEM((2, 256, LAT), BF16),
        pltpu.VMEM((2, 2, 4, 2, 16, 512), BF16),
        pltpu.VMEM((2, 2, 4, 2, 16, 384), BF16),
        pltpu.VMEM((2, 2, 2, 2, 16, 512), BF16),
        pltpu.VMEM((2, 2, 2, 2, 16, 384), BF16),
        pltpu.VMEM((2, 2, 2, 16, 512), BF16),
        pltpu.VMEM((2, 2, 2, 16, 384), BF16),
        pltpu.VMEM((4, 2, 16, 512), BF16),
        pltpu.VMEM((4, 2, 16, 384), BF16),
        pltpu.VMEM((2, 4, 16, 512), BF16),
        pltpu.VMEM((2, 4, 16, 384), BF16),
        dma((6,)),
        dma((16,)), dma((16,)),
        dma((2, 2)), dma((2, 2)),
        dma((3,)), dma((3,)),
        dma((2, 2)), dma((2, 2)),
        dma((2,)), dma((2,)),
        dma((3, 2)), dma((3, 2)),
        dma((4, 2)), dma((4, 2)),
        dma((8, 2)), dma((8, 2)),
        dma((2,)), dma((2,)),
        dma((2, 2, 2, 3)), dma((2, 2, 2, 3)),
        dma((2, 4)), dma((2, 4)),
        dma((2, 4)), dma((2, 4)),
    ]
    return pl.pallas_call(
        kernel,
        out_shape=jax.ShapeDtypeStruct((8, 2 * MINE), BF16),
        in_specs=[anywhere] * 6,
        out_specs=vmem,
        scratch_shapes=scratch,
        compiler_params=pltpu.CompilerParams(
            collective_id=0, has_side_effects=True, vmem_limit_bytes=60 * 1024 * 1024
        ),
        cost_estimate=pl.CostEstimate(flops=3_500_000_000, bytes_accessed=3_000_000, transcendentals=1_048_576),
    )(block_order, latent, queries.transpose(1, 2, 0), key_up_weight, value_up_weight, w_o.T)


def solution(mesh):
    placed = (
        P("blk", "head", None),
        P(("blk", "head"), None),
        P("head", None, None),
        P("head", None, None),
        P("head", "blk"),
        P(),
    )
    return jax.shard_map(
        shards, mesh=mesh, in_specs=placed, out_specs=P(("blk", "head"), None), check_vma=False
    )
```
